32 devices in a mesh: dp: 16 (over z, x, core), fsdp: 2 (over y).
Axes of the slice: x: 2, y: 2, z: 4, core: 2. Of those that a mesh axis runs over, the one named last changes fastest.
Arguments:
- tokens: bfloat16 [32, 561, 768], P(('dp', 'fsdp')), may hold values from -6 to 6
- coords: int32 [32, 2, 561], P(('dp', 'fsdp')), may hold values from 0 to 1023
- rel_pos: int32 [32, 561, 561], P(('dp', 'fsdp')), may hold values from 0 to 31
- rel_box: int32 [32, 2, 561, 561], P(('dp', 'fsdp')), may hold values from 0 to 63
- entity_pairs: int32 [32, 128, 2], P(('dp', 'fsdp')), may hold values from -1 to 560, as said below
- entity_grad: bfloat16 [32, 128, 2, 768], P(('dp', 'fsdp')), may hold values from -6 to 6
- w_qkv: bfloat16 [768, 2304], P(('dp', 'fsdp')), may hold values from -0.21875 to 0.21875
- w_attn_out: bfloat16 [768, 768], P(('dp', 'fsdp')), may hold values from -1.75 to 1.75
- dcpe_table: bfloat16 [2048, 768], P(('dp', 'fsdp')), may hold values from -3 to 3
- biases: bfloat16 [6, 768], P(None, ('dp', 'fsdp')), may hold values from -1.796875 to 1.796875
- norm_gains: bfloat16 [2, 768], P(None, ('dp', 'fsdp')), may hold values from 0.5 to 1.5
- w_ff_in: bfloat16 [768, 3072], P(('dp', 'fsdp')), may hold values from -0.21875 to 0.21875
- w_ff_out: bfloat16 [3072, 768], P(('dp', 'fsdp')), may hold values from -0.109375 to 0.109375
- ff_bias: bfloat16 [3072], P(('dp', 'fsdp')), may hold values from -1.796875 to 1.796875
- rel_table: bfloat16 [160, 12], replicated, may hold values from -3 to 3
Outputs:
- layer_out: bfloat16 [32, 561, 768], P(('dp', 'fsdp'))
- input_grad: float32 [32, 561, 768], P(('dp', 'fsdp'))
- w_qkv_grad: float32 [768, 2304], P(('dp', 'fsdp'))
- w_attn_out_grad: float32 [768, 768], P(('dp', 'fsdp'))
- dcpe_table_grad: float32 [2048, 768], P(('dp', 'fsdp'))
- biases_grad: float32 [6, 768], P(None, ('dp', 'fsdp'))
- norm_gains_grad: float32 [2, 768], P(None, ('dp', 'fsdp'))
- w_ff_in_grad: float32 [768, 3072], P(('dp', 'fsdp'))
- w_ff_out_grad: float32 [3072, 768], P(('dp', 'fsdp'))
- ff_bias_grad: float32 [3072], P(('dp', 'fsdp'))
- rel_table_grad: float32 [160, 12], replicated
The draws below stay inside these ranges and needn't reach their ends.
Inputs may be any that keep to these rules, and one draw needn't show every extreme that they name: `entity_pairs`: each entry names a token of its page or is -1; a live pair names two different tokens, a padded pair is -1 twice, and a page's padded pairs follow its live ones. A token may be named by several slots of its page.
All inputs are finite; a program needn't handle non-finite values.
Results may differ from the reference program's by a relative error of at most 0.015.
The reference program's roundings to bfloat16 on the way count: a program that leaves them out, or rounds other values in their place, can miss the bound.
Values may be sent and summed in bfloat16 or wider, within the bound.
No kernel may reach another device: no remote copies, remote signals or barrier semaphores. Data moves between devices by JAX's collectives and lax.ppermute only.
A program may use at most 256 MiB of HBM per device.

```python
import jax
import jax.numpy as jnp
from jax import lax

D = 768
HEADS = 12
HEAD_DIM = 64
FF = 3072
COORDS = 1024
B1 = 32
B2 = 64
PAGE = 561
PAIRS = 128
PAGES = 32


def draw_entity_pairs(key, part):
    key = jax.random.fold_in(key, 11)
    order_key, live_key = jax.random.split(key)
    page_keys = jax.random.split(order_key, PAGES)
    shuffled = jax.vmap(lambda page_key: jax.random.permutation(page_key, PAGE - 1))(page_keys).astype(jnp.int32)
    slot_ids = lax.iota(jnp.int32, PAIRS)
    head_index = slot_ids // 2
    tail_index = (PAIRS + 1) // 2 + slot_ids
    reused_index = jnp.maximum(slot_ids - 3, 0) // 2
    heads = shuffled[:, head_index]
    fresh_tails = shuffled[:, tail_index]
    reused_tails = shuffled[:, reused_index]
    tails = jnp.where((slot_ids % 4 == 3)[None, :], reused_tails, fresh_tails)
    tails = jnp.where((slot_ids == 0)[None, :], jnp.int32(PAGE - 1), tails).astype(jnp.int32)
    chosen = jnp.stack([heads, tails], axis=2)
    live_count = jax.random.randint(live_key, (PAGES, 1, 1), PAIRS // 2, PAIRS, dtype=jnp.int32)
    return jnp.where(slot_ids[None, :, None] < live_count, chosen, -1).astype(jnp.int32)


def set_ends(values, own_key, low, high):
    place = [jax.random.randint(jax.random.fold_in(own_key, axis), (), 0, length) for axis, length in enumerate(values.shape)]
    widest = values.shape.index(max(values.shape))
    next_to = place[:widest] + [(place[widest] + 1) % values.shape[widest]] + place[widest + 1:]
    return values.at[tuple(place)].set(low).at[tuple(next_to)].set(high)


def shard_levels(key, extent, pieces, least, high):
    level = 1.0
    for dim, shards_of in pieces:
        draws = jax.random.uniform(jax.random.fold_in(jax.random.fold_in(key, 6), dim), (shards_of,), jnp.float32, least / len(pieces), high / len(pieces))
        level = level * jnp.repeat(jnp.exp(draws), extent[dim] // shards_of).reshape((-1,) + (1,) * (len(extent) - 1 - dim))
    return level


def scatter_about(rng, shape, spread, bound, cuts=(), kind=jnp.bfloat16):
    values = jax.random.normal(rng, shape, jnp.float32) * spread
    if len(cuts) > 0:
        values = shard_levels(rng, shape, cuts, -0.22, 0.18) * values
    return jnp.clip(values, min=-bound, max=bound).astype(kind)


def setup_inputs(seed: int = 0) -> dict:
    keys = jax.random.split(jax.random.key(seed), 16)
    return {
        "tokens": scatter_about(keys[0], (PAGES, PAGE, D), 1.0, 6.0, ((0, 32),)),
        "coords": set_ends(jax.random.randint(keys[1], (PAGES, 2, PAGE), 0, COORDS), jax.random.fold_in(keys[1], 1), 0, COORDS - 1).astype(jnp.int32),
        "rel_pos": set_ends(jax.random.randint(keys[2], (PAGES, PAGE, PAGE), 0, B1), jax.random.fold_in(keys[2], 1), 0, B1 - 1).astype(jnp.int32),
        "rel_box": set_ends(jax.random.randint(keys[3], (PAGES, 2, PAGE, PAGE), 0, B2), jax.random.fold_in(keys[3], 1), 0, B2 - 1).astype(jnp.int32),
        "entity_pairs": draw_entity_pairs(jax.random.fold_in(keys[15], 71), 0),
        "entity_grad": scatter_about(keys[5], (PAGES, PAIRS, 2, D), 1.0, 6.0, ((0, 32),)),
        "w_qkv": scatter_about(keys[6], (D, 3 * D), D ** -0.5, 0.21875, ((0, 32),)),
        "w_attn_out": scatter_about(keys[7], (D, D), (D // 64) ** -0.5, 1.75, ((0, 32),)),
        "dcpe_table": scatter_about(keys[8], (2 * COORDS, D), 0.5, 3.0, ((0, 32),)),
        "biases": scatter_about(keys[9], (6, D), 0.3, 1.796875, ((1, 32),)),
        "norm_gains": jnp.clip(1.0 + 0.1 * jax.random.normal(keys[10], (2, D), jnp.float32), 0.5, 1.5).astype(jnp.bfloat16),
        "w_ff_in": scatter_about(keys[11], (D, FF), D ** -0.5, 0.21875, ((0, 32),)),
        "w_ff_out": scatter_about(keys[12], (FF, D), FF ** -0.5, 0.109375, ((0, 32),)),
        "ff_bias": scatter_about(keys[13], (FF,), 0.3, 1.796875, ((0, 32),)),
        "rel_table": scatter_about(keys[14], (B1 + 2 * B2, HEADS), 0.5, 3.0),
    }


@jax.custom_vjp
def low(v):
    return lax.optimization_barrier(v.astype(jnp.bfloat16)).astype(jnp.float32)

@jax.custom_vjp
def low_back(v):
    return v

def low_keep(v):
    return (low(v), None)

def low_pass(kept, grad):
    return (grad,)

def back_keep(v):
    return (v, None)

def back_low(kept, grad):
    return (low(grad),)
low.defvjp(low_keep, low_pass)
low_back.defvjp(back_keep, back_low)
highest = lax.Precision.HIGHEST
epsilon = 1e-05

def norm_rows(values, gain, shift):
    row_mean = lax.optimization_barrier(jnp.mean(values, axis=-1, keepdims=True))
    centred = values - row_mean
    variance = lax.optimization_barrier(jnp.mean(centred * centred, axis=-1, keepdims=True))
    return centred * lax.rsqrt(variance + epsilon) * gain + shift

def split_heads(values):
    return values.reshape(values.shape[0], PAGE, HEADS, HEAD_DIM).transpose(0, 2, 1, 3)

def page_block(bias_table, inputs):
    query_page, key_page, value_page, pos_page, box_page = inputs
    score_bias = bias_table[pos_page] + bias_table[B1 + box_page[0]] + bias_table[B1 + B2 + box_page[1]]
    scores = low_back(jnp.einsum('hqd,hkd->hqk', query_page, key_page, precision=highest) + score_bias.transpose(2, 0, 1))
    largest = lax.optimization_barrier(jnp.max(scores, axis=-1, keepdims=True))
    raised = jnp.exp(scores - largest)
    attention = low(raised / lax.optimization_barrier(jnp.sum(raised, axis=-1, keepdims=True)))
    return jnp.einsum('hqk,hkd->hqd', attention, value_page, precision=highest)

def forward(params, tokens, coords, rel_pos, rel_box):
    w_qkv, w_attn_out, dcpe_table, biases, norm_gains, w_ff_in, w_ff_out, ff_bias, rel_table = params
    columns = lax.iota(jnp.int32, 2 * COORDS)
    position_hot = ((coords[:, 0, :, None] == columns) | (coords[:, 1, :, None] + COORDS == columns)).astype(jnp.float32)
    position = low_back(jnp.einsum('gpc,cd->gpd', position_hot, dcpe_table, precision=highest))
    begin = tokens + position
    begin_rows = low(begin)
    united_proj = jnp.einsum('gpd,de->gpe', begin_rows, w_qkv, precision=highest)
    queries = low_back(low((united_proj[..., :D] + biases[0]) * 0.125))
    key_rows = low_back(low(united_proj[..., D:2 * D]))
    value_rows = low_back(low(united_proj[..., 2 * D:] + biases[1]))
    blocked = jax.checkpoint(page_block)
    context = lax.map(lambda inputs: blocked(rel_table, inputs), (split_heads(queries), split_heads(key_rows), split_heads(value_rows), rel_pos, rel_box))
    context = low_back(low(context.transpose(0, 2, 1, 3).reshape(tokens.shape)))
    attended = low_back(jnp.einsum('gpd,de->gpe', context, w_attn_out, precision=highest) + biases[2])
    mid_norm = norm_rows(begin + attended, norm_gains[0], biases[3])
    ff_inner = low_back(jnp.einsum('gpd,df->gpf', low(mid_norm), w_ff_in, precision=highest) + ff_bias)
    ff_act = low(jax.nn.gelu(ff_inner, approximate=False))
    ff_outer = low_back(jnp.einsum('gpf,fd->gpd', ff_act, w_ff_out, precision=highest) + biases[4])
    return norm_rows(mid_norm + ff_outer, norm_gains[1], biases[5])

def reference(tokens, coords, rel_pos, rel_box, entity_pairs, entity_grad, w_qkv, w_attn_out, dcpe_table, biases, norm_gains, w_ff_in, w_ff_out, ff_bias, rel_table):
    params = tuple((weight.astype(jnp.float32) for weight in (w_qkv, w_attn_out, dcpe_table, biases, norm_gains, w_ff_in, w_ff_out, ff_bias, rel_table)))
    group_size = 4 if PAGES % 4 == 0 else 2 if PAGES % 2 == 0 else 1
    group_count = PAGES // group_size

    def grouped(array):
        return array.reshape((group_count, group_size) + array.shape[1:])

    def one_group(running, inputs):
        token_group, coord_group, pos_group, box_group, pair_group, grad_group = inputs
        outputs, pullback = jax.vjp(lambda weights, begin: forward(weights, begin, coord_group, pos_group, box_group), params, token_group.astype(jnp.float32))
        slot_tokens = pair_group.reshape(group_size, 2 * PAIRS).astype(jnp.int32)
        safe_tokens = jnp.where(slot_tokens >= 0, slot_tokens, PAGE).astype(jnp.int32)
        page_index = jnp.broadcast_to(lax.iota(jnp.int32, group_size)[:, None], (group_size, 2 * PAIRS)).astype(jnp.int32)
        slot_grads = grad_group.reshape(group_size, 2 * PAIRS, D).astype(jnp.float32)
        out_cot = jnp.zeros((group_size, PAGE, D), jnp.float32).at[page_index, safe_tokens].add(slot_grads, mode='drop')
        weight_grads, begin_grad = pullback(out_cot)
        running = tuple((held_grad + new_grad for held_grad, new_grad in zip(running, weight_grads)))
        return (running, (outputs.astype(jnp.bfloat16), begin_grad))
    initial = tuple((jnp.zeros(weight.shape, jnp.float32) for weight in params))
    summed, (layer_out, input_grad) = lax.scan(one_group, initial, tuple((grouped(array) for array in (tokens, coords, rel_pos, rel_box, entity_pairs, entity_grad))))
    return (layer_out.reshape(PAGES, PAGE, D), input_grad.reshape(PAGES, PAGE, D), summed[0], summed[1], summed[2], summed[3], summed[4], summed[5], summed[6], summed[7], summed[8])
```

```python
from functools import partial

import jax
import jax.numpy as jnp
from jax import lax
from jax.experimental import pallas as pl
from jax.experimental.pallas import tpu as pltpu
from jax.sharding import PartitionSpec as P

HEADS = 12
HEAD_DIM = 64
B1 = 32
B2 = 64
PAIR = 2 * HEAD_DIM
EPSILON = 1e-05
AXES = ("dp", "fsdp")
VMEM_LIMIT = 58 * 2**20
NEVER = -1e30
OUTSIDE = -4096

bf16 = jnp.bfloat16
f32 = jnp.float32


def dot(a, b):
    return jnp.dot(a, b, preferred_element_type=f32)


def dot_nt(a, b):
    return lax.dot_general(a, b, (((1,), (1,)), ((), ())), preferred_element_type=f32)


def dot_tn(a, b):
    return lax.dot_general(a, b, (((0,), (0,)), ((), ())), preferred_element_type=f32)


def params():
    return pltpu.CompilerParams(vmem_limit_bytes=VMEM_LIMIT)


def cost(flops, moved):
    return pl.CostEstimate(flops=int(flops), bytes_accessed=int(moved), transcendentals=0)


def full(shape):
    return pl.BlockSpec(shape, lambda *_: (0,) * len(shape))


def bias_kernel(live, index_ref, table_ref, out_ref):
    rows, width = out_ref.shape[1:]
    first_row = pl.program_id(0) * rows
    tables = [jnp.broadcast_to(table_ref[r : r + 1, :], (8, 128)) for r in range(2 * HEADS)]

    def eight_rows(step, carry):
        at = pl.multiple_of(step * 8, 8)
        key_ids = first_row + at + lax.broadcasted_iota(jnp.int32, (8, 128), 0)
        dead = jnp.where(key_ids < live, 0.0, NEVER)
        for left in range(0, width, 128):
            packed = index_ref[pl.ds(at, 8), left : left + 128]
            flat = packed & (B1 - 1)
            across = (lax.shift_right_logical(packed, 5) & (B2 - 1)) + B1
            downward = lax.shift_right_logical(packed, 11)
            for head in range(HEADS):
                low, high = tables[2 * head], tables[2 * head + 1]
                looked = (
                    jnp.take_along_axis(low, flat, axis=1, mode="promise_in_bounds")
                    + jnp.take_along_axis(low, across, axis=1, mode="promise_in_bounds")
                    + jnp.take_along_axis(high, downward, axis=1, mode="promise_in_bounds")
                    + dead
                )
                right = min(left + 128, width)
                out_ref[head, pl.ds(at, 8), left:right] = looked[:, : right - left]
        return carry

    lax.fori_loop(0, rows // 8, eight_rows, 0)


def score_bias(packed, rel_table, live):
    keys = width = packed.shape[0]
    rows = 64
    lookup = jnp.zeros((HEADS, 2, 128), f32)
    lookup = lookup.at[:, 0, : B1 + B2].set(rel_table[: B1 + B2].T.astype(f32))
    lookup = lookup.at[:, 1, :B2].set(rel_table[B1 + B2 :].T.astype(f32))
    return pl.pallas_call(
        partial(bias_kernel, live),
        grid=(keys // rows,),
        in_specs=[pl.BlockSpec((rows, packed.shape[1]), lambda i: (i, 0)), full((2 * HEADS, 128))],
        out_specs=pl.BlockSpec((HEADS, rows, width), lambda i: (0, i, 0)),
        out_shape=jax.ShapeDtypeStruct((HEADS, keys, width), f32),
        compiler_params=params(),
        cost_estimate=cost(3e10, 4 * HEADS * keys * width),
    )(packed, lookup.reshape(2 * HEADS, 128))


def embed_kernel(token_ref, place_ref, table_ref, weight_ref, small_ref, begin_ref, rows_ref, united_ref):
    half = table_ref.shape[0] // 2
    width = token_ref.shape[1]
    columns = lax.broadcasted_iota(jnp.int32, (token_ref.shape[0], half), 1)
    total = token_ref[...].astype(f32)
    for side in range(2):
        hot = jnp.where(place_ref[:, side : side + 1] == columns, 1.0, 0.0).astype(bf16)
        total += dot(hot, table_ref[side * half : (side + 1) * half, :])
    begin_ref[...] = total
    rows = total.astype(bf16)
    rows_ref[...] = rows
    query = dot(rows, weight_ref[:, :width]) + small_ref[0:1, :]
    united_ref[:, :width] = (query * 0.125).astype(bf16)
    united_ref[:, width : 2 * width] = dot(rows, weight_ref[:, width : 2 * width]).astype(bf16)
    value = dot(rows, weight_ref[:, 2 * width :]) + small_ref[1:2, :]
    united_ref[:, 2 * width :] = value.astype(bf16)


def embed(tokens, places, dcpe_table, w_qkv, small):
    count, width = tokens.shape
    return pl.pallas_call(
        embed_kernel,
        out_shape=(
            jax.ShapeDtypeStruct((count, width), f32),
            jax.ShapeDtypeStruct((count, width), bf16),
            jax.ShapeDtypeStruct((count, 3 * width), bf16),
        ),
        compiler_params=params(),
        cost_estimate=cost(2 * count * width * (dcpe_table.shape[0] + 3 * width), 12e6),
    )(tokens, places, dcpe_table, w_qkv, small)


def head_mask(head):
    return lax.broadcasted_iota(jnp.int32, (1, PAIR), 1) // HEAD_DIM == head


def attend_kernel(query_ref, key_ref, value_ref, bias_ref, attention_ref, context_ref):
    query, key = query_ref[...], key_ref[...]
    value_t = value_ref[...].astype(f32).T.astype(bf16)
    parts = []
    for head in range(2):
        scores = dot_nt(jnp.where(head_mask(head), key, 0), query) + bias_ref[head]
        raised = jnp.exp(scores - jnp.max(scores, axis=0, keepdims=True))
        attention = (raised * (1.0 / jnp.sum(raised, axis=0, keepdims=True))).astype(bf16)
        attention_ref[head] = attention
        parts.append(dot(value_t[head * HEAD_DIM : (head + 1) * HEAD_DIM], attention))
    context_ref[...] = jnp.concatenate(parts, axis=0).T.astype(bf16)


def attend(united, bias):
    count = united.shape[0]
    pairs = HEADS // 2
    column = lambda shift: pl.BlockSpec((count, PAIR), lambda p: (0, p + shift))
    square = pl.BlockSpec((2, count, count), lambda p: (p, 0, 0))
    return pl.pallas_call(
        attend_kernel,
        grid=(pairs,),
        in_specs=[column(0), column(pairs), column(2 * pairs), square],
        out_specs=(square, column(0)),
        out_shape=(
            jax.ShapeDtypeStruct((HEADS, count, count), bf16),
            jax.ShapeDtypeStruct((count, HEADS * HEAD_DIM), bf16),
        ),
        compiler_params=params(),
        cost_estimate=cost(4 * HEADS * count * count * HEAD_DIM, 6 * HEADS * count * count),
    )(united, united, united, bias)


def attend_back_kernel(
    query_ref, key_ref, value_ref, attention_ref, d_context_ref, d_query_ref, d_key_ref, d_value_ref, d_scores_ref
):
    query, value, d_context = query_ref[...], value_ref[...], d_context_ref[...]
    key_t = key_ref[...].astype(f32).T.astype(bf16)
    parts = []
    d_key = jnp.zeros(query.shape, f32)
    d_value = jnp.zeros(query.shape, f32)
    for head in range(2):
        mask = head_mask(head)
        d_attention = dot_nt(jnp.where(mask, value, 0), d_context)
        attention_low = attention_ref[head]
        attention = attention_low.astype(f32)
        centre = jnp.sum(attention * d_attention, axis=0, keepdims=True)
        d_scores = (attention * (d_attention - centre)).astype(bf16)
        d_scores_ref[head] = d_scores
        d_key += dot(d_scores, jnp.where(mask, query, 0))
        d_value += dot(attention_low, jnp.where(mask, d_context, 0))
        parts.append(dot(key_t[head * HEAD_DIM : (head + 1) * HEAD_DIM], d_scores))
    d_query_ref[...] = jnp.concatenate(parts, axis=0).T.astype(bf16) * bf16(0.125)
    d_key_ref[...] = d_key.astype(bf16)
    d_value_ref[...] = d_value.astype(bf16)


def attend_back(united, attention, d_context):
    count = united.shape[0]
    pairs = HEADS // 2
    column = lambda shift: pl.BlockSpec((count, PAIR), lambda p: (0, p + shift))
    square = pl.BlockSpec((2, count, count), lambda p: (p, 0, 0))
    joined = jax.ShapeDtypeStruct((count, HEADS * HEAD_DIM), bf16)
    return pl.pallas_call(
        attend_back_kernel,
        grid=(pairs,),
        in_specs=[column(0), column(pairs), column(2 * pairs), square, column(0)],
        out_specs=(column(0), column(0), column(0), square),
        out_shape=(joined, joined, joined, jax.ShapeDtypeStruct((HEADS, count, count), bf16)),
        compiler_params=params(),
        cost_estimate=cost(8 * HEADS * count * count * HEAD_DIM, 4 * HEADS * count * count),
    )(united, united, united, attention, d_context)


def unit_rows(values):
    centred = values - jnp.mean(values, axis=1, keepdims=True)
    scale = lax.rsqrt(jnp.mean(centred * centred, axis=1, keepdims=True) + EPSILON)
    return centred * scale, scale


def unit_rows_back(units, scale, d_units):
    spread = jnp.mean(d_units * units, axis=1, keepdims=True)
    return scale * (d_units - jnp.mean(d_units, axis=1, keepdims=True) - units * spread)


def column_sum(values):
    return jnp.sum(values.astype(f32), axis=0, keepdims=True)


def middle_kernel(
    live,
    tile,
    begin_ref,
    context_ref,
    w_out_ref,
    w_in_ref,
    w_back_ref,
    small_ref,
    hidden_bias_ref,
    slot_ref,
    slot_grad_ref,
    layer_ref,
    g_in_ref,
    g_back_ref,
    g_out_ref,
    d_pre_ref,
    d_context_ref,
    sums_ref,
    hidden_sum_ref,
    act_ref,
    slope_ref,
    rows_t_ref,
):
    count, width = begin_ref.shape
    hidden = w_back_ref.shape[0]
    tiles = hidden // tile
    row = lambda i: small_ref[i : i + 1, :]
    attended = dot(context_ref[...], w_out_ref[...]) + row(2)
    units, scale = unit_rows(begin_ref[...] + attended)
    mid = units * row(6) + row(3)
    mid_rows = mid.astype(bf16)
    rows_t_ref[...] = mid.T.astype(bf16)

    def forward_tile(step, total):
        at = pl.ds(pl.multiple_of(step * tile, tile), tile)
        inner = dot(mid_rows, w_in_ref[:, at]) + hidden_bias_ref[:, at]
        share = 0.5 * lax.erf(inner * (2.0**-0.5)) + 0.5
        bell = jnp.exp(inner * inner * -0.5) * (0.5 * 2.0**0.5 / jnp.pi**0.5)
        act = (inner * share).astype(bf16)
        act_ref[:, at] = act
        slope_ref[:, at] = (share + inner * bell).astype(bf16)
        return total + dot(act, w_back_ref[at, :])

    outer = lax.fori_loop(0, tiles, forward_tile, jnp.zeros((count, width), f32))
    out_units, out_scale = unit_rows(mid + outer + row(4))
    layer_ref[...] = (out_units * row(7) + row(5)).astype(bf16)

    token_ids = lax.broadcasted_iota(jnp.int32, (count, slot_ref.shape[1]), 0)
    slot_hot = jnp.where(slot_ref[...] == token_ids, 1.0, 0.0).astype(bf16)
    out_cot = dot(slot_hot, slot_grad_ref[...])
    d_sum = unit_rows_back(out_units, out_scale, out_cot * row(7))
    d_outer = d_sum.astype(bf16)

    def backward_tile(step, total):
        at = pl.ds(pl.multiple_of(step * tile, tile), tile)
        d_act = dot_nt(d_outer, w_back_ref[at, :])
        d_inner = (d_act * slope_ref[:, at].astype(f32)).astype(bf16)
        g_back_ref[at, :] = dot_tn(act_ref[:, at], d_outer).astype(bf16)
        g_in_ref[:, at] = dot(rows_t_ref[...], d_inner).astype(bf16)
        hidden_sum_ref[:, at] = column_sum(d_inner)
        return total + dot_nt(d_inner, w_in_ref[:, at])

    d_mid = lax.fori_loop(0, tiles, backward_tile, d_sum)
    d_pre = unit_rows_back(units, scale, d_mid * row(6))
    d_pre_ref[...] = d_pre
    d_att = d_pre.astype(bf16)
    g_out_ref[...] = dot_tn(context_ref[...], d_att).astype(bf16)
    d_context_ref[...] = dot_nt(d_att, w_out_ref[...]).astype(bf16)
    sums_ref[0:1, :] = column_sum(d_att)
    sums_ref[1:2, :] = column_sum(d_mid)
    sums_ref[2:3, :] = column_sum(d_outer)
    sums_ref[3:4, :] = column_sum(out_cot)
    sums_ref[4:5, :] = column_sum(d_mid * units)
    sums_ref[5:6, :] = column_sum(out_cot * out_units)
    sums_ref[6:8, :] = jnp.zeros((2, width), f32)


def middle(live, begin, context, w_attn_out, w_ff_in, w_ff_out, small, hidden_bias, slots, slot_grads):
    count, width = begin.shape
    hidden = w_ff_out.shape[0]
    return pl.pallas_call(
        partial(middle_kernel, live, 512),
        out_shape=(
            jax.ShapeDtypeStruct((count, width), bf16),
            jax.ShapeDtypeStruct((width, hidden), bf16),
            jax.ShapeDtypeStruct((hidden, width), bf16),
            jax.ShapeDtypeStruct((width, width), bf16),
            jax.ShapeDtypeStruct((count, width), f32),
            jax.ShapeDtypeStruct((count, width), bf16),
            jax.ShapeDtypeStruct((8, width), f32),
            jax.ShapeDtypeStruct((1, hidden), f32),
        ),
        scratch_shapes=[
            pltpu.VMEM((count, hidden), bf16),
            pltpu.VMEM((count, hidden), bf16),
            pltpu.VMEM((width, count), bf16),
        ],
        compiler_params=params(),
        cost_estimate=cost(12 * count * width * hidden, 30e6),
    )(begin, context, w_attn_out, w_ff_in, w_ff_out, small, hidden_bias, slots, slot_grads)


def embed_back_kernel(
    d_query_ref,
    d_key_ref,
    d_value_ref,
    weight_ref,
    d_pre_ref,
    rows_ref,
    place_ref,
    input_grad_ref,
    g_qkv_ref,
    g_table_ref,
    sums_ref,
):
    count, width = rows_ref.shape
    rows_t = rows_ref[...].astype(f32).T.astype(bf16)
    total = d_pre_ref[...]
    for part, d_ref in enumerate((d_query_ref, d_key_ref, d_value_ref)):
        at = slice(part * width, (part + 1) * width)
        total += dot_nt(d_ref[...], weight_ref[:, at])
        g_qkv_ref[:, at] = dot(rows_t, d_ref[...]).astype(bf16)
    input_grad_ref[...] = total
    low = total.astype(bf16)
    half = g_table_ref.shape[0] // 2
    values = lax.broadcasted_iota(jnp.int32, (half, count), 0)
    for side in range(2):
        hot = jnp.where(place_ref[side : side + 1, :] == values, 1.0, 0.0).astype(bf16)
        g_table_ref[side * half : (side + 1) * half, :] = dot(hot, low).astype(bf16)
    sums_ref[0:1, :] = column_sum(d_query_ref[...])
    sums_ref[1:2, :] = column_sum(d_value_ref[...])
    sums_ref[2:8, :] = jnp.zeros((6, width), f32)


def embed_back(d_query, d_key, d_value, w_qkv, d_pre, begin_rows, places, table_rows):
    count, width = begin_rows.shape
    return pl.pallas_call(
        embed_back_kernel,
        out_shape=(
            jax.ShapeDtypeStruct((count, width), f32),
            jax.ShapeDtypeStruct((width, 3 * width), bf16),
            jax.ShapeDtypeStruct((table_rows, width), bf16),
            jax.ShapeDtypeStruct((8, width), f32),
        ),
        compiler_params=params(),
        cost_estimate=cost(2 * count * width * (table_rows + 6 * width), 20e6),
    )(d_query, d_key, d_value, w_qkv, d_pre, begin_rows, places)


GROUP = 8
TABLES = ((0, B1), (5, B2), (11, B2))


def table_kernel(index_ref, d_scores_ref, out_ref, total_ref):
    keys, count = d_scores_ref.shape[1:]
    columns = 2 * HEADS * GROUP

    @pl.when(pl.program_id(0) == 0)
    def _():
        total_ref[...] = jnp.zeros_like(total_ref)

    d_scores = d_scores_ref[...].astype(f32)
    packed = index_ref[:, :count]
    base = 0
    for shift, buckets in TABLES:
        bucket = lax.shift_right_logical(packed, shift) & (buckets - 1)
        upper, lowest = lax.shift_right_logical(bucket, 1), bucket & 1
        uppers = buckets // 2
        values = lax.broadcasted_iota(jnp.int32, (uppers, count), 0)
        left, right = [], []
        for first in range(0, keys, GROUP):
            group = slice(first, first + GROUP)
            left.append(
                jnp.concatenate(
                    [jnp.where(upper[k : k + 1] == values, 1.0, 0.0).astype(bf16) for k in range(first, first + GROUP)],
                    axis=0,
                )
            )
            right.append(
                jnp.concatenate(
                    [
                        jnp.where((lowest[group] == bit)[None], d_scores[:, group, :], 0.0).reshape(
                            HEADS * GROUP, count
                        )
                        for bit in range(2)
                    ],
                    axis=0,
                ).astype(bf16)
            )
        total_ref[base : base + uppers * GROUP, :] += dot_nt(
            jnp.concatenate(left, axis=1), jnp.concatenate(right, axis=1)
        )
        base += uppers * GROUP

    @pl.when(pl.program_id(0) == pl.num_programs(0) - 1)
    def _():
        base, pieces = 0, []
        for _, buckets in TABLES:
            shape = (GROUP, buckets // 2, columns)
            block = total_ref[base : base + shape[0] * shape[1], :].reshape(shape)
            own = lax.broadcasted_iota(jnp.int32, shape, 2) % GROUP == lax.broadcasted_iota(jnp.int32, shape, 0)
            pieces.append(jnp.sum(jnp.where(own, block, 0.0), axis=0))
            base += shape[0] * shape[1]
        out_ref[...] = jnp.concatenate(pieces, axis=0)


def table_grad(packed, d_scores):
    count = packed.shape[0]
    keys = 32
    uppers = (B1 + 2 * B2) // 2
    columns = 2 * HEADS * GROUP
    folded = pl.pallas_call(
        table_kernel,
        grid=(count // keys,),
        in_specs=[
            pl.BlockSpec((keys, packed.shape[1]), lambda i: (i, 0)),
            pl.BlockSpec((HEADS, keys, count), lambda i: (0, i, 0)),
        ],
        out_specs=full((uppers, columns)),
        out_shape=jax.ShapeDtypeStruct((uppers, columns), f32),
        scratch_shapes=[pltpu.VMEM((uppers * GROUP, columns), f32)],
        compiler_params=params(),
        cost_estimate=cost(2e10, 2 * HEADS * count * count),
    )(packed, d_scores)
    return folded.reshape(uppers, 2, HEADS, GROUP).sum(axis=3).reshape(2 * uppers, HEADS)


def swap(values, bit, devices):
    return lax.ppermute(values, AXES, [(i, i ^ bit) for i in range(devices)])


def reduce_blocks(blocks, bits, index, devices):
    order = []
    width = devices
    open_bits = []
    b = 1
    while b < devices:
        open_bits.append(b)
        b *= 2
    for bit in bits:
        place = open_bits.index(bit)
        inner = 2**place
        outer = 2 ** (len(open_bits) - 1 - place)
        view = blocks.reshape((outer, 2, inner) + blocks.shape[1:])
        mine = (index // bit) % 2
        away = lax.dynamic_index_in_dim(view, 1 - mine, axis=1, keepdims=False)
        keep = lax.dynamic_index_in_dim(view, mine, axis=1, keepdims=False)
        came = swap(away, bit, devices)
        summed = (keep.astype(f32) + came.astype(f32)).astype(blocks.dtype)
        blocks = summed.reshape((outer * inner,) + blocks.shape[1:])
        open_bits.pop(place)
    return blocks[0]


def sum_everywhere(values, bits, devices):
    for bit in bits:
        values = values + swap(values, bit, devices)
    return values


def to_blocks(grad, devices, width):
    rows, columns = grad.shape
    parts = columns // width
    blocks = grad.reshape(devices, rows // devices, parts, width)
    return blocks.transpose(0, 2, 1, 3).reshape(devices, parts * (rows // devices), width)


def from_block(block, parts):
    rows, width = block.shape
    return block.reshape(parts, rows // parts, width).transpose(1, 0, 2).reshape(rows // parts, parts * width)


def from_blocks(blocks, parts):
    devices, rows, width = blocks.shape
    split = blocks.reshape(devices, parts, rows // parts, width)
    return split.transpose(0, 2, 1, 3).reshape(devices * (rows // parts), parts * width)


def on_device(
    devices,
    bits,
    tokens,
    coords,
    rel_pos,
    rel_box,
    entity_pairs,
    entity_grad,
    w_qkv,
    w_attn_out,
    dcpe_table,
    biases,
    norm_gains,
    w_ff_in,
    w_ff_out,
    ff_bias,
    rel_table,
):
    live, width = tokens.shape[1], tokens.shape[2]
    hidden = ff_bias.shape[0] * devices
    count = -(-live // 64) * 64
    extra = count - live
    index = lax.axis_index(AXES)
    shard = biases.shape[1]

    small_own = jnp.zeros((8, width), bf16)
    small_own = small_own.at[:6, :shard].set(biases).at[6:8, :shard].set(norm_gains)
    small_own = small_own.at[0, 128 : 128 + ff_bias.shape[0]].set(ff_bias)
    first_own = jnp.concatenate([from_block_rows(w_qkv, width), w_attn_out, dcpe_table, small_own], axis=0)
    second_own = jnp.concatenate([from_block_rows(w_ff_in, width), w_ff_out], axis=0)
    first = lax.all_gather(first_own, AXES, axis=0)
    second = lax.all_gather(second_own, AXES, axis=0)

    packed = rel_pos[0] + rel_box[0, 0] * 32 + rel_box[0, 1] * 2048
    packed = jnp.pad(packed.T, ((0, extra), (0, -(-count // 128) * 128 - live)))
    bias = score_bias(packed, rel_table, live)
    places = jnp.pad(coords[0], ((0, 0), (0, extra)), constant_values=OUTSIDE)
    slots = entity_pairs.reshape(1, -1)
    slot_grads = entity_grad.reshape(slots.shape[1], width)
    padded = jnp.pad(tokens[0], ((0, extra), (0, 0)))

    q_rows, o_rows, t_rows = 3 * w_qkv.shape[0], w_attn_out.shape[0], dcpe_table.shape[0]
    full_qkv = from_blocks(first[:, :q_rows], 3)
    full_out = first[:, q_rows : q_rows + o_rows].reshape(width, width)
    full_table = first[:, q_rows + o_rows : q_rows + o_rows + t_rows].reshape(-1, width)
    small_all = first[:, q_rows + o_rows + t_rows :]
    small = small_all[:, :, :shard].transpose(1, 0, 2).reshape(8, width).astype(f32)
    hidden_bias = small_all[:, 0, 128 : 128 + ff_bias.shape[0]].reshape(1, hidden).astype(f32)
    f_rows = second_own.shape[0] - w_ff_out.shape[0]
    full_in = from_blocks(second[:, :f_rows], hidden // width)
    full_back = second[:, f_rows:].reshape(hidden, width)

    begin, begin_rows, united = embed(padded, places.T, full_table, full_qkv, small)
    attention, context = attend(united, bias)
    layer_out, g_in, g_back, g_out, d_pre, d_context, sums, hidden_sum = middle(
        live, begin, context, full_out, full_in, full_back, small, hidden_bias, slots, slot_grads
    )
    ff_blocks = jnp.concatenate([to_blocks(g_in, devices, width), g_back.reshape(devices, -1, width)], axis=1)
    ff_own = reduce_blocks(ff_blocks, bits, index, devices)

    d_query, d_key, d_value, d_scores = attend_back(united, attention, d_context)
    input_grad, g_qkv, g_table, more_sums = embed_back(
        d_query, d_key, d_value, full_qkv, d_pre, begin_rows, places, full_table.shape[0]
    )
    grads = jnp.concatenate([more_sums[:2], sums[:6]], axis=0)
    small_blocks = jnp.zeros((devices, 8, width), bf16)
    small_blocks = small_blocks.at[:, :, :shard].set(grads.reshape(8, devices, shard).transpose(1, 0, 2).astype(bf16))
    small_blocks = small_blocks.at[:, 0, 128 : 128 + ff_bias.shape[0]].set(
        hidden_sum.reshape(devices, ff_bias.shape[0]).astype(bf16)
    )
    blocks = jnp.concatenate(
        [
            to_blocks(g_qkv, devices, width),
            g_out.reshape(devices, -1, width),
            g_table.reshape(devices, -1, width),
            small_blocks,
        ],
        axis=1,
    )
    own = reduce_blocks(blocks, bits, index, devices).astype(f32)
    table_sum = sum_everywhere(table_grad(packed, d_scores), bits, devices)
    small_sum = own[q_rows + o_rows + t_rows :]
    ff_own = ff_own.astype(f32)
    return (
        layer_out[None, :live],
        input_grad[None, :live],
        from_block(own[:q_rows], 3),
        own[q_rows : q_rows + o_rows],
        own[q_rows + o_rows : q_rows + o_rows + t_rows],
        small_sum[:6, :shard],
        small_sum[6:8, :shard],
        from_block(ff_own[:f_rows], hidden // width),
        ff_own[f_rows:],
        small_sum[0, 128 : 128 + ff_bias.shape[0]],
        table_sum,
    )


def from_block_rows(shard, width):
    rows, columns = shard.shape
    return shard.reshape(rows, columns // width, width).transpose(1, 0, 2).reshape(-1, width)


def solution(mesh):
    outer, inner = mesh.shape["dp"], mesh.shape["fsdp"]
    devices = outer * inner
    bits = [inner] + [1 << k for k in range(devices.bit_length() - 1) if 1 << k != inner]
    rows = P(AXES, None)
    three = P(AXES, None, None)
    four = P(AXES, None, None, None)
    columns = P(None, AXES)
    return jax.shard_map(
        partial(on_device, devices, bits),
        mesh=mesh,
        in_specs=(three, three, three, four, three, four, rows, rows, rows, columns, columns, rows, rows, P(AXES), P()),
        out_specs=(three, three, rows, rows, rows, columns, columns, rows, rows, P(AXES), P()),
        check_vma=False,
    )
```

```python
from functools import partial

import jax
import jax.numpy as jnp
from jax import lax
from jax.experimental import pallas as pl
from jax.experimental.pallas import tpu as pltpu
from jax.sharding import Mesh
from jax.sharding import PartitionSpec as P

HEADS = 12
HEAD_DIM = 64
B1 = 32
B2 = 64
PAIR = 2 * HEAD_DIM
EPSILON = 1e-05
VMEM_LIMIT = 58 * 2**20
NEVER = -1e30
OUTSIDE = -4096

bf16 = jnp.bfloat16
f32 = jnp.float32


def dot(a, b):
    return jnp.dot(a, b, preferred_element_type=f32)


def dot_nt(a, b):
    return lax.dot_general(a, b, (((1,), (1,)), ((), ())), preferred_element_type=f32)


def dot_tn(a, b):
    return lax.dot_general(a, b, (((0,), (0,)), ((), ())), preferred_element_type=f32)


def params():
    return pltpu.CompilerParams(vmem_limit_bytes=VMEM_LIMIT)


def cost(flops, moved):
    return pl.CostEstimate(flops=int(flops / 1000), bytes_accessed=int(moved / 1000), transcendentals=0)


def waits(arrays):
    return [pl.BlockSpec(memory_space=pl.ANY)] * len(arrays)


def full(shape):
    return pl.BlockSpec(shape, lambda *_: (0,) * len(shape))


def bias_kernel(live, index_ref, table_ref, out_ref):
    rows, width = out_ref.shape[1:]
    first_row = pl.program_id(0) * rows
    tables = [jnp.broadcast_to(table_ref[r : r + 1, :], (8, 128)) for r in range(2 * HEADS)]

    def eight_rows(step, carry):
        at = pl.multiple_of(step * 8, 8)
        key_ids = first_row + at + lax.broadcasted_iota(jnp.int32, (8, 128), 0)
        dead = jnp.where(key_ids < live, 0.0, NEVER)
        for left in range(0, width, 128):
            packed = index_ref[pl.ds(at, 8), left : left + 128]
            flat = packed & (B1 - 1)
            across = (lax.shift_right_logical(packed, 5) & (B2 - 1)) + B1
            downward = lax.shift_right_logical(packed, 11)
            for head in range(HEADS):
                low, high = tables[2 * head], tables[2 * head + 1]
                looked = (
                    jnp.take_along_axis(low, flat, axis=1, mode="promise_in_bounds")
                    + jnp.take_along_axis(low, across, axis=1, mode="promise_in_bounds")
                    + jnp.take_along_axis(high, downward, axis=1, mode="promise_in_bounds")
                    + dead
                )
                right = min(left + 128, width)
                out_ref[head, pl.ds(at, 8), left:right] = looked[:, : right - left]
        return carry

    lax.fori_loop(0, rows // 8, eight_rows, 0)


def score_bias(packed, rel_table, live):
    keys = width = packed.shape[0]
    rows = 64
    lookup = jnp.zeros((HEADS, 2, 128), f32)
    lookup = lookup.at[:, 0, : B1 + B2].set(rel_table[: B1 + B2].T.astype(f32))
    lookup = lookup.at[:, 1, :B2].set(rel_table[B1 + B2 :].T.astype(f32))
    return pl.pallas_call(
        partial(bias_kernel, live),
        grid=(keys // rows,),
        in_specs=[pl.BlockSpec((rows, packed.shape[1]), lambda i: (i, 0)), full((2 * HEADS, 128))],
        out_specs=pl.BlockSpec((HEADS, rows, width), lambda i: (0, i, 0)),
        out_shape=jax.ShapeDtypeStruct((HEADS, keys, width), f32),
        compiler_params=params(),
        cost_estimate=cost(3e10, 4 * HEADS * keys * width),
    )(packed, lookup.reshape(2 * HEADS, 128))


def embed_kernel(
    token_ref, place_ref, table_ref, query_ref, key_ref, value_ref, small_ref, begin_ref, rows_ref, united_ref
):
    half = table_ref.shape[0] // 2
    width = token_ref.shape[1]
    columns = lax.broadcasted_iota(jnp.int32, (token_ref.shape[0], half), 1)
    total = token_ref[...].astype(f32)
    for side in range(2):
        hot = jnp.where(place_ref[:, side : side + 1] == columns, 1.0, 0.0).astype(bf16)
        total += dot(hot, table_ref[side * half : (side + 1) * half, :])
    begin_ref[...] = total
    rows = total.astype(bf16)
    rows_ref[...] = rows
    query = dot(rows, query_ref[...]) + small_ref[0:1, :]
    united_ref[:, :width] = (query * 0.125).astype(bf16)
    united_ref[:, width : 2 * width] = dot(rows, key_ref[...]).astype(bf16)
    value = dot(rows, value_ref[...]) + small_ref[1:2, :]
    united_ref[:, 2 * width :] = value.astype(bf16)


def embed(tokens, places, dcpe_table, w_qkv, small):
    count, width = tokens.shape
    return pl.pallas_call(
        embed_kernel,
        out_shape=(
            jax.ShapeDtypeStruct((count, width), f32),
            jax.ShapeDtypeStruct((count, width), bf16),
            jax.ShapeDtypeStruct((count, 3 * width), bf16),
        ),
        compiler_params=params(),
        cost_estimate=cost(2 * count * width * (dcpe_table.shape[0] + 3 * width), 12e6),
    )(tokens, places, dcpe_table, *w_qkv, small)


def head_mask(head):
    return lax.broadcasted_iota(jnp.int32, (1, PAIR), 1) // HEAD_DIM == head


def attend_kernel(query_ref, key_ref, value_ref, bias_ref, attention_ref, context_ref):
    query, key = query_ref[...], key_ref[...]
    value_t = value_ref[...].astype(f32).T.astype(bf16)
    parts = []
    for head in range(2):
        scores = dot_nt(jnp.where(head_mask(head), key, 0), query) + bias_ref[head]
        raised = jnp.exp(scores - jnp.max(scores, axis=0, keepdims=True))
        attention = (raised * (1.0 / jnp.sum(raised, axis=0, keepdims=True))).astype(bf16)
        attention_ref[head] = attention
        parts.append(dot(value_t[head * HEAD_DIM : (head + 1) * HEAD_DIM], attention))
    context_ref[...] = jnp.concatenate(parts, axis=0).T.astype(bf16)


def attend(united, bias):
    count = united.shape[0]
    pairs = HEADS // 2
    column = lambda shift: pl.BlockSpec((count, PAIR), lambda p: (0, p + shift))
    square = pl.BlockSpec((2, count, count), lambda p: (p, 0, 0))
    return pl.pallas_call(
        attend_kernel,
        grid=(pairs,),
        in_specs=[column(0), column(pairs), column(2 * pairs), square],
        out_specs=(square, column(0)),
        out_shape=(
            jax.ShapeDtypeStruct((HEADS, count, count), bf16),
            jax.ShapeDtypeStruct((count, HEADS * HEAD_DIM), bf16),
        ),
        compiler_params=params(),
        cost_estimate=cost(4 * HEADS * count * count * HEAD_DIM, 6 * HEADS * count * count),
    )(united, united, united, bias)


def attend_back_kernel(query_ref, key_ref, value_ref, attention_ref, d_context_ref, *refs):
    d_query_ref, d_key_ref, d_value_ref, d_scores_ref = refs[-4:]
    query, value, d_context = query_ref[...], value_ref[...], d_context_ref[...]
    key_t = key_ref[...].astype(f32).T.astype(bf16)
    parts = []
    d_key = jnp.zeros(query.shape, f32)
    d_value = jnp.zeros(query.shape, f32)
    for head in range(2):
        mask = head_mask(head)
        d_attention = dot_nt(jnp.where(mask, value, 0), d_context)
        attention_low = attention_ref[head]
        attention = attention_low.astype(f32)
        centre = jnp.sum(attention * d_attention, axis=0, keepdims=True)
        d_scores = (attention * (d_attention - centre)).astype(bf16)
        d_scores_ref[head] = d_scores
        d_key += dot(d_scores, jnp.where(mask, query, 0))
        d_value += dot(attention_low, jnp.where(mask, d_context, 0))
        parts.append(dot(key_t[head * HEAD_DIM : (head + 1) * HEAD_DIM], d_scores))
    d_query_ref[...] = jnp.concatenate(parts, axis=0).T.astype(bf16) * bf16(0.125)
    d_key_ref[...] = d_key.astype(bf16)
    d_value_ref[...] = d_value.astype(bf16)


def attend_back(united, attention, d_context, first, last, after=()):
    count = united.shape[0]
    pairs = HEADS // 2
    column = lambda shift: pl.BlockSpec((count, PAIR), lambda p: (0, p + shift))
    square = lambda shift: pl.BlockSpec((2, count, count), lambda p: (p + shift, 0, 0))
    joined = jax.ShapeDtypeStruct((count, (last - first) * PAIR), bf16)
    return pl.pallas_call(
        attend_back_kernel,
        grid=(last - first,),
        in_specs=[column(first), column(first + pairs), column(first + 2 * pairs), square(first), column(first)]
        + waits(after),
        out_specs=(column(0), column(0), column(0), square(0)),
        out_shape=(joined, joined, joined, jax.ShapeDtypeStruct((2 * (last - first), count, count), bf16)),
        compiler_params=params(),
        cost_estimate=cost(8 * HEADS * count * count * HEAD_DIM, 4 * HEADS * count * count),
    )(united, united, united, attention, d_context, *after)


def unit_rows(values):
    centred = values - jnp.mean(values, axis=1, keepdims=True)
    scale = lax.rsqrt(jnp.mean(centred * centred, axis=1, keepdims=True) + EPSILON)
    return centred * scale, scale


def unit_rows_back(units, scale, d_units):
    spread = jnp.mean(d_units * units, axis=1, keepdims=True)
    return scale * (d_units - jnp.mean(d_units, axis=1, keepdims=True) - units * spread)


def column_sum(values):
    return jnp.sum(values.astype(f32), axis=0, keepdims=True)


def split_cores(values, rows):
    inner = values.shape[0] // rows
    return values.reshape((inner // 4, 2, 2, rows, values.shape[1]))


def middle_kernel(packed, place_ref, begin_ref, context_ref, w_out_ref, w_in_hbm, w_back_hbm, *refs):
    (
        small_ref,
        hidden_bias_ref,
        slot_ref,
        slot_grad_ref,
        layer_ref,
        g_one_ref,
        g_two_ref,
        g_out_ref,
        d_pre_ref,
        d_context_ref,
        sums_ref,
        hidden_sum_ref,
        w_in_ref,
        w_back_ref,
        act_ref,
        slope_ref,
        d_inner_ref,
        total_ref,
        load_sems,
    ), refs = refs[:19], refs[19:]
    count, width = begin_ref.shape
    parts = w_in_ref.shape[0]

    def load_in(part):
        return pltpu.make_async_copy(w_in_hbm.at[part], w_in_ref.at[part], load_sems.at[part])

    def load_back(part):
        return pltpu.make_async_copy(w_back_hbm.at[part], w_back_ref.at[part], load_sems.at[parts + part])

    for part in range(parts):
        load_in(part).start()
        load_back(part).start()

    row = lambda i: small_ref[i : i + 1, :]
    attended = dot(context_ref[...], w_out_ref[...]) + row(2)
    units, scale = unit_rows(begin_ref[...] + attended)
    mid = units * row(6) + row(3)
    mid_rows = mid.astype(bf16)
    total_ref[...] = mid + row(4)

    def forward_part(part, carry):
        load_in(part).wait()
        inner = dot(mid_rows, w_in_ref[part]) + hidden_bias_ref[pl.ds(part, 1), :]
        share = 0.5 * lax.erf(inner * (2.0**-0.5)) + 0.5
        bell = jnp.exp(inner * inner * -0.5) * (0.5 * 2.0**0.5 / jnp.pi**0.5)
        act = (inner * share).astype(bf16)
        act_ref[part] = act
        slope_ref[part] = (share + inner * bell).astype(bf16)
        load_back(part).wait()
        total_ref[...] += dot(act, w_back_ref[part])
        return carry

    lax.fori_loop(0, parts, forward_part, 0)
    out_units, out_scale = unit_rows(total_ref[...])
    layer_ref[...] = (out_units * row(7) + row(5)).astype(bf16)[: layer_ref.shape[0]]

    token_ids = lax.broadcasted_iota(jnp.int32, (count, slot_ref.shape[1]), 0)
    slot_hot = jnp.where(slot_ref[...] == token_ids, 1.0, 0.0).astype(bf16)
    out_cot = dot(slot_hot, slot_grad_ref[...])
    sums_ref[3:4, :] = column_sum(out_cot)
    sums_ref[5:6, :] = column_sum(out_cot * out_units)
    d_sum = unit_rows_back(out_units, out_scale, out_cot * row(7))
    sums_ref[2:3, :] = column_sum(d_sum.astype(bf16))
    d_outer = d_sum.astype(bf16)
    total_ref[...] = d_sum
    rows_t = mid.T.astype(bf16)
    if packed:
        buffer_ref, store_sems = refs
        core = place_ref[2]
        devices = buffer_ref.shape[1] * 4
        d_rows, h_rows = width // devices, width * parts // devices
        blocks_each = width // h_rows // 4

    def stores(at, rows, first, blocks, sem):
        copies = []
        for side, target in enumerate((g_one_ref, g_two_ref)):
            source = buffer_ref.at[side, pl.ds(first, blocks), :, pl.ds(at, rows)]
            target = target.at[pl.ds(first, blocks), :, pl.ds(at, rows)]
            copies.append(pltpu.make_async_copy(source, target, store_sems.at[side, sem]))
        return copies

    def store_back(part):
        return stores(parts * d_rows, h_rows, part * blocks_each, blocks_each, part)

    def store_in(pair):
        return stores(pl.multiple_of(pair * 2 * d_rows, 16), 2 * d_rows, 0, devices // 4, parts + pair)

    def backward_part(part, carry):
        d_act = dot_nt(d_outer, w_back_ref[part])
        d_inner = (d_act * slope_ref[part].astype(f32)).astype(bf16)
        hidden_sum_ref[pl.ds(part, 1), :] = column_sum(d_inner)
        total_ref[...] += dot_nt(d_inner, w_in_ref[part])
        d_inner_ref[part] = d_inner
        g_back = dot_tn(act_ref[part], d_outer).astype(bf16)
        if packed:
            blocks = split_cores(g_back, h_rows)
            at = pl.ds(part * blocks_each, blocks_each)
            for side in range(2):
                buffer_ref[side ^ core, at, :, parts * d_rows :] = blocks[:, side]
            for copy in store_back(part):
                copy.start()
        else:
            g_two_ref[part] = g_back
            g_one_ref[part] = dot(rows_t, d_inner).astype(bf16)
        return carry

    lax.fori_loop(0, parts, backward_part, 0)

    def pack_pair(pair, carry):
        at = pl.ds(pl.multiple_of(pair * 2 * d_rows, 16), 2 * d_rows)
        for left in range(0, width, 256):
            columns = slice(left, left + 256)
            pieces = [
                dot(rows_t, d_inner_ref[2 * pair + which, :, columns]).reshape(devices, d_rows, 256)
                for which in range(2)
            ]
            joined = jnp.concatenate(pieces, axis=1).astype(bf16).reshape(devices // 4, 2, 2, 2 * d_rows, 256)
            for side in range(2):
                buffer_ref[side ^ core, :, :, at, columns] = joined[:, side]
        for copy in store_in(pair):
            copy.start()
        return carry

    if packed:
        lax.fori_loop(0, parts // 2, pack_pair, 0)

    d_mid = total_ref[...]
    d_pre = unit_rows_back(units, scale, d_mid * row(6))
    d_pre_ref[...] = d_pre
    d_att = d_pre.astype(bf16)
    g_out_ref[...] = dot_tn(context_ref[...], d_att).astype(bf16)
    d_context_ref[...] = dot_nt(d_att, w_out_ref[...]).astype(bf16)
    sums_ref[0:1, :] = column_sum(d_att)
    sums_ref[1:2, :] = column_sum(d_mid)
    sums_ref[4:5, :] = column_sum(d_mid * units)
    sums_ref[6:8, :] = jnp.zeros((2, width), f32)
    if packed:
        for part in range(parts):
            for copy in store_back(part):
                copy.wait()
        for pair in range(parts // 2):
            for copy in store_in(pair):
                copy.wait()


def middle(place, packed, devices, live, begin, context, w_attn_out, w_ff_in, w_ff_out, small, hidden_bias, slots, slot_grads):
    count, width = begin.shape
    parts = w_ff_in.shape[0]
    hidden = parts * width
    vmem = pl.BlockSpec(memory_space=pltpu.VMEM)
    away = pl.BlockSpec(memory_space=pl.ANY)
    scratch = [
        pltpu.VMEM((parts, width, width), bf16),
        pltpu.VMEM((parts, width, width), bf16),
        pltpu.VMEM((parts, count, width), bf16),
        pltpu.VMEM((parts, count, width), bf16),
        pltpu.VMEM((parts, count, width), bf16),
        pltpu.VMEM((count, width), f32),
        pltpu.SemaphoreType.DMA((2 * parts,)),
    ]
    if packed:
        half = (devices // 4, 2, 2 * hidden // devices, width)
        grads = (jax.ShapeDtypeStruct(half, bf16),) * 2
        scratch += [pltpu.VMEM((2,) + half, bf16), pltpu.SemaphoreType.DMA((2, parts + parts // 2))]
    else:
        grads = (jax.ShapeDtypeStruct((parts, width, width), bf16),) * 2
    grad_space = away if packed else vmem
    return pl.pallas_call(
        partial(middle_kernel, packed),
        in_specs=[pl.BlockSpec(memory_space=pltpu.SMEM)] + [vmem] * 3 + [away] * 2 + [vmem] * 4,
        out_specs=(vmem, grad_space, grad_space) + (vmem,) * 5,
        out_shape=(jax.ShapeDtypeStruct((live, width), bf16),)
        + grads
        + (
            jax.ShapeDtypeStruct((width, width), bf16),
            jax.ShapeDtypeStruct((count, width), f32),
            jax.ShapeDtypeStruct((count, width), bf16),
            jax.ShapeDtypeStruct((8, width), f32),
            jax.ShapeDtypeStruct((parts, width), f32),
        ),
        scratch_shapes=scratch,
        compiler_params=params(),
        cost_estimate=cost(12 * count * width * hidden, 30e6),
    )(place, begin, context, w_attn_out, w_ff_in, w_ff_out, small, hidden_bias, slots, slot_grads)


def embed_back_kernel(halves, packed, place_ref, *refs):
    d_refs, refs = refs[: 3 * halves], refs[3 * halves :]
    w_hbm, refs = refs[:3], refs[3:]
    g_out_ref, d_pre_ref, rows_ref, coords_ref = refs[:4]
    scratch = 4 if packed else 2
    input_grad_ref, g_one_ref, g_two_ref, sums_ref = refs[-4 - scratch : -scratch]
    w_ref, load_sems = refs[-scratch:][:2]
    count, width = rows_ref.shape
    loads = [pltpu.make_async_copy(w_hbm[part], w_ref.at[part], load_sems.at[part]) for part in range(3)]
    for copy in loads:
        copy.start()
    rows_t = rows_ref[...].astype(f32).T.astype(bf16)
    grads = [
        jnp.concatenate([d_refs[3 * half + part][...] for half in range(halves)], axis=1) for part in range(3)
    ]
    total = d_pre_ref[...]
    for part in range(3):
        loads[part].wait()
        total += dot_nt(grads[part], w_ref[part])
    input_grad_ref[...] = total
    low = total.astype(bf16)
    sums_ref[...] = jnp.zeros((8, width), f32)
    sums_ref[0:1, :] = column_sum(grads[0])
    sums_ref[1:2, :] = column_sum(grads[2])

    if packed:
        buffer_ref, store_sems = refs[-2:]
        core = place_ref[2]
        devices = buffer_ref.shape[1] * 4
        d_rows = width // devices
        t_rows = buffer_ref.shape[3] - 4 * d_rows
        stores = []

        def store(at, rows, first, last):
            for side, target in enumerate((g_one_ref, g_two_ref)):
                source = buffer_ref.at[side, pl.ds(first, last - first), :, pl.ds(at, rows)]
                target = target.at[pl.ds(first, last - first), :, pl.ds(at, rows)]
                copy = pltpu.make_async_copy(source, target, store_sems.at[len(stores)])
                copy.start()
                stores.append(copy)

    half = g_two_ref.shape[0] // 2 if not packed else t_rows * devices // 2
    values = lax.broadcasted_iota(jnp.int32, (half, count), 0)
    for side in range(2):
        hot = jnp.where(coords_ref[side : side + 1, :] == values, 1.0, 0.0).astype(bf16)
        g_table = dot(hot, low).astype(bf16)
        if packed:
            blocks = split_cores(g_table, t_rows)
            first = side * blocks.shape[0]
            for which in range(2):
                buffer_ref[which ^ core, first : first + blocks.shape[0], :, 4 * d_rows :] = blocks[:, which]
            store(4 * d_rows, t_rows, first, first + blocks.shape[0])
        else:
            g_two_ref[side * half : (side + 1) * half, :] = g_table
    if packed:
        for left in range(0, width, 256):
            columns = slice(left, left + 256)
            pieces = [dot(rows_t, grad[:, columns]).reshape(devices, d_rows, 256) for grad in grads]
            pieces.append(g_out_ref[:, columns].astype(f32).reshape(devices, d_rows, 256))
            joined = jnp.concatenate(pieces, axis=1).astype(bf16).reshape(devices // 4, 2, 2, 4 * d_rows, 256)
            for which in range(2):
                buffer_ref[which ^ core, :, :, : 4 * d_rows, columns] = joined[:, which]
        store(0, 4 * d_rows, 0, devices // 4)
        for copy in stores:
            copy.wait()
    else:
        for part in range(3):
            g_one_ref[:, part * width : (part + 1) * width] = dot(rows_t, grads[part]).astype(bf16)


def embed_back(place, packed, devices, d_halves, w_qkv, g_out, d_pre, begin_rows, coords, table_rows, after=()):
    count, width = begin_rows.shape
    vmem = pl.BlockSpec(memory_space=pltpu.VMEM)
    away = pl.BlockSpec(memory_space=pl.ANY)
    d_all = [d for half in d_halves for d in half]
    scratch = [pltpu.VMEM((3, width, width), bf16), pltpu.SemaphoreType.DMA((3,))]
    if packed:
        half = (devices // 4, 2, 4 * (width // devices) + table_rows // devices, width)
        grads = (jax.ShapeDtypeStruct(half, bf16),) * 2
        scratch += [pltpu.VMEM((2,) + half, bf16), pltpu.SemaphoreType.DMA((6,))]
    else:
        grads = (
            jax.ShapeDtypeStruct((width, 3 * width), bf16),
            jax.ShapeDtypeStruct((table_rows, width), bf16),
        )
    grad_space = away if packed else vmem
    return pl.pallas_call(
        partial(embed_back_kernel, len(d_halves), packed),
        in_specs=[pl.BlockSpec(memory_space=pltpu.SMEM)]
        + [vmem] * len(d_all)
        + [away] * 3
        + [vmem] * 4
        + waits(after),
        out_specs=(vmem, grad_space, grad_space, vmem),
        out_shape=(jax.ShapeDtypeStruct((count, width), f32),)
        + grads
        + (jax.ShapeDtypeStruct((8, width), f32),),
        scratch_shapes=scratch,
        compiler_params=params(),
        cost_estimate=cost(2 * count * width * (table_rows + 6 * width), 20e6),
    )(place, *d_all, *w_qkv, g_out, d_pre, begin_rows, coords, *after)


GROUP = 8
TABLES = ((0, B1), (5, B2), (11, B2))


def table_kernel(halves, index_ref, *refs):
    d_refs = refs[:halves]
    out_ref, total_ref = refs[-2:]
    keys, count = d_refs[0].shape[1:]
    columns = 2 * HEADS * GROUP

    @pl.when(pl.program_id(0) == 0)
    def _():
        total_ref[...] = jnp.zeros_like(total_ref)

    d_scores = jnp.concatenate([d_ref[...].astype(f32) for d_ref in d_refs], axis=0)
    packed = index_ref[:, :count]
    base = 0
    for shift, buckets in TABLES:
        bucket = lax.shift_right_logical(packed, shift) & (buckets - 1)
        upper, lowest = lax.shift_right_logical(bucket, 1), bucket & 1
        uppers = buckets // 2
        values = lax.broadcasted_iota(jnp.int32, (uppers, count), 0)
        left, right = [], []
        for first in range(0, keys, GROUP):
            group = slice(first, first + GROUP)
            hot = [jnp.where(upper[k : k + 1] == values, 1.0, 0.0).astype(bf16) for k in range(first, first + GROUP)]
            left.append(jnp.concatenate(hot, axis=0))
            split = [
                jnp.where((lowest[group] == bit)[None], d_scores[:, group, :], 0.0).reshape(HEADS * GROUP, count)
                for bit in range(2)
            ]
            right.append(jnp.concatenate(split, axis=0).astype(bf16))
        total_ref[base : base + uppers * GROUP, :] += dot_nt(
            jnp.concatenate(left, axis=1), jnp.concatenate(right, axis=1)
        )
        base += uppers * GROUP

    @pl.when(pl.program_id(0) == pl.num_programs(0) - 1)
    def _():
        base, pieces = 0, []
        for _, buckets in TABLES:
            shape = (GROUP, buckets // 2, columns)
            block = total_ref[base : base + shape[0] * shape[1], :].reshape(shape)
            own = lax.broadcasted_iota(jnp.int32, shape, 2) % GROUP == lax.broadcasted_iota(jnp.int32, shape, 0)
            pieces.append(jnp.sum(jnp.where(own, block, 0.0), axis=0))
            base += shape[0] * shape[1]
        out_ref[...] = jnp.concatenate(pieces, axis=0)


def table_grad(packed, d_halves, first, last, after=()):
    count = packed.shape[0]
    keys = 32
    uppers = (B1 + 2 * B2) // 2
    columns = 2 * HEADS * GROUP
    return pl.pallas_call(
        partial(table_kernel, len(d_halves)),
        grid=(last - first,),
        in_specs=[pl.BlockSpec((keys, packed.shape[1]), lambda i: (i + first, 0))]
        + [pl.BlockSpec((d.shape[0], keys, count), lambda i: (0, i + first, 0)) for d in d_halves]
        + waits(after),
        out_specs=full((uppers, columns)),
        out_shape=jax.ShapeDtypeStruct((uppers, columns), f32),
        scratch_shapes=[pltpu.VMEM((uppers * GROUP, columns), f32)],
        compiler_params=params(),
        cost_estimate=cost(1e10, 2 * HEADS * count * count),
    )(packed, *d_halves, *after)


def unfold_table(folded):
    uppers = folded.shape[0]
    return folded.reshape(uppers, 2, HEADS, GROUP).sum(axis=3).reshape(2 * uppers, HEADS)


PLACE = ("z", "x", "c", "y")


def swap(values, axis, size, bit):
    return lax.ppermute(values, axis, [(i, i ^ bit) for i in range(size)])


def combine_kernel(sources, place_ref, *refs):
    count = sum(len(source) for source in sources)
    kept, came, outs = refs[:count], refs[count : 2 * count], refs[-len(sources) :]
    at = 0
    for source, out_ref in zip(sources, outs):
        for slot in range(len(source)):
            total = kept[at][...].astype(f32) + came[at][...].astype(f32)
            out_ref[:, slot] = total.astype(bf16).reshape(out_ref.shape[:1] + out_ref.shape[2:])
            at += 1


def combine(place, steps, outs, after=(), worth=1e6):
    kept, came, in_specs = [], [], []
    out_specs, out_shapes = [], []
    for out in outs:
        for first, second, block, index in out:
            kept.append(first)
            came.append(second)
            in_specs.append(pl.BlockSpec(block, index))
        rows, width = out[0][2][-2:]
        middle_size = out[0][2][0]
        for extent in out[0][2][1:-2]:
            middle_size *= extent
        shape = (len(out), middle_size, rows, width)
        out_specs.append(pl.BlockSpec((1,) + shape, lambda step, place: (step, 0, 0, 0, 0)))
        out_shapes.append(jax.ShapeDtypeStruct((steps,) + shape, bf16))
    return pl.pallas_call(
        partial(combine_kernel, [[None] * len(out) for out in outs]),
        grid_spec=pltpu.PrefetchScalarGridSpec(
            num_scalar_prefetch=1, grid=(steps,), in_specs=in_specs * 2 + waits(after), out_specs=out_specs
        ),
        out_shape=out_shapes,
        compiler_params=params(),
        cost_estimate=cost(worth, worth),
    )(place, *kept, *came, *after)


class PackedSum:
    def __init__(self, place, keep, away, sizes):
        self.place, self.sizes = place, sizes
        shape = (sizes["z"], sizes["x"], sizes["y"]) + keep.shape[2:]
        self.cut, self.width = keep.shape[2] // 2, keep.shape[3]
        self.keep, self.came = keep.reshape(shape), swap(away, "c", 2, 1).reshape(shape)

    def send_first(self, after):
        block_x, block_y = (1, 1, 2, self.cut, self.width), (1, 2, 1, self.cut, self.width)
        pair = (self.keep, self.came)
        keep_a, away_a, keep_b, away_b = combine(
            self.place,
            4,
            [
                [pair + (block_x, lambda s, p: (s, p[1], 0, 0, 0))],
                [pair + (block_x, lambda s, p: (s, 1 - p[1], 0, 0, 0))],
                [pair + (block_y, lambda s, p: (s, 0, p[3], 1, 0))],
                [pair + (block_y, lambda s, p: (s, 0, 1 - p[3], 1, 0))],
            ],
            after,
        )
        self.pairs = ((keep_a, swap(away_a, "x", 2, 1)), (keep_b, swap(away_b, "y", 2, 1)))
        return [away_a, away_b]

    def send_second(self, after, worth=1e6):
        block = (1, 1, 1, self.cut, self.width)
        pair_a, pair_b = self.pairs
        keep_a, away_a, keep_b, away_b = combine(
            self.place,
            4,
            [
                [pair_a + (block, lambda s, p: (s, 0, p[3], 0, 0))],
                [pair_a + (block, lambda s, p: (s, 0, 1 - p[3], 0, 0))],
                [pair_b + (block, lambda s, p: (s, 0, p[1], 0, 0))],
                [pair_b + (block, lambda s, p: (s, 0, 1 - p[1], 0, 0))],
            ],
            after,
            worth,
        )
        self.pairs = ((keep_a, swap(away_a, "y", 2, 1)), (keep_b, swap(away_b, "x", 2, 1)))
        return [away_a, away_b]

    def send_third(self, after):
        block = (1, 1, 1, self.cut, self.width)
        mine = lambda s, p: (2 * s + p[0] % 2, 0, 0, 0, 0)
        other = lambda s, p: (2 * s + 1 - p[0] % 2, 0, 0, 0, 0)
        keep, away = combine(
            self.place,
            2,
            [[pair + (block, mine) for pair in self.pairs], [pair + (block, other) for pair in self.pairs]],
            after,
        )
        self.pairs = ((keep, swap(away, "z", 4, 1)),)
        return [away]

    def send_fourth(self, after):
        block = (1, 2, 1, self.cut, self.width)
        pair = self.pairs[0]
        keep, away = combine(
            self.place,
            1,
            [
                [pair + (block, lambda s, p: (p[0] // 2, 0, 0, 0, 0))],
                [pair + (block, lambda s, p: (1 - p[0] // 2, 0, 0, 0, 0))],
            ],
            after,
        )
        self.pairs = ((keep, swap(away, "z", 4, 2)),)
        return [away]

    def result(self):
        keep, came = self.pairs[0]
        return (keep.astype(f32) + came.astype(f32)).reshape(2 * self.cut, self.width)


class Sum:
    def __init__(self, blocks, sizes):
        self.sizes = sizes
        devices = sizes["z"] * sizes["x"] * sizes["c"] * sizes["y"]
        self.terms = [blocks.reshape(tuple(sizes[a] for a in PLACE) + (-1, blocks.shape[-1]))]
        self.came = None
        self.next_bit = {a: 1 for a in PLACE}

    def part(self, dim, which):
        total = None
        for term in self.terms:
            shape = term.shape
            view = term.reshape(shape[:dim] + (shape[dim] // 2, 2) + shape[dim + 1 :])
            piece = lax.dynamic_index_in_dim(view, which, axis=dim + 1, keepdims=False)
            total = piece if total is None else (total.astype(f32) + piece.astype(f32))
        return total.astype(bf16)

    def send(self, axis):
        self.land()
        dim, bit, size = PLACE.index(axis), self.next_bit[axis], self.sizes[axis]
        self.next_bit[axis] = 2 * bit
        mine = lax.axis_index(axis) // bit % 2
        away = self.part(dim, 1 - mine)
        self.came = swap(away, axis, size, bit)
        self.kept = self.part(dim, mine)
        return away

    def land(self):
        if self.came is not None:
            self.terms = [self.kept, self.came]
            self.came = None

    def open_steps(self, axis):
        return self.next_bit[axis] < self.sizes[axis]

    def result(self):
        self.land()
        total = self.terms[0].astype(f32) + self.terms[1].astype(f32)
        return total.reshape(total.shape[4:])


def sum_step(values, axis, sizes):
    bit = 1
    while bit < sizes[axis]:
        values = values + swap(values, axis, sizes[axis], bit)
        bit *= 2
    return values


def column_parts(matrix, width):
    return [matrix[:, at : at + width] for at in range(0, matrix.shape[1], width)]


def blocks_of(parts, devices):
    return jnp.concatenate([part.reshape(devices, -1, part.shape[1]) for part in parts], axis=1)


def take(blocks, at, rows):
    return blocks[:, at : at + rows].reshape(-1, blocks.shape[2])


def on_device(
    sizes,
    tokens,
    coords,
    rel_pos,
    rel_box,
    entity_pairs,
    entity_grad,
    w_qkv,
    w_attn_out,
    dcpe_table,
    biases,
    norm_gains,
    w_ff_in,
    w_ff_out,
    ff_bias,
    rel_table,
):
    devices = sizes["z"] * sizes["x"] * sizes["c"] * sizes["y"]
    live, width = tokens.shape[1], tokens.shape[2]
    hidden = ff_bias.shape[0] * devices
    count = -(-live // 64) * 64
    extra = count - live
    shard, ff_shard = biases.shape[1], ff_bias.shape[0]
    d_rows, t_rows, h_rows = w_qkv.shape[0], dcpe_table.shape[0], w_ff_out.shape[0]
    ff_parts = hidden // width

    small_own = jnp.concatenate([biases, norm_gains], axis=0)
    hidden_own = jnp.pad(ff_bias.reshape(1, -1), ((0, 7), (0, 0)))
    small_own = jnp.pad(
        jnp.concatenate([jnp.pad(small_own, ((0, 0), (0, 128 - shard))), hidden_own], axis=1),
        ((0, 0), (0, width - 128 - ff_shard)),
    )
    own = jnp.concatenate(
        column_parts(w_qkv, width) + [w_attn_out] + column_parts(w_ff_in, width) + [w_ff_out, dcpe_table, small_own],
        axis=0,
    )
    whole = lax.all_gather(own, PLACE, axis=0)

    packed = rel_pos[0] + rel_box[0, 0] * 32 + rel_box[0, 1] * 2048
    packed = jnp.pad(packed.T, ((0, extra), (0, -(-count // 128) * 128 - live)))
    bias = score_bias(packed, rel_table, live)
    places = jnp.pad(coords[0], ((0, 0), (0, extra)), constant_values=OUTSIDE)
    slots = entity_pairs.reshape(1, -1)
    slot_grads = entity_grad.reshape(slots.shape[1], width)
    padded = jnp.pad(tokens[0], ((0, extra), (0, 0)))

    w_parts = [take(whole, i * d_rows, d_rows) for i in range(4)]
    in_parts = jnp.stack([take(whole, i * d_rows, d_rows) for i in range(4, 4 + ff_parts)])
    at = (4 + ff_parts) * d_rows
    full_back = take(whole, at, h_rows).reshape(ff_parts, width, width)
    full_table = take(whole, at + h_rows, t_rows)
    small_all = whole[:, at + h_rows + t_rows :]
    small = small_all[:, :, :shard].transpose(1, 0, 2).reshape(8, width).astype(f32)
    hidden_bias = small_all[:, 0, 128 : 128 + ff_shard].reshape(ff_parts, width).astype(f32)

    begin, begin_rows, united = embed(padded, places.T, full_table, w_parts[:3], small)
    attention, context = attend(united, bias)
    place = jnp.stack([lax.axis_index(axis) for axis in PLACE]).astype(jnp.int32)
    fast = sizes == {"z": 4, "x": 2, "c": 2, "y": 2} and d_rows % 8 == 0
    layer_out, g_one, g_two, g_out, d_pre, d_context, sums, hidden_sum = middle(
        place, fast, devices, live, begin, context, w_parts[3], in_parts, full_back, small, hidden_bias, slots, slot_grads
    )

    pairs = HEADS // 2
    back = partial(attend_back, united, attention, d_context)
    finish = partial(embed_back, place, fast, devices)
    rest = (w_parts[:3], g_out, d_pre, begin_rows, places, full_table.shape[0])
    steps = packed.shape[0] // 32
    if fast:
        came = swap(g_two, "c", 2, 1)
        half_one = back(0, pairs // 2)
        ff = (g_one.astype(f32) + came.astype(f32)).astype(bf16)
        ff = ff.reshape((sizes["z"], sizes["x"], sizes["y"]) + ff.shape[2:]).transpose(1, 2, 0, 3, 4)
        ff = ff.reshape((-1,) + ff.shape[2:])
        half_two = back(pairs // 2, pairs, [ff])
        ff = lax.psum_scatter(ff, ("x", "y"), scatter_dimension=0, tiled=False)
        ff_own = lax.psum_scatter(ff, "z", scatter_dimension=0, tiled=False).astype(f32)
        input_grad, g_one, g_two, more_sums = finish((half_one[:3], half_two[:3]), *rest)
        attn = PackedSum(place, g_one, g_two, sizes)
        table = partial(table_grad, packed, (half_one[3], half_two[3]))
        sent = attn.send_first([more_sums])
        early = table(0, 11, sent)
        sent = attn.send_second([early])
        latest = table(11, steps, sent)
        folded = early + latest
        sent = attn.send_third([latest])
        input_grad, _ = lax.optimization_barrier((input_grad, sent[0]))
        more_sums, sums, _ = lax.optimization_barrier((more_sums, sums, latest))
        sent = attn.send_fourth(sent)
        attn_own = attn.result()
        g_in = jnp.concatenate([ff_own[i * d_rows : (i + 1) * d_rows] for i in range(ff_parts)], axis=1)
        g_back = ff_own[ff_parts * d_rows :]
        g_qkv = jnp.concatenate([attn_own[i * d_rows : (i + 1) * d_rows] for i in range(3)], axis=1)
        g_out = attn_own[3 * d_rows : 4 * d_rows]
        g_table = attn_own[4 * d_rows :]
    else:
        half = back(0, pairs)
        input_grad, g_qkv, g_table, more_sums = finish((half[:3],), *rest)
        folded = table_grad(packed, half[3:], 0, steps)
        g_in, g_back = jnp.concatenate(list(g_one), axis=1), g_two.reshape(hidden, width)
        totals = [Sum(grad, sizes) for grad in (g_in, g_back, g_qkv, g_out, g_table)]
        for axis in PLACE:
            while totals[0].open_steps(axis):
                for total in totals:
                    total.send(axis)
        g_in, g_back, g_qkv, g_out, g_table = (total.result() for total in totals)

    table_sum = jnp.pad(unfold_table(folded).reshape(-1), (0, -rel_table.size % width)).reshape(-1, width)
    small_sum = jnp.concatenate([more_sums[:2], sums[:6], hidden_sum, table_sum], axis=0)
    small_sum = sum_step(sum_step(small_sum, "c", sizes), "x", sizes)
    if fast:
        small_sum, _ = lax.optimization_barrier((small_sum, sent[0]))
    small_sum = sum_step(sum_step(small_sum, "y", sizes), "z", sizes)
    index = lax.axis_index(PLACE)
    vectors = lax.dynamic_slice_in_dim(small_sum[:8], index * shard, shard, axis=1)
    ff_sum = small_sum[8 : 8 + ff_parts].reshape(-1)
    table_sum = small_sum[8 + ff_parts :].reshape(-1)[: rel_table.size].reshape(rel_table.shape)
    return (
        layer_out[None],
        input_grad[None, :live],
        g_qkv,
        g_out,
        g_table,
        vectors[:6],
        vectors[6:],
        g_in,
        g_back,
        lax.dynamic_slice_in_dim(ff_sum, index * ff_shard, ff_shard, axis=0),
        table_sum,
    )


def solution(mesh):
    outer, inner = mesh.shape["dp"], mesh.shape["fsdp"]
    sizes = {"z": outer // 4, "x": 2, "c": 2, "y": inner}
    split = Mesh(mesh.devices.reshape(tuple(sizes[a] for a in PLACE)), PLACE)
    rows = P(PLACE, None)
    three = P(PLACE, None, None)
    four = P(PLACE, None, None, None)
    columns = P(None, PLACE)
    return jax.shard_map(
        partial(on_device, sizes),
        mesh=split,
        in_specs=(three, three, three, four, three, four, rows, rows, rows, columns, columns, rows, rows, P(PLACE), P()),
        out_specs=(three, three, rows, rows, rows, columns, columns, rows, rows, P(PLACE), P()),
        check_vma=False,
    )
```

```python
from functools import partial

import jax
import jax.numpy as jnp
from jax import lax
from jax.experimental import pallas as pl
from jax.experimental.pallas import tpu as pltpu
from jax.sharding import Mesh
from jax.sharding import PartitionSpec as P

HEADS = 12
HEAD_DIM = 64
B1 = 32
B2 = 64
PAIR = 2 * HEAD_DIM
EPSILON = 1e-05
VMEM_LIMIT = 58 * 2**20
NEVER = -1e30
OUTSIDE = -4096

bf16 = jnp.bfloat16
f32 = jnp.float32


def dot(a, b):
    return jnp.dot(a, b, preferred_element_type=f32)


def dot_nt(a, b):
    return lax.dot_general(a, b, (((1,), (1,)), ((), ())), preferred_element_type=f32)


def dot_tn(a, b):
    return lax.dot_general(a, b, (((0,), (0,)), ((), ())), preferred_element_type=f32)


def params():
    return pltpu.CompilerParams(vmem_limit_bytes=VMEM_LIMIT)


def cost(flops, moved):
    return pl.CostEstimate(flops=int(flops / 1000), bytes_accessed=int(moved / 1000), transcendentals=0)


def waits(arrays):
    return [pl.BlockSpec(memory_space=pl.ANY)] * len(arrays)


def full(shape):
    return pl.BlockSpec(shape, lambda *_: (0,) * len(shape))


def buckets_kernel(pos_ref, box_ref, out_ref, rows_ref):
    live = pos_ref.shape[0]
    whole = live // 8 * 8
    rows_ref[...] = jnp.zeros_like(rows_ref)

    def packed(at):
        return pos_ref[at, 0, :] + box_ref[at, 0, :] * 32 + box_ref[at, 1, :] * 2048

    def eight_rows(step, carry):
        at = pl.ds(pl.multiple_of(step * 8, 8), 8)
        rows_ref[at, :live] = packed(at)
        return carry

    lax.fori_loop(0, whole // 8, eight_rows, 0)
    if whole < live:
        rows_ref[whole:live, :live] = packed(pl.ds(whole, live - whole))
    out_ref[...] = rows_ref[...].T[: out_ref.shape[0]]


def packed_buckets(rel_pos, rel_box, count):
    wide = -(-count // 128) * 128
    return pl.pallas_call(
        buckets_kernel,
        out_shape=jax.ShapeDtypeStruct((count, wide), jnp.int32),
        scratch_shapes=[pltpu.VMEM((wide, wide), jnp.int32)],
        compiler_params=params(),
        cost_estimate=cost(1e6, 1e6),
    )(rel_pos, rel_box)


def bias_kernel(live, index_ref, table_ref, *refs):
    out_ref = refs[-1]
    heads, rows, width = out_ref.shape
    first_row = pl.program_id(0) * rows
    tables = [jnp.broadcast_to(table_ref[r : r + 1, :], (8, 128)) for r in range(2 * heads)]

    def eight_rows(step, carry):
        at = pl.multiple_of(step * 8, 8)
        key_ids = first_row + at + lax.broadcasted_iota(jnp.int32, (8, 128), 0)
        dead = jnp.where(key_ids < live, 0.0, NEVER)
        for left in range(0, width, 128):
            packed = index_ref[pl.ds(at, 8), left : left + 128]
            flat = packed & (B1 - 1)
            across = (lax.shift_right_logical(packed, 5) & (B2 - 1)) + B1
            downward = lax.shift_right_logical(packed, 11)
            for head in range(heads):
                low, high = tables[2 * head], tables[2 * head + 1]
                looked = (
                    jnp.take_along_axis(low, flat, axis=1, mode="promise_in_bounds")
                    + jnp.take_along_axis(low, across, axis=1, mode="promise_in_bounds")
                    + jnp.take_along_axis(high, downward, axis=1, mode="promise_in_bounds")
                    + dead
                )
                right = min(left + 128, width)
                out_ref[head, pl.ds(at, 8), left:right] = looked[:, : right - left]
        return carry

    lax.fori_loop(0, rows // 8, eight_rows, 0)


def score_bias(packed, lookup, live, after=()):
    keys = width = packed.shape[0]
    heads = lookup.shape[0] // 2
    rows = 64
    return pl.pallas_call(
        partial(bias_kernel, live),
        grid=(keys // rows,),
        in_specs=[pl.BlockSpec((rows, packed.shape[1]), lambda i: (i, 0)), full(lookup.shape)] + waits(after),
        out_specs=pl.BlockSpec((heads, rows, width), lambda i: (0, i, 0)),
        out_shape=jax.ShapeDtypeStruct((heads, keys, width), f32),
        compiler_params=params(),
        cost_estimate=cost(3e10, 4 * heads * keys * width),
    )(packed, lookup, *after)


def lookup_rows(rel_table):
    near = jnp.pad(rel_table[: B1 + B2].T, ((0, 0), (0, 128 - B1 - B2)))
    far = jnp.pad(rel_table[B1 + B2 :].T, ((0, 0), (0, 128 - B2)))
    return jnp.stack([near, far], axis=1).reshape(2 * HEADS, 128).astype(f32)


def project(tokens, places_ref, table_half, weights, small_ref, begin_ref, rows_ref, united_ref):
    count, width = tokens.shape
    total = tokens.astype(f32)
    for side in range(2):
        table = table_half(side)
        columns = lax.broadcasted_iota(jnp.int32, (count, table.shape[0]), 1)
        hot = jnp.where(places_ref[:, side : side + 1] == columns, 1.0, 0.0).astype(bf16)
        total += dot(hot, table)
    begin_ref[...] = total
    rows = total.astype(bf16)
    rows_ref[...] = rows
    query, key, value = weights()
    united_ref[:, :width] = ((dot(rows, query) + small_ref[0:1, :]) * 0.125).astype(bf16)
    united_ref[:, width : 2 * width] = dot(rows, key).astype(bf16)
    united_ref[:, 2 * width :] = (dot(rows, value) + small_ref[1:2, :]).astype(bf16)


def embed_kernel(token_ref, places_ref, table_ref, query_ref, key_ref, value_ref, small_ref, *outs):
    half = table_ref.shape[0] // 2
    project(
        token_ref[...],
        places_ref,
        lambda side: table_ref[side * half : (side + 1) * half, :],
        lambda: (query_ref[...], key_ref[...], value_ref[...]),
        small_ref,
        *outs,
    )


def embed_packed_kernel(token_ref, places_ref, small_ref, whole_hbm, *refs):
    begin_ref, rows_ref, united_ref, *weight_refs, near_ref, far_ref, table_ref, sems = refs[-11:]
    devices, pair, width = near_ref.shape
    table_at = 2 * pair
    loads = [
        pltpu.make_async_copy(whole_hbm.at[:, pl.ds(table_at, table_ref.shape[1])], table_ref, sems.at[0]),
        pltpu.make_async_copy(whole_hbm.at[:, pl.ds(0, pair)], near_ref, sems.at[1]),
        pltpu.make_async_copy(whole_hbm.at[:, pl.ds(pair, pair)], far_ref, sems.at[2]),
    ]
    for load in loads:
        load.start()
    loads[0].wait()

    def table_half(side):
        rows = table_ref[side * devices // 2 : (side + 1) * devices // 2]
        return rows.reshape(devices // 2 * rows.shape[1], width)

    def weights():
        for index, ref in enumerate((near_ref, far_ref)):
            loads[1 + index].wait()
            both = ref[...].astype(f32)
            for which in range(2):
                rows = both[:, which * pair // 2 : (which + 1) * pair // 2]
                weight_refs[2 * index + which][...] = rows.reshape(width, width).astype(bf16)
        return [ref[...] for ref in weight_refs[:3]]

    project(token_ref[...], places_ref, table_half, weights, small_ref, begin_ref, rows_ref, united_ref)


def embed(tokens, places, small, weights, after=()):
    count, width = tokens.shape
    outs = (
        jax.ShapeDtypeStruct((count, width), f32),
        jax.ShapeDtypeStruct((count, width), bf16),
        jax.ShapeDtypeStruct((count, 3 * width), bf16),
    )
    estimate = cost(2 * count * width * 5 * width, 12e6)
    vmem = pl.BlockSpec(memory_space=pltpu.VMEM)
    if len(weights) > 1:
        return pl.pallas_call(embed_kernel, out_shape=outs, compiler_params=params(), cost_estimate=estimate)(
            tokens, places, *weights, small
        )
    devices = weights[0].shape[0]
    d_rows = width // devices
    return pl.pallas_call(
        embed_packed_kernel,
        in_specs=[vmem] * 3 + [pl.BlockSpec(memory_space=pl.ANY)] + waits(after),
        out_shape=outs + (jax.ShapeDtypeStruct((width, width), bf16),) * 4,
        scratch_shapes=[
            pltpu.VMEM((devices, 2 * d_rows, width), bf16),
            pltpu.VMEM((devices, 2 * d_rows, width), bf16),
            pltpu.VMEM((devices, weights[0].shape[1] - 4 * d_rows - 16, width), bf16),
            pltpu.SemaphoreType.DMA((3,)),
        ],
        compiler_params=params(),
        cost_estimate=estimate,
    )(tokens, places, small, weights[0], *after)


def head_mask(head):
    return lax.broadcasted_iota(jnp.int32, (1, PAIR), 1) // HEAD_DIM == head


def attend_kernel(query_ref, key_ref, value_ref, bias_ref, *refs):
    attention_ref, context_ref = refs[-2:]
    query, key = query_ref[...], key_ref[...]
    value_t = value_ref[...].astype(f32).T.astype(bf16)
    parts = []
    for head in range(2):
        scores = dot_nt(jnp.where(head_mask(head), key, 0), query) + bias_ref[head]
        raised = jnp.exp(scores - jnp.max(scores, axis=0, keepdims=True))
        attention = (raised * (1.0 / jnp.sum(raised, axis=0, keepdims=True))).astype(bf16)
        attention_ref[head] = attention
        parts.append(dot(value_t[head * HEAD_DIM : (head + 1) * HEAD_DIM], attention))
    context_ref[...] = jnp.concatenate(parts, axis=0).T.astype(bf16)


def attend(united, bias, first, last, after=()):
    count = united.shape[0]
    pairs = HEADS // 2
    column = lambda shift: pl.BlockSpec((count, PAIR), lambda p: (0, p + shift))
    square = pl.BlockSpec((2, count, count), lambda p: (p, 0, 0))
    return pl.pallas_call(
        attend_kernel,
        grid=(last - first,),
        in_specs=[column(first), column(first + pairs), column(first + 2 * pairs), square] + waits(after),
        out_specs=(square, column(0)),
        out_shape=(
            jax.ShapeDtypeStruct((2 * (last - first), count, count), bf16),
            jax.ShapeDtypeStruct((count, (last - first) * PAIR), bf16),
        ),
        compiler_params=params(),
        cost_estimate=cost(4 * HEADS * count * count * HEAD_DIM, 6 * HEADS * count * count),
    )(united, united, united, bias, *after)


def attend_back_kernel(query_ref, key_ref, value_ref, attention_ref, d_context_ref, *refs):
    d_query_ref, d_key_ref, d_value_ref, d_scores_ref = refs[-4:]
    query, value, d_context = query_ref[...], value_ref[...], d_context_ref[...]
    key_t = key_ref[...].astype(f32).T.astype(bf16)
    parts = []
    d_key = jnp.zeros(query.shape, f32)
    d_value = jnp.zeros(query.shape, f32)
    for head in range(2):
        mask = head_mask(head)
        d_attention = dot_nt(jnp.where(mask, value, 0), d_context)
        attention_low = attention_ref[head]
        attention = attention_low.astype(f32)
        centre = jnp.sum(attention * d_attention, axis=0, keepdims=True)
        d_scores = (attention * (d_attention - centre)).astype(bf16)
        d_scores_ref[head] = d_scores
        d_key += dot(d_scores, jnp.where(mask, query, 0))
        d_value += dot(attention_low, jnp.where(mask, d_context, 0))
        parts.append(dot(key_t[head * HEAD_DIM : (head + 1) * HEAD_DIM], d_scores))
    d_query_ref[...] = jnp.concatenate(parts, axis=0).T.astype(bf16) * bf16(0.125)
    d_key_ref[...] = d_key.astype(bf16)
    d_value_ref[...] = d_value.astype(bf16)


def attend_back(united, attention, d_context, first, last, after=()):
    count = united.shape[0]
    pairs = HEADS // 2
    column = lambda shift: pl.BlockSpec((count, PAIR), lambda p: (0, p + shift))
    square = lambda shift: pl.BlockSpec((2, count, count), lambda p: (p + shift, 0, 0))
    joined = jax.ShapeDtypeStruct((count, (last - first) * PAIR), bf16)
    return pl.pallas_call(
        attend_back_kernel,
        grid=(last - first,),
        in_specs=[column(first), column(first + pairs), column(first + 2 * pairs), square(0), column(first)]
        + waits(after),
        out_specs=(column(0), column(0), column(0), square(0)),
        out_shape=(joined, joined, joined, jax.ShapeDtypeStruct((2 * (last - first), count, count), bf16)),
        compiler_params=params(),
        cost_estimate=cost(8 * HEADS * count * count * HEAD_DIM, 4 * HEADS * count * count),
    )(united, united, united, attention, d_context, *after)


def unit_rows(values):
    centred = values - jnp.mean(values, axis=1, keepdims=True)
    scale = lax.rsqrt(jnp.mean(centred * centred, axis=1, keepdims=True) + EPSILON)
    return centred * scale, scale


def unit_rows_back(units, scale, d_units):
    spread = jnp.mean(d_units * units, axis=1, keepdims=True)
    return scale * (d_units - jnp.mean(d_units, axis=1, keepdims=True) - units * spread)


def column_sum(values):
    return jnp.sum(values.astype(f32), axis=0, keepdims=True)


def split_cores(values, rows):
    inner = values.shape[0] // rows
    return values.reshape((inner // 4, 2, 2, rows, values.shape[1]))


def middle_kernel(packed, place_ref, begin_ref, left_ref, right_ref, w_out_ref, one_hbm, two_hbm, *refs):
    small_ref, hidden_bias_ref, slot_ref, slot_grad_ref, layer_ref, g_out_ref, *refs = refs
    d_pre_ref, d_context_ref, sums_ref, hidden_sum_ref, g_one_ref, *refs = refs
    if not packed:
        g_two_ref, *refs = refs
    w_in_ref, w_back_ref, act_ref, slope_ref, d_inner_ref, total_ref, load_sems, *refs = refs
    count, width = begin_ref.shape
    parts = w_in_ref.shape[0]
    context = jnp.concatenate([left_ref[...], right_ref[...]], axis=1)
    w_in = lambda part: w_in_ref[part].reshape(width, width)
    if packed:
        buffer_ref, store_sems = refs
        core = place_ref[2]
        devices = buffer_ref.shape[1] * 4
        d_rows, h_rows = width // devices, width * parts // devices
        blocks_each = width // h_rows // 4
        w_back = lambda part: w_back_ref[pl.ds(part * blocks_each, blocks_each)].reshape(width, width)
        loads = []
        for side, source in enumerate((one_hbm, two_hbm)):
            in_rows, back_rows = pl.ds(0, parts * d_rows), pl.ds(parts * d_rows, h_rows)
            target = buffer_ref.at[side, :, :, in_rows]
            loads.append(pltpu.make_async_copy(source.at[:, :, in_rows], target, load_sems.at[side]))
            target = w_back_ref.at[:, side ^ core]
            loads.append(pltpu.make_async_copy(source.at[:, :, back_rows], target, load_sems.at[2 + side]))
    else:
        w_back = lambda part: w_back_ref[part]
        loads = [
            pltpu.make_async_copy(one_hbm, w_in_ref, load_sems.at[0]),
            pltpu.make_async_copy(two_hbm, w_back_ref, load_sems.at[1]),
        ]
    for load in loads:
        load.start()

    row = lambda i: small_ref[i : i + 1, :]
    attended = dot(context, w_out_ref[...]) + row(2)
    units, scale = unit_rows(begin_ref[...] + attended)
    mid = units * row(6) + row(3)
    mid_rows = mid.astype(bf16)
    total_ref[...] = mid + row(4)
    for load in loads:
        load.wait()

    def unpack(block, carry):
        for side in range(2):
            for pair in range(parts // 2):
                at = pair * 2 * d_rows
                both = buffer_ref[side, block, :, at : at + 2 * d_rows].astype(f32)
                for which in range(2):
                    rows = both[:, which * d_rows : (which + 1) * d_rows].reshape(2 * d_rows, width)
                    w_in_ref[2 * pair + which, block, side ^ core] = rows.astype(bf16)
        return carry

    if packed:
        lax.fori_loop(0, devices // 4, unpack, 0)

    def forward_part(part, carry):
        inner = dot(mid_rows, w_in(part)) + hidden_bias_ref[pl.ds(part, 1), :]
        share = 0.5 * lax.erf(inner * (2.0**-0.5)) + 0.5
        bell = jnp.exp(inner * inner * -0.5) * (0.5 * 2.0**0.5 / jnp.pi**0.5)
        act = (inner * share).astype(bf16)
        act_ref[part] = act
        slope_ref[part] = (share + inner * bell).astype(bf16)
        total_ref[...] += dot(act, w_back(part))
        return carry

    lax.fori_loop(0, parts, forward_part, 0)
    out_units, out_scale = unit_rows(total_ref[...])
    layer_ref[...] = (out_units * row(7) + row(5)).astype(bf16)[: layer_ref.shape[0]]

    token_ids = lax.broadcasted_iota(jnp.int32, (count, slot_ref.shape[1]), 0)
    slot_hot = jnp.where(slot_ref[...] == token_ids, 1.0, 0.0).astype(bf16)
    out_cot = dot(slot_hot, slot_grad_ref[...])
    sums_ref[3:4, :] = column_sum(out_cot)
    sums_ref[5:6, :] = column_sum(out_cot * out_units)
    d_sum = unit_rows_back(out_units, out_scale, out_cot * row(7))
    sums_ref[2:3, :] = column_sum(d_sum.astype(bf16))
    d_outer = d_sum.astype(bf16)
    total_ref[...] = d_sum
    rows_t = mid.T.astype(bf16)

    def stores(at, rows, first, blocks, sem):
        copies = []
        for side in range(2):
            for step in range(blocks // 2):
                z = first // 2 + step
                source = buffer_ref.at[side, pl.ds(2 * z, 2), :, pl.ds(at, rows)]
                target = g_one_ref.at[side, :, :, z, pl.ds(at, rows)]
                copies.append(pltpu.make_async_copy(source, target, store_sems.at[side, step, sem]))
        return copies

    def store_back(part):
        return stores(parts * d_rows, h_rows, part * blocks_each, blocks_each, part)

    def store_in(pair):
        return stores(pl.multiple_of(pair * 2 * d_rows, 16), 2 * d_rows, 0, devices // 4, parts + pair)

    def backward_part(part, carry):
        d_act = dot_nt(d_outer, w_back(part))
        d_inner = (d_act * slope_ref[part].astype(f32)).astype(bf16)
        hidden_sum_ref[pl.ds(part, 1), :] = column_sum(d_inner)
        total_ref[...] += dot_nt(d_inner, w_in(part))
        d_inner_ref[part] = d_inner
        g_back = dot_tn(act_ref[part], d_outer).astype(bf16)
        if packed:
            blocks = split_cores(g_back, h_rows)
            at = pl.ds(part * blocks_each, blocks_each)
            for side in range(2):
                buffer_ref[side, at, :, parts * d_rows :] = blocks[:, side]
            for copy in store_back(part):
                copy.start()
        else:
            g_two_ref[part] = g_back
            g_one_ref[part] = dot(rows_t, d_inner).astype(bf16)
        return carry

    lax.fori_loop(0, parts, backward_part, 0)

    def pack_pair(pair, carry):
        at = pl.ds(pl.multiple_of(pair * 2 * d_rows, 16), 2 * d_rows)
        for left in range(0, width, 256):
            columns = slice(left, left + 256)
            pieces = [
                dot(rows_t, d_inner_ref[2 * pair + which, :, columns]).reshape(devices, d_rows, 256)
                for which in range(2)
            ]
            joined = jnp.concatenate(pieces, axis=1).astype(bf16).reshape(devices // 4, 2, 2, 2 * d_rows, 256)
            for side in range(2):
                buffer_ref[side, :, :, at, columns] = joined[:, side]
        for copy in store_in(pair):
            copy.start()
        return carry

    if packed:
        lax.fori_loop(0, parts // 2, pack_pair, 0)

    d_mid = total_ref[...]
    d_pre = unit_rows_back(units, scale, d_mid * row(6))
    d_pre_ref[...] = d_pre
    d_att = d_pre.astype(bf16)
    g_out_ref[...] = dot_tn(context, d_att).astype(bf16)
    d_context_ref[...] = dot_nt(d_att, w_out_ref[...]).astype(bf16)
    sums_ref[0:1, :] = column_sum(d_att)
    sums_ref[1:2, :] = column_sum(d_mid)
    sums_ref[4:5, :] = column_sum(d_mid * units)
    sums_ref[6:8, :] = jnp.zeros((2, width), f32)
    if packed:
        for part in range(parts):
            for copy in store_back(part):
                copy.wait()
        for pair in range(parts // 2):
            for copy in store_in(pair):
                copy.wait()


def middle(place, packed, devices, live, begin, context, w_attn_out, w_one, w_two, small, hidden_bias, slots, slot_grads):
    count, width = begin.shape
    parts = hidden_bias.shape[0]
    hidden = parts * width
    vmem = pl.BlockSpec(memory_space=pltpu.VMEM)
    away = pl.BlockSpec(memory_space=pl.ANY)
    if packed:
        weights = [(parts, devices // 4, 2, 2 * width // devices, width), (devices // 4, 2, 2, hidden // devices, width)]
    else:
        weights = [(parts, width, width)] * 2
    scratch = [pltpu.VMEM(shape, bf16) for shape in weights + [(parts, count, width)] * 3]
    scratch += [pltpu.VMEM((count, width), f32), pltpu.SemaphoreType.DMA((4,))]
    if packed:
        rows = 2 * hidden // devices
        grads = (jax.ShapeDtypeStruct((2, 2, 2, devices // 8, rows, width), bf16),)
        scratch += [
            pltpu.VMEM((2, devices // 4, 2, rows, width), bf16),
            pltpu.SemaphoreType.DMA((2, devices // 8, parts + parts // 2)),
        ]
    else:
        grads = (jax.ShapeDtypeStruct((parts, width, width), bf16),) * 2
    grad_space = away if packed else vmem
    return pl.pallas_call(
        partial(middle_kernel, packed),
        in_specs=[pl.BlockSpec(memory_space=pltpu.SMEM)] + [vmem] * 4 + [away] * 2 + [vmem] * 4,
        out_specs=(vmem,) * 6 + (grad_space,) * len(grads),
        out_shape=(
            jax.ShapeDtypeStruct((live, width), bf16),
            jax.ShapeDtypeStruct((width, width), bf16),
            jax.ShapeDtypeStruct((count, width), f32),
            jax.ShapeDtypeStruct((count, width), bf16),
            jax.ShapeDtypeStruct((8, width), f32),
            jax.ShapeDtypeStruct((parts, width), f32),
        )
        + grads,
        scratch_shapes=scratch,
        compiler_params=params(),
        cost_estimate=cost(12 * count * width * hidden, 30e6),
    )(place, begin, *context, w_attn_out, w_one, w_two, small, hidden_bias, slots, slot_grads)


def store_blocks(buffer_ref, targets, sems, blocks, first, at, first_sem, core):
    spaces, rows = blocks.shape[0], blocks.shape[3]
    for which in range(2):
        buffer_ref[which ^ core, first : first + spaces, :, at : at + rows] = blocks[:, which]
    copies = []
    for side, target in enumerate(targets):
        source = buffer_ref.at[side, pl.ds(first, spaces), :, pl.ds(at, rows)]
        target = target.at[pl.ds(first, spaces), :, pl.ds(at, rows)]
        copies.append(pltpu.make_async_copy(source, target, sems.at[first_sem + side]))
        copies[-1].start()
    return copies


def qkv_back_kernel(halves, packed, place_ref, *refs):
    d_refs, refs = refs[: 3 * halves], refs[3 * halves :]
    g_out_ref, rows_ref = refs[:2]
    g_one_ref, g_two_ref, sums_ref = refs[-5:-2] if packed else refs[-3:]
    count, width = rows_ref.shape
    rows_t = rows_ref[...].astype(f32).T.astype(bf16)
    grads = [
        jnp.concatenate([d_refs[3 * half + part][...] for half in range(halves)], axis=1) for part in range(3)
    ]
    sums_ref[...] = jnp.zeros((8, width), f32)
    sums_ref[0:1, :] = column_sum(grads[0])
    sums_ref[1:2, :] = column_sum(grads[2])
    if not packed:
        for part in range(3):
            g_one_ref[:, part * width : (part + 1) * width] = dot(rows_t, grads[part]).astype(bf16)
        g_two_ref[...] = g_out_ref[...]
        return
    buffer_ref, sems = refs[-2:]
    core = place_ref[2]
    devices = buffer_ref.shape[1] * 4
    d_rows = width // devices
    for left in range(0, width, 256):
        columns = slice(left, left + 256)
        pieces = [dot(rows_t, grad[:, columns]).reshape(devices, d_rows, 256) for grad in grads]
        pieces.append(g_out_ref[:, columns].astype(f32).reshape(devices, d_rows, 256))
        joined = jnp.concatenate(pieces, axis=1).astype(bf16).reshape(devices // 4, 2, 2, 4 * d_rows, 256)
        for which in range(2):
            buffer_ref[which ^ core, :, :, :, columns] = joined[:, which]
    copies = [
        pltpu.make_async_copy(buffer_ref.at[side], target, sems.at[side])
        for side, target in enumerate((g_one_ref, g_two_ref))
    ]
    for copy in copies:
        copy.start()
    for copy in copies:
        copy.wait()


def qkv_back(place, packed, devices, d_halves, g_out, begin_rows, after=()):
    count, width = begin_rows.shape
    vmem = pl.BlockSpec(memory_space=pltpu.VMEM)
    away = pl.BlockSpec(memory_space=pl.ANY)
    d_all = [d for half in d_halves for d in half]
    scratch = []
    if packed:
        half = (devices // 4, 2, 4 * (width // devices), width)
        grads = (jax.ShapeDtypeStruct(half, bf16),) * 2
        scratch = [pltpu.VMEM((2,) + half, bf16), pltpu.SemaphoreType.DMA((2,))]
    else:
        grads = (jax.ShapeDtypeStruct((width, 3 * width), bf16), jax.ShapeDtypeStruct((width, width), bf16))
    grad_space = away if packed else vmem
    return pl.pallas_call(
        partial(qkv_back_kernel, len(d_halves), packed),
        in_specs=[pl.BlockSpec(memory_space=pltpu.SMEM)] + [vmem] * (len(d_all) + 2) + waits(after),
        out_specs=(grad_space, grad_space, vmem),
        out_shape=grads + (jax.ShapeDtypeStruct((8, width), f32),),
        scratch_shapes=scratch,
        compiler_params=params(),
        cost_estimate=cost(6 * count * width * width, 10e6),
    )(place, *d_all, g_out, begin_rows, *after)


def embed_back_kernel(halves, packed, place_ref, *refs):
    d_refs, refs = refs[: 3 * halves], refs[3 * halves :]
    w_hbm, refs = refs[:3], refs[3:]
    d_pre_ref, coords_ref = refs[:2]
    scratch = 4 if packed else 2
    outs = refs[-scratch - (3 if packed else 2) : -scratch]
    input_grad_ref = outs[0]
    w_ref, load_sems = refs[-scratch:][:2]
    count, width = d_pre_ref.shape
    loads = [pltpu.make_async_copy(w_hbm[part], w_ref.at[part], load_sems.at[part]) for part in range(3)]
    for copy in loads:
        copy.start()
    total = d_pre_ref[...]
    for part in range(3):
        loads[part].wait()
        grad = jnp.concatenate([d_refs[3 * half + part][...] for half in range(halves)], axis=1)
        total += dot_nt(grad, w_ref[part])
    input_grad_ref[...] = total
    low = total.astype(bf16)
    if packed:
        buffer_ref, store_sems = refs[-2:]
        devices, t_rows = buffer_ref.shape[1] * 4, buffer_ref.shape[3]
        half = t_rows * devices // 2
    else:
        half = outs[1].shape[0] // 2
    values = lax.broadcasted_iota(jnp.int32, (half, count), 0)
    copies = []
    for side in range(2):
        hot = jnp.where(coords_ref[side : side + 1, :] == values, 1.0, 0.0).astype(bf16)
        g_table = dot(hot, low).astype(bf16)
        if packed:
            blocks = split_cores(g_table, t_rows)
            first = side * blocks.shape[0]
            copies += store_blocks(buffer_ref, outs[1:], store_sems, blocks, first, 0, 2 * side, place_ref[2])
        else:
            outs[1][side * half : (side + 1) * half, :] = g_table
    for copy in copies:
        copy.wait()


def embed_back(place, packed, devices, d_halves, w_qkv, d_pre, coords, table_rows, after=()):
    count, width = d_pre.shape
    vmem = pl.BlockSpec(memory_space=pltpu.VMEM)
    away = pl.BlockSpec(memory_space=pl.ANY)
    d_all = [d for half in d_halves for d in half]
    scratch = [pltpu.VMEM((3, width, width), bf16), pltpu.SemaphoreType.DMA((3,))]
    if packed:
        half = (devices // 4, 2, table_rows // devices, width)
        grads = (jax.ShapeDtypeStruct(half, bf16),) * 2
        scratch += [pltpu.VMEM((2,) + half, bf16), pltpu.SemaphoreType.DMA((4,))]
    else:
        grads = (jax.ShapeDtypeStruct((table_rows, width), bf16),)
    return pl.pallas_call(
        partial(embed_back_kernel, len(d_halves), packed),
        in_specs=[pl.BlockSpec(memory_space=pltpu.SMEM)]
        + [vmem] * len(d_all)
        + [away] * 3
        + [vmem] * 2
        + waits(after),
        out_specs=(vmem,) + ((away,) if packed else (vmem,)) * len(grads),
        out_shape=(jax.ShapeDtypeStruct((count, width), f32),) + grads,
        scratch_shapes=scratch,
        compiler_params=params(),
        cost_estimate=cost(2 * count * width * (table_rows + 3 * width), 15e6),
    )(place, *d_all, *w_qkv, d_pre, coords, *after)


GROUP = 8
TABLE_BLOCKS = 6
TABLES = ((0, B1), (5, B2), (11, B2))


def table_kernel(halves, index_ref, *refs):
    d_refs = refs[:halves]
    out_ref, total_ref = refs[-2:]
    keys, count = d_refs[0].shape[1:]
    columns = 2 * HEADS * GROUP

    @pl.when(pl.program_id(0) == 0)
    def _():
        total_ref[...] = jnp.zeros_like(total_ref)

    d_scores = jnp.concatenate([d_ref[...].astype(f32) for d_ref in d_refs], axis=0)
    packed = index_ref[:, :count]
    base = 0
    for shift, buckets in TABLES:
        bucket = lax.shift_right_logical(packed, shift) & (buckets - 1)
        upper, lowest = lax.shift_right_logical(bucket, 1).astype(f32), bucket & 1
        uppers = buckets // 2
        values = lax.broadcasted_iota(jnp.int32, (uppers, count), 0).astype(f32).astype(bf16)
        left, right = [], []
        for first in range(0, keys, GROUP):
            group = slice(first, first + GROUP)
            hot = [
                jnp.where(jnp.broadcast_to(upper[k : k + 1], values.shape).astype(bf16) == values, bf16(1), bf16(0))
                for k in range(first, first + GROUP)
            ]
            left.append(jnp.concatenate(hot, axis=0))
            split = [
                jnp.where((lowest[group] == bit)[None], d_scores[:, group, :], 0.0).reshape(HEADS * GROUP, count)
                for bit in range(2)
            ]
            right.append(jnp.concatenate(split, axis=0).astype(bf16))
        total_ref[base : base + uppers * GROUP, :] += dot_nt(
            jnp.concatenate(left, axis=1), jnp.concatenate(right, axis=1)
        )
        base += uppers * GROUP

    @pl.when(pl.program_id(0) == pl.num_programs(0) - 1)
    def _():
        base, pieces = 0, []
        for _, buckets in TABLES:
            shape = (GROUP, buckets // 2, columns)
            block = total_ref[base : base + shape[0] * shape[1], :].reshape(shape)
            own = lax.broadcasted_iota(jnp.int32, shape, 2) % GROUP == lax.broadcasted_iota(jnp.int32, shape, 0)
            pieces.append(jnp.sum(jnp.where(own, block, 0.0), axis=0))
            base += shape[0] * shape[1]
        out_ref[...] = jnp.concatenate(pieces, axis=0)


def table_grad(packed, d_halves, first, last, after=()):
    count = packed.shape[0]
    keys = count // TABLE_BLOCKS
    uppers = (B1 + 2 * B2) // 2
    columns = 2 * HEADS * GROUP
    return pl.pallas_call(
        partial(table_kernel, len(d_halves)),
        grid=(last - first,),
        in_specs=[pl.BlockSpec((keys, packed.shape[1]), lambda i: (i + first, 0))]
        + [pl.BlockSpec((d.shape[0], keys, count), lambda i: (0, i + first, 0)) for d in d_halves]
        + waits(after),
        out_specs=full((uppers, columns)),
        out_shape=jax.ShapeDtypeStruct((uppers, columns), f32),
        scratch_shapes=[pltpu.VMEM((uppers * GROUP, columns), f32)],
        compiler_params=params(),
        cost_estimate=cost(1e10, 2 * HEADS * count * count),
    )(packed, *d_halves, *after)


def unfold_table(folded):
    uppers = folded.shape[0]
    return folded.reshape(uppers, 2, HEADS, GROUP).sum(axis=3).reshape(2 * uppers, HEADS)


PLACE = ("z", "x", "c", "y")


def swap(values, axis, size, bit):
    return lax.ppermute(values, axis, [(i, i ^ bit) for i in range(size)])


def pack_kernel(w_qkv_ref, w_out_ref, table_ref, small_ref, w_in_ref, w_back_ref, attn_ref, ff_ref):
    rows, width = w_out_ref.shape
    parts = lambda ref: [ref[:, at : at + width].astype(f32) for at in range(0, ref.shape[1], width)]
    beside = parts(w_qkv_ref) + [w_out_ref[...].astype(f32)]
    attn_ref[: 4 * rows, :] = jnp.concatenate(beside, axis=0).astype(bf16)
    table_end = 4 * rows + table_ref.shape[0]
    attn_ref[4 * rows : table_end, :] = table_ref[...]
    attn_ref[table_end:, :] = small_ref[...]
    in_parts = parts(w_in_ref)
    ff_ref[: len(in_parts) * rows, :] = jnp.concatenate(in_parts, axis=0).astype(bf16)
    ff_ref[len(in_parts) * rows :, :] = w_back_ref[...]


def pack(w_qkv, w_attn_out, dcpe_table, small, w_ff_in, w_ff_out):
    rows, width = w_attn_out.shape
    attn_rows = 4 * rows + dcpe_table.shape[0] + small.shape[0]
    ff_rows = w_ff_in.shape[1] // width * rows + w_ff_out.shape[0]
    return pl.pallas_call(
        pack_kernel,
        out_shape=(
            jax.ShapeDtypeStruct((attn_rows, width), bf16),
            jax.ShapeDtypeStruct((ff_rows, width), bf16),
        ),
        compiler_params=params(),
        cost_estimate=cost(1e6, 1e6),
    )(w_qkv, w_attn_out, dcpe_table, small, w_ff_in, w_ff_out)


def spread_kernel(pieces, cuts, place_ref, *refs):
    outs = refs[-len(cuts) :]
    for piece in range(pieces):

        @pl.when(pl.program_id(0) == piece)
        def _(piece=piece):
            for index, (out_ref, (at, rows)) in enumerate(zip(outs, cuts)):
                source = refs[index * pieces + piece]
                extent = source.shape[:-2]
                out_ref[...] = source[..., at : at + rows, :].reshape(out_ref.shape)


def spread(place, axes, groups, cuts, after=()):
    pieces = len(groups[0])
    operands, in_specs, out_specs, out_shapes = [], [], [], []
    for axis, group, (at, rows) in zip(axes, groups, cuts):
        shape = group[0].shape
        operands += group
        in_specs += [pl.BlockSpec(shape, lambda step, place, zeros=(0,) * len(shape): zeros)] * pieces
        lead = len(shape) - 2
        out_specs.append(
            pl.BlockSpec(
                shape[:-2] + (1, rows, shape[-1]),
                lambda step, place, lead=lead, axis=axis: (0,) * lead + (place[axis] ^ step, 0, 0),
            )
        )
        out_shapes.append(jax.ShapeDtypeStruct(shape[:-2] + (pieces, rows, shape[-1]), bf16))
    return pl.pallas_call(
        partial(spread_kernel, pieces, cuts),
        grid_spec=pltpu.PrefetchScalarGridSpec(
            num_scalar_prefetch=1, grid=(pieces,), in_specs=in_specs + waits(after), out_specs=out_specs
        ),
        out_shape=out_shapes,
        compiler_params=params(),
        cost_estimate=cost(1e6, 1e6),
    )(place, *operands, *after)


def join_kernel(cut, place_ref, head_ref, head_came_ref, tail_ref, tail_came_ref, *refs):
    out_ref = refs[-1]
    mine_x, mine_y = place_ref[1], place_ref[3]
    out_ref[0, :, mine_y, :cut] = head_ref[0]
    out_ref[0, :, 1 - mine_y, :cut] = head_came_ref[0]
    out_ref[0, mine_x, :, cut:] = tail_ref[0]
    out_ref[0, 1 - mine_x, :, cut:] = tail_came_ref[0]


def join(place, head, head_came, tail, tail_came, after=()):
    spaces, _, cut, width = head.shape
    rows = cut + tail.shape[2]
    return pl.pallas_call(
        partial(join_kernel, cut),
        grid_spec=pltpu.PrefetchScalarGridSpec(
            num_scalar_prefetch=1,
            grid=(spaces,),
            in_specs=[pl.BlockSpec((1, 2, cut, width), lambda s, p: (s, 0, 0, 0))] * 2
            + [pl.BlockSpec((1, 2, rows - cut, width), lambda s, p: (s, 0, 0, 0))] * 2
            + waits(after),
            out_specs=pl.BlockSpec((1, 2, 2, rows, width), lambda s, p: (s, 0, 0, 0, 0)),
        ),
        out_shape=jax.ShapeDtypeStruct((spaces, 2, 2, rows, width), bf16),
        compiler_params=params(),
        cost_estimate=cost(1e6, 1e6),
    )(place, head, head_came, tail, tail_came, *after)


def combine_kernel(sources, place_ref, *refs):
    count = sum(len(source) for source in sources)
    kept, came, outs = refs[:count], refs[count : 2 * count], refs[-len(sources) :]
    at = 0
    for source, out_ref in zip(sources, outs):
        first = 0
        for _ in source:
            total = kept[at][...].astype(f32) + came[at][...].astype(f32)
            rows, width = total.shape[-2:]
            out_ref[0, :, first : first + rows, :] = total.astype(bf16).reshape(out_ref.shape[1], rows, width)
            first += rows
            at += 1


def combine(place, steps, outs, after=(), worth=1e6):
    kept, came, in_specs = [], [], []
    out_specs, out_shapes = [], []
    for out in outs:
        for first, second, block, index in out:
            kept.append(first)
            came.append(second)
            in_specs.append(pl.BlockSpec(block, index))
        inner = 1
        for extent in out[0][2][1:-2]:
            inner *= extent
        shape = (inner, sum(entry[2][-2] for entry in out), out[0][2][-1])
        out_specs.append(pl.BlockSpec((1,) + shape, lambda step, place: (step, 0, 0, 0)))
        out_shapes.append(jax.ShapeDtypeStruct((steps,) + shape, bf16))
    return pl.pallas_call(
        partial(combine_kernel, [[None] * len(out) for out in outs]),
        grid_spec=pltpu.PrefetchScalarGridSpec(
            num_scalar_prefetch=1, grid=(steps,), in_specs=in_specs * 2 + waits(after), out_specs=out_specs
        ),
        out_shape=out_shapes,
        compiler_params=params(),
        cost_estimate=cost(worth, worth),
    )(place, *kept, *came, *after)


class PackedSum:
    def __init__(self, place, keep, away, sizes):
        self.place, self.sizes = place, sizes
        shape = (sizes["z"], sizes["x"], sizes["y"]) + keep.shape[2:]
        self.cut, self.width = keep.shape[2] // 2, keep.shape[3]
        self.keep, self.came = keep.reshape(shape), swap(away, "c", 2, 1).reshape(shape)

    def send_first(self, after):
        block_x, block_y = (1, 1, 2, self.cut, self.width), (1, 2, 1, self.cut, self.width)
        pair = (self.keep, self.came)
        keep_a, away_a, keep_b, away_b = combine(
            self.place,
            self.sizes["z"],
            [
                [pair + (block_x, lambda s, p: (s, p[1], 0, 0, 0))],
                [pair + (block_x, lambda s, p: (s, 1 - p[1], 0, 0, 0))],
                [pair + (block_y, lambda s, p: (s, 0, p[3], 1, 0))],
                [pair + (block_y, lambda s, p: (s, 0, 1 - p[3], 1, 0))],
            ],
            after,
        )
        self.pairs = ((keep_a, swap(away_a, "x", 2, 1)), (keep_b, swap(away_b, "y", 2, 1)))
        return [away_a, away_b]

    def send_second(self, after):
        block = (1, 1, self.cut, self.width)
        pair_a, pair_b = self.pairs
        keep_a, away_a, keep_b, away_b = combine(
            self.place,
            self.sizes["z"],
            [
                [pair_a + (block, lambda s, p: (s, p[3], 0, 0))],
                [pair_a + (block, lambda s, p: (s, 1 - p[3], 0, 0))],
                [pair_b + (block, lambda s, p: (s, p[1], 0, 0))],
                [pair_b + (block, lambda s, p: (s, 1 - p[1], 0, 0))],
            ],
            after,
        )
        self.pairs = ((keep_a, swap(away_a, "y", 2, 1)), (keep_b, swap(away_b, "x", 2, 1)))
        return [away_a, away_b]


def send_along_z(place, pairs, after):
    step = lambda pair, other: pair + ((1,) + pair[0].shape[1:], lambda s, p: (p[0] ^ other, 0, 0, 0))
    keep, *away = combine(place, 1, [[step(pair, other) for pair in pairs] for other in range(4)], after)
    return keep, [swap(rows, "z", 4, 1 + other) for other, rows in enumerate(away)], away


def finish_kernel(keep_ref, one_ref, two_ref, three_ref, *refs):
    qkv_ref, out_ref, table_ref = refs[-3:]
    total = keep_ref[0, 0].astype(f32) + one_ref[0, 0].astype(f32)
    total += two_ref[0, 0].astype(f32) + three_ref[0, 0].astype(f32)
    rows, width = out_ref.shape
    for part in range(3):
        qkv_ref[:, part * width : (part + 1) * width] = total[part * rows : (part + 1) * rows]
    out_ref[...] = total[3 * rows : 4 * rows]
    table_ref[...] = total[4 * rows :]


def finish_attn(keep, came, rows, after):
    packed, width = keep.shape[2:]
    return pl.pallas_call(
        finish_kernel,
        in_specs=[pl.BlockSpec(memory_space=pltpu.VMEM)] * 4 + waits(after),
        out_shape=(
            jax.ShapeDtypeStruct((rows, 3 * width), f32),
            jax.ShapeDtypeStruct((rows, width), f32),
            jax.ShapeDtypeStruct((packed - 4 * rows, width), f32),
        ),
        compiler_params=params(),
        cost_estimate=cost(1e6, 1e6),
    )(keep, *came, *after)


def finish_ff_kernel(own_ref, *refs):
    in_ref, back_ref = refs[-2:]
    total = own_ref[...].astype(f32)
    rows, width = in_ref.shape[0], back_ref.shape[1]
    parts = in_ref.shape[1] // width
    for part in range(parts):
        in_ref[:, part * width : (part + 1) * width] = total[part * rows : (part + 1) * rows]
    back_ref[...] = total[parts * rows :]


def finish_ff(own, rows, parts, after):
    packed, width = own.shape
    return pl.pallas_call(
        finish_ff_kernel,
        in_specs=[pl.BlockSpec(memory_space=pltpu.VMEM)] + waits(after),
        out_shape=(
            jax.ShapeDtypeStruct((rows, parts * width), f32),
            jax.ShapeDtypeStruct((packed - parts * rows, width), f32),
        ),
        compiler_params=params(),
        cost_estimate=cost(1e6, 1e6),
    )(own, *after)


class Sum:
    def __init__(self, blocks, sizes):
        self.sizes = sizes
        devices = sizes["z"] * sizes["x"] * sizes["c"] * sizes["y"]
        self.terms = [blocks.reshape(tuple(sizes[a] for a in PLACE) + (-1, blocks.shape[-1]))]
        self.came = None
        self.next_bit = {a: 1 for a in PLACE}

    def part(self, dim, which):
        total = None
        for term in self.terms:
            shape = term.shape
            view = term.reshape(shape[:dim] + (shape[dim] // 2, 2) + shape[dim + 1 :])
            piece = lax.dynamic_index_in_dim(view, which, axis=dim + 1, keepdims=False)
            total = piece if total is None else (total.astype(f32) + piece.astype(f32))
        return total.astype(bf16)

    def send(self, axis):
        self.land()
        dim, bit, size = PLACE.index(axis), self.next_bit[axis], self.sizes[axis]
        self.next_bit[axis] = 2 * bit
        mine = lax.axis_index(axis) // bit % 2
        away = self.part(dim, 1 - mine)
        self.came = swap(away, axis, size, bit)
        self.kept = self.part(dim, mine)
        return away

    def land(self):
        if self.came is not None:
            self.terms = [self.kept, self.came]
            self.came = None

    def open_steps(self, axis):
        return self.next_bit[axis] < self.sizes[axis]

    def result(self):
        self.land()
        total = self.terms[0].astype(f32) + self.terms[1].astype(f32)
        return total.reshape(total.shape[4:])


def sum_step(values, axis, sizes):
    bit = 1
    while bit < sizes[axis]:
        values = values + swap(values, axis, sizes[axis], bit)
        bit *= 2
    return values


def small_sums(sums, more_sums, hidden_sum, folded, rel_table, width):
    table_sum = jnp.pad(unfold_table(folded).reshape(-1), (0, -rel_table.size % width)).reshape(-1, width)
    return jnp.concatenate([more_sums[:2], sums[:6], hidden_sum, table_sum], axis=0)


def column_parts(matrix, width):
    return [matrix[:, at : at + width] for at in range(0, matrix.shape[1], width)]


def blocks_of(parts, devices):
    return jnp.concatenate([part.reshape(devices, -1, part.shape[1]) for part in parts], axis=1)


def take(blocks, at, rows):
    return blocks[:, at : at + rows].reshape(-1, blocks.shape[2])


def on_device(
    sizes,
    tokens,
    coords,
    rel_pos,
    rel_box,
    entity_pairs,
    entity_grad,
    w_qkv,
    w_attn_out,
    dcpe_table,
    biases,
    norm_gains,
    w_ff_in,
    w_ff_out,
    ff_bias,
    rel_table,
):
    devices = sizes["z"] * sizes["x"] * sizes["c"] * sizes["y"]
    live, width = tokens.shape[1], tokens.shape[2]
    hidden = ff_bias.shape[0] * devices
    count = -(-live // 64) * 64
    extra = count - live
    shard, ff_shard = biases.shape[1], ff_bias.shape[0]
    d_rows, t_rows, h_rows = w_qkv.shape[0], dcpe_table.shape[0], w_ff_out.shape[0]
    ff_parts = hidden // width

    fast = sizes == {"z": 4, "x": 2, "c": 2, "y": 2} and d_rows % 8 == 0
    place = jnp.stack([lax.axis_index(axis) for axis in PLACE]).astype(jnp.int32)
    pairs = HEADS // 2
    at = 4 * d_rows + t_rows

    packed = packed_buckets(rel_pos.reshape(live, 1, live), rel_box[0].transpose(1, 0, 2), count)
    lookup = lookup_rows(rel_table)
    near, far = lookup[:HEADS], lookup[HEADS:]
    places = jnp.pad(coords[0], ((0, 0), (0, extra)), constant_values=OUTSIDE)
    slots = entity_pairs.reshape(1, -1)
    slot_grads = entity_grad.reshape(slots.shape[1], width)
    padded = jnp.pad(tokens[0], ((0, extra), (0, 0)))

    vectors = jnp.pad(jnp.concatenate([biases, norm_gains], axis=0), ((0, 0), (0, width - shard)))
    small_own = jnp.concatenate([vectors, jnp.pad(ff_bias[None], ((0, 7), (0, width - ff_shard)))], axis=0)
    if fast:
        attn_own, ff_own = pack(w_qkv, w_attn_out, dcpe_table, small_own, w_ff_in, w_ff_out)
    else:
        attn_own = jnp.concatenate(column_parts(w_qkv, width) + [w_attn_out, dcpe_table, small_own], axis=0)
        ff_own = jnp.concatenate(column_parts(w_ff_in, width) + [w_ff_out], axis=0)
    whole = lax.all_gather(attn_own, PLACE, axis=0)
    small = whole[:, at : at + 8, :shard].transpose(1, 0, 2).reshape(8, width).astype(f32)
    hidden_bias = whole[:, at + 8, :ff_shard].reshape(ff_parts, width).astype(f32)

    if fast:
        cut = ff_own.shape[0] // 2
        by_z = [ff_own] + [swap(ff_own, "z", 4, bit) for bit in (1, 2, 3)]
        bias_one = score_bias(packed, near, live)
        head, tail = spread(place, (0, 0), [by_z, by_z], [(0, cut), (cut, cut)], [bias_one])
        head_came, tail_came = swap(head, "x", 2, 1), swap(tail, "y", 2, 1)
        bias_two = score_bias(packed, far, live, [head, tail])
        groups = [(head, head_came), (tail, tail_came)]
        head, tail = spread(place, (1, 3), groups, [(0, cut), (0, cut)], [bias_two])
        head_came, tail_came = swap(head, "y", 2, 1), swap(tail, "x", 2, 1)
        begin, begin_rows, united, *w_parts = embed(padded, places.T, small, [whole], [head, tail])
        attention_one, context_one = attend(united, bias_one, 0, pairs // 2)
        w_one = join(place, head, head_came, tail, tail_came, [context_one])
        w_two = swap(w_one, "c", 2, 1)
        attention_two, context_two = attend(united, bias_two, pairs // 2, pairs, [w_one])
        w_one, w_two = (w.reshape((devices // 4, 2) + w.shape[3:]) for w in (w_one, w_two))
    else:
        second = lax.all_gather(ff_own, PLACE, axis=0)
        w_parts = [take(whole, i * d_rows, d_rows) for i in range(4)]
        full_table = take(whole, 4 * d_rows, t_rows)
        w_one = jnp.stack([take(second, i * d_rows, d_rows) for i in range(ff_parts)])
        w_two = take(second, ff_parts * d_rows, h_rows).reshape(ff_parts, width, width)
        begin, begin_rows, united = embed(padded, places.T, small, [full_table] + w_parts[:3])
        attention_one, context_one = attend(united, score_bias(packed, near, live), 0, pairs // 2)
        attention_two, context_two = attend(united, score_bias(packed, far, live), pairs // 2, pairs)
    context = (context_one, context_two)
    layer_out, g_out, d_pre, d_context, sums, hidden_sum, *g_ff = middle(
        place, fast, devices, live, begin, context, w_parts[3], w_one, w_two, small, hidden_bias, slots, slot_grads
    )

    back_one = partial(attend_back, united, attention_one, d_context, 0, pairs // 2)
    back_two = partial(attend_back, united, attention_two, d_context, pairs // 2, pairs)
    if fast:
        ff = g_ff[0].reshape((-1,) + g_ff[0].shape[3:])
        ff = lax.psum_scatter(ff, ("c", "x", "y"), scatter_dimension=0, tiled=False)
        half_one = back_one()
        half_two = back_two([half_one[0]])
        halves = (half_one[:3], half_two[:3])
        g_one, g_two, more_sums = qkv_back(place, fast, devices, halves, g_out, begin_rows)
        attn = PackedSum(place, g_one, g_two, sizes)
        input_grad, g_one, g_two = embed_back(
            place, fast, devices, halves, w_parts[:3], d_pre, places, t_rows * devices, [more_sums]
        )
        position = PackedSum(place, g_one, g_two, sizes)
        sent = attn.send_first([input_grad])
        sent = position.send_first(sent)
        table = partial(table_grad, packed, (half_one[3], half_two[3]))
        early = table(0, 3, sent)
        sent = attn.send_second([early])
        later = table(3, TABLE_BLOCKS, sent)
        sent = position.send_second([later])
        ff, small_sum, _ = lax.optimization_barrier(
            (ff, small_sums(sums, more_sums, hidden_sum, early + later, rel_table, width), sent[0])
        )
        ff = lax.psum_scatter(ff, "z", scatter_dimension=0, tiled=False)
        for axis in ("c", "x", "y"):
            small_sum = small_sum + swap(small_sum, axis, sizes[axis], 1)
        keep, came, away = send_along_z(place, attn.pairs + position.pairs, [small_sum])
        small_sum, input_grad, _ = lax.optimization_barrier((small_sum, input_grad, away[0]))
        for bit in (1, 2):
            small_sum = small_sum + swap(small_sum, "z", sizes["z"], bit)
        g_in, g_back = finish_ff(ff, d_rows, ff_parts, [small_sum])
        g_qkv, g_out, g_table = finish_attn(keep, came, d_rows, [g_in])
    else:
        half_one, half_two = back_one(), back_two()
        halves = (half_one[:3], half_two[:3])
        g_qkv, g_out, more_sums = qkv_back(place, fast, devices, halves, g_out, begin_rows)
        input_grad, g_table = embed_back(
            place, fast, devices, halves, w_parts[:3], d_pre, places, t_rows * devices
        )
        folded = table_grad(packed, (half_one[3], half_two[3]), 0, TABLE_BLOCKS)
        g_in, g_back = jnp.concatenate(list(g_ff[0]), axis=1), g_ff[1].reshape(hidden, width)
        totals = [Sum(grad, sizes) for grad in (g_in, g_back, g_qkv, g_out, g_table)]
        for axis in PLACE:
            while totals[0].open_steps(axis):
                for total in totals:
                    total.send(axis)
        g_in, g_back, g_qkv, g_out, g_table = (total.result() for total in totals)
        small_sum = small_sums(sums, more_sums, hidden_sum, folded, rel_table, width)
        for axis in PLACE:
            small_sum = sum_step(small_sum, axis, sizes)

    index = lax.axis_index(PLACE)
    vectors = lax.dynamic_slice_in_dim(small_sum[:8], index * shard, shard, axis=1)
    ff_sum = small_sum[8 : 8 + ff_parts].reshape(-1)
    table_sum = small_sum[8 + ff_parts :].reshape(-1)[: rel_table.size].reshape(rel_table.shape)
    return (
        layer_out[None],
        input_grad[None, :live],
        g_qkv,
        g_out,
        g_table,
        vectors[:6],
        vectors[6:],
        g_in,
        g_back,
        lax.dynamic_slice_in_dim(ff_sum, index * ff_shard, ff_shard, axis=0),
        table_sum,
    )


def solution(mesh):
    outer, inner = mesh.shape["dp"], mesh.shape["fsdp"]
    sizes = {"z": outer // 4, "x": 2, "c": 2, "y": inner}
    split = Mesh(mesh.devices.reshape(tuple(sizes[a] for a in PLACE)), PLACE)
    rows = P(PLACE, None)
    three = P(PLACE, None, None)
    four = P(PLACE, None, None, None)
    columns = P(None, PLACE)
    return jax.shard_map(
        partial(on_device, sizes),
        mesh=split,
        in_specs=(three, three, three, four, three, four, rows, rows, rows, columns, columns, rows, rows, P(PLACE), P()),
        out_specs=(three, three, rows, rows, rows, columns, columns, rows, rows, P(PLACE), P()),
        check_vma=False,
    )
```

```python
from functools import partial

import jax
import jax.numpy as jnp
from jax import lax
from jax.experimental import pallas as pl
from jax.experimental.pallas import tpu as pltpu
from jax.sharding import Mesh
from jax.sharding import PartitionSpec as P

HEADS = 12
HEAD_DIM = 64
B1 = 32
B2 = 64
PAIR = 2 * HEAD_DIM
EPSILON = 1e-05
VMEM_LIMIT = 58 * 2**20
NEVER = -1e30
OUTSIDE = -4096

bf16 = jnp.bfloat16
f32 = jnp.float32


def dot(a, b):
    return jnp.dot(a, b, preferred_element_type=f32)


def dot_nt(a, b):
    return lax.dot_general(a, b, (((1,), (1,)), ((), ())), preferred_element_type=f32)


def dot_tn(a, b):
    return lax.dot_general(a, b, (((0,), (0,)), ((), ())), preferred_element_type=f32)


def params():
    return pltpu.CompilerParams(vmem_limit_bytes=VMEM_LIMIT)


def cost(flops, moved):
    return pl.CostEstimate(flops=int(flops / 1000), bytes_accessed=int(moved / 1000), transcendentals=0)


def waits(arrays):
    return [pl.BlockSpec(memory_space=pl.ANY)] * len(arrays)


def full(shape):
    return pl.BlockSpec(shape, lambda *_: (0,) * len(shape))


def buckets_kernel(pos_ref, box_ref, out_ref, rows_ref):
    live = pos_ref.shape[0]
    whole = live // 8 * 8
    rows_ref[...] = jnp.zeros_like(rows_ref)

    def packed(at):
        return pos_ref[at, 0, :] + box_ref[at, 0, :] * 32 + box_ref[at, 1, :] * 2048

    def eight_rows(step, carry):
        at = pl.ds(pl.multiple_of(step * 8, 8), 8)
        rows_ref[at, :live] = packed(at)
        return carry

    lax.fori_loop(0, whole // 8, eight_rows, 0)
    if whole < live:
        rows_ref[whole:live, :live] = packed(pl.ds(whole, live - whole))
    out_ref[...] = rows_ref[...].T[: out_ref.shape[0]]


def packed_buckets(rel_pos, rel_box, count):
    wide = -(-count // 128) * 128
    return pl.pallas_call(
        buckets_kernel,
        out_shape=jax.ShapeDtypeStruct((count, wide), jnp.int32),
        scratch_shapes=[pltpu.VMEM((wide, wide), jnp.int32)],
        compiler_params=params(),
        cost_estimate=cost(1e6, 1e6),
    )(rel_pos, rel_box)


def bias_kernel(live, index_ref, table_ref, *refs):
    out_ref = refs[-1]
    heads, rows, width = out_ref.shape
    first_row = pl.program_id(0) * rows
    tables = [jnp.broadcast_to(table_ref[r : r + 1, :], (8, 128)) for r in range(2 * heads)]

    def eight_rows(step, carry):
        at = pl.multiple_of(step * 8, 8)
        key_ids = first_row + at + lax.broadcasted_iota(jnp.int32, (8, 128), 0)
        dead = jnp.where(key_ids < live, 0.0, NEVER)
        for left in range(0, width, 128):
            packed = index_ref[pl.ds(at, 8), left : left + 128]
            flat = packed & (B1 - 1)
            across = (lax.shift_right_logical(packed, 5) & (B2 - 1)) + B1
            downward = lax.shift_right_logical(packed, 11)
            for head in range(heads):
                low, high = tables[2 * head], tables[2 * head + 1]
                looked = (
                    jnp.take_along_axis(low, flat, axis=1, mode="promise_in_bounds")
                    + jnp.take_along_axis(low, across, axis=1, mode="promise_in_bounds")
                    + jnp.take_along_axis(high, downward, axis=1, mode="promise_in_bounds")
                    + dead
                )
                right = min(left + 128, width)
                out_ref[head, pl.ds(at, 8), left:right] = looked[:, : right - left]
        return carry

    lax.fori_loop(0, rows // 8, eight_rows, 0)


def score_bias(packed, lookup, live, after=()):
    keys = width = packed.shape[0]
    heads = lookup.shape[0] // 2
    rows = 64
    return pl.pallas_call(
        partial(bias_kernel, live),
        grid=(keys // rows,),
        in_specs=[pl.BlockSpec((rows, packed.shape[1]), lambda i: (i, 0)), full(lookup.shape)] + waits(after),
        out_specs=pl.BlockSpec((heads, rows, width), lambda i: (0, i, 0)),
        out_shape=jax.ShapeDtypeStruct((heads, keys, width), f32),
        compiler_params=params(),
        cost_estimate=cost(3e10, 4 * heads * keys * width),
    )(packed, lookup, *after)


def lookup_rows(rel_table):
    near = jnp.pad(rel_table[: B1 + B2].T, ((0, 0), (0, 128 - B1 - B2)))
    far = jnp.pad(rel_table[B1 + B2 :].T, ((0, 0), (0, 128 - B2)))
    return jnp.stack([near, far], axis=1).reshape(2 * HEADS, 128).astype(f32)


def project(tokens, places_ref, table_half, weights, small_ref, begin_ref, rows_ref, united_ref):
    count, width = tokens.shape
    total = tokens.astype(f32)
    for side in range(2):
        table = table_half(side)
        columns = lax.broadcasted_iota(jnp.int32, (count, table.shape[0]), 1)
        hot = jnp.where(places_ref[:, side : side + 1] == columns, 1.0, 0.0).astype(bf16)
        total += dot(hot, table)
    begin_ref[...] = total
    rows = total.astype(bf16)
    rows_ref[...] = rows
    query, key, value = weights()
    united_ref[:, :width] = ((dot(rows, query) + small_ref[0:1, :]) * 0.125).astype(bf16)
    united_ref[:, width : 2 * width] = dot(rows, key).astype(bf16)
    united_ref[:, 2 * width :] = (dot(rows, value) + small_ref[1:2, :]).astype(bf16)


def embed_kernel(token_ref, places_ref, table_ref, query_ref, key_ref, value_ref, small_ref, *outs):
    half = table_ref.shape[0] // 2
    project(
        token_ref[...],
        places_ref,
        lambda side: table_ref[side * half : (side + 1) * half, :],
        lambda: (query_ref[...], key_ref[...], value_ref[...]),
        small_ref,
        *outs,
    )


def spread_vectors(raw, ff_parts):
    devices = raw.shape[0]
    width = ff_parts[0].shape[1]
    shard, ff_shard = width // devices, width * len(ff_parts) // devices
    column = lax.broadcasted_iota(jnp.int32, (1, width), 1).astype(f32)
    lane = lax.broadcasted_iota(jnp.int32, (128, width), 0).astype(f32)
    low = raw.astype(f32)

    def copied(rows, extent):
        block = jnp.floor((column + 0.5) * (1.0 / extent))
        copies = jnp.where(column - block * extent == lane, 1.0, 0.0).astype(bf16)
        return dot(rows.astype(bf16), copies), block

    repeated, block = copied(low[:, :8].reshape(devices * 8, 128), shard)
    device = lax.broadcasted_iota(jnp.int32, (devices, 8, width), 0).astype(f32)
    vectors = jnp.sum(jnp.where(block == device, repeated.reshape(devices, 8, width), 0.0), axis=0)
    repeated, block = copied(low[:, 8:9].reshape(devices, 128), ff_shard)
    device = lax.broadcasted_iota(jnp.int32, (devices, width), 0).astype(f32)
    for part, ref in enumerate(ff_parts):
        first = part * (width // ff_shard)
        ref[...] = jnp.sum(jnp.where(block + first == device, repeated, 0.0), axis=0, keepdims=True)
    return vectors


def embed_packed_kernel(token_ref, places_ref, whole_hbm, *refs):
    united_ref, small_ref, hidden_bias_ref, *hbm_refs = refs[-18:-9]
    near_ref, far_ref, table_ref, raw_ref, begin_ref, rows_ref, weight_ref, load_sems, store_sems = refs[-9:]
    devices, pair, width = near_ref.shape
    at = 2 * pair
    raw_at = at + table_ref.shape[1]
    loads = [
        pltpu.make_async_copy(whole_hbm.at[:, pl.ds(at, table_ref.shape[1])], table_ref, load_sems.at[0]),
        pltpu.make_async_copy(whole_hbm.at[:, pl.ds(0, pair)], near_ref, load_sems.at[1]),
        pltpu.make_async_copy(whole_hbm.at[:, pl.ds(pair, pair)], far_ref, load_sems.at[2]),
        pltpu.make_async_copy(whole_hbm.at[:, pl.ds(raw_at, 16), pl.ds(0, 128)], raw_ref, load_sems.at[3]),
    ]
    for load in loads:
        load.start()
    stores = []

    def store(source, target):
        stores.append(pltpu.make_async_copy(source, target, store_sems.at[len(stores)]))
        stores[-1].start()

    loads[3].wait()
    parts = hidden_bias_ref.shape[0]
    small_ref[...] = spread_vectors(raw_ref[...], [hidden_bias_ref.at[pl.ds(part, 1)] for part in range(parts)])
    loads[0].wait()

    def table_half(side):
        rows = table_ref[side * devices // 2 : (side + 1) * devices // 2]
        return rows.reshape(devices // 2 * rows.shape[1], width)

    def weights():
        store(begin_ref, hbm_refs[0])
        store(rows_ref, hbm_refs[1])
        for index, ref in enumerate((near_ref, far_ref)):
            loads[1 + index].wait()
            both = ref[...].astype(f32)
            for which in range(2):
                part = 2 * index + which
                rows = both[:, which * pair // 2 : (which + 1) * pair // 2]
                weight_ref[part] = rows.reshape(width, width).astype(bf16)
                store(weight_ref.at[part], hbm_refs[2 + part])
        return [weight_ref[part] for part in range(3)]

    project(token_ref[...], places_ref, table_half, weights, small_ref, begin_ref, rows_ref, united_ref)
    for copy in stores:
        copy.wait()


def embed_packed(tokens, places, whole, table_rows, ff_parts, after):
    count, width = tokens.shape
    devices = whole.shape[0]
    d_rows = width // devices
    vmem = pl.BlockSpec(memory_space=pltpu.VMEM)
    away = pl.BlockSpec(memory_space=pl.ANY)
    square = jax.ShapeDtypeStruct((width, width), bf16)
    united, small, hidden_bias, begin, rows, *weights = pl.pallas_call(
        embed_packed_kernel,
        in_specs=[vmem] * 2 + [away] + waits(after),
        out_specs=(vmem,) * 3 + (away,) * 6,
        out_shape=(
            jax.ShapeDtypeStruct((count, 3 * width), bf16),
            jax.ShapeDtypeStruct((8, width), f32),
            jax.ShapeDtypeStruct((ff_parts, width), f32),
            jax.ShapeDtypeStruct((count, width), f32),
            jax.ShapeDtypeStruct((count, width), bf16),
        )
        + (square,) * 4,
        scratch_shapes=[
            pltpu.VMEM((devices, 2 * d_rows, width), bf16),
            pltpu.VMEM((devices, 2 * d_rows, width), bf16),
            pltpu.VMEM((devices, table_rows, width), bf16),
            pltpu.VMEM((devices, 16, 128), bf16),
            pltpu.VMEM((count, width), f32),
            pltpu.VMEM((count, width), bf16),
            pltpu.VMEM((4, width, width), bf16),
            pltpu.SemaphoreType.DMA((4,)),
            pltpu.SemaphoreType.DMA((6,)),
        ],
        compiler_params=params(),
        cost_estimate=cost(2 * count * width * 5 * width, 12e6),
    )(tokens, places, whole, *after)
    return begin, rows, united, weights, small, hidden_bias


def embed(tokens, places, small, weights):
    count, width = tokens.shape
    return pl.pallas_call(
        embed_kernel,
        out_shape=(
            jax.ShapeDtypeStruct((count, width), f32),
            jax.ShapeDtypeStruct((count, width), bf16),
            jax.ShapeDtypeStruct((count, 3 * width), bf16),
        ),
        compiler_params=params(),
        cost_estimate=cost(2 * count * width * 5 * width, 12e6),
    )(tokens, places, *weights, small)


def head_mask(head):
    return lax.broadcasted_iota(jnp.int32, (1, PAIR), 1) // HEAD_DIM == head


def attend_kernel(half, query_ref, key_ref, value_ref, *refs):
    bias_refs = refs[:2]
    attention_ref, context_ref = refs[-2:]
    query, key = query_ref[...], key_ref[...]
    value_t = value_ref[...].astype(f32).T.astype(bf16)

    def pair(bias_ref):
        parts = []
        for head in range(2):
            scores = dot_nt(jnp.where(head_mask(head), key, 0), query) + bias_ref[head]
            raised = jnp.exp(scores - jnp.max(scores, axis=0, keepdims=True))
            attention = (raised * (1.0 / jnp.sum(raised, axis=0, keepdims=True))).astype(bf16)
            attention_ref[head] = attention
            parts.append(dot(value_t[head * HEAD_DIM : (head + 1) * HEAD_DIM], attention))
        context_ref[...] = jnp.concatenate(parts, axis=0).T.astype(bf16)

    first = pl.program_id(0) < half

    @pl.when(first)
    def _():
        pair(bias_refs[0])

    @pl.when(jnp.logical_not(first))
    def _():
        pair(bias_refs[1])


def attend(united, bias_one, bias_two, after=()):
    count = united.shape[0]
    pairs = HEADS // 2
    half = bias_one.shape[0] // 2
    column = lambda shift: pl.BlockSpec((count, PAIR), lambda p: (0, p + shift))
    square = lambda index: pl.BlockSpec((2, count, count), lambda p: (index(p), 0, 0))
    return pl.pallas_call(
        partial(attend_kernel, half),
        grid=(pairs,),
        in_specs=[
            column(0),
            column(pairs),
            column(2 * pairs),
            square(lambda p: jnp.minimum(p, half - 1)),
            square(lambda p: jnp.maximum(p - half, 0)),
        ]
        + waits(after),
        out_specs=(square(lambda p: p), column(0)),
        out_shape=(
            jax.ShapeDtypeStruct((HEADS, count, count), bf16),
            jax.ShapeDtypeStruct((count, HEADS * HEAD_DIM), bf16),
        ),
        compiler_params=params(),
        cost_estimate=cost(4 * HEADS * count * count * HEAD_DIM, 6 * HEADS * count * count),
    )(united, united, united, bias_one, bias_two, *after)


def attend_back_kernel(query_ref, key_ref, value_ref, attention_ref, d_context_ref, *refs):
    d_query_ref, d_key_ref, d_value_ref, d_scores_ref = refs[-4:]
    query, value, d_context = query_ref[...], value_ref[...], d_context_ref[...]
    key_t = key_ref[...].astype(f32).T.astype(bf16)
    parts = []
    d_key = jnp.zeros(query.shape, f32)
    d_value = jnp.zeros(query.shape, f32)
    for head in range(2):
        mask = head_mask(head)
        d_attention = dot_nt(jnp.where(mask, value, 0), d_context)
        attention_low = attention_ref[head]
        attention = attention_low.astype(f32)
        centre = jnp.sum(attention * d_attention, axis=0, keepdims=True)
        d_scores = (attention * (d_attention - centre)).astype(bf16)
        d_scores_ref[head] = d_scores
        d_key += dot(d_scores, jnp.where(mask, query, 0))
        d_value += dot(attention_low, jnp.where(mask, d_context, 0))
        parts.append(dot(key_t[head * HEAD_DIM : (head + 1) * HEAD_DIM], d_scores))
    d_query_ref[...] = jnp.concatenate(parts, axis=0).T.astype(bf16) * bf16(0.125)
    d_key_ref[...] = d_key.astype(bf16)
    d_value_ref[...] = d_value.astype(bf16)


def attend_back(united, attention, d_context):
    count = united.shape[0]
    pairs = HEADS // 2
    column = lambda shift: pl.BlockSpec((count, PAIR), lambda p: (0, p + shift))
    square = pl.BlockSpec((2, count, count), lambda p: (p, 0, 0))
    joined = jax.ShapeDtypeStruct((count, HEADS * HEAD_DIM), bf16)
    return pl.pallas_call(
        attend_back_kernel,
        grid=(pairs,),
        in_specs=[column(0), column(pairs), column(2 * pairs), square, column(0)],
        out_specs=(column(0), column(0), column(0), square),
        out_shape=(joined, joined, joined, jax.ShapeDtypeStruct((HEADS, count, count), bf16)),
        compiler_params=params(),
        cost_estimate=cost(8 * HEADS * count * count * HEAD_DIM, 4 * HEADS * count * count),
    )(united, united, united, attention, d_context)


def unit_rows(values):
    centred = values - jnp.mean(values, axis=1, keepdims=True)
    scale = lax.rsqrt(jnp.mean(centred * centred, axis=1, keepdims=True) + EPSILON)
    return centred * scale, scale


def unit_rows_back(units, scale, d_units):
    spread = jnp.mean(d_units * units, axis=1, keepdims=True)
    return scale * (d_units - jnp.mean(d_units, axis=1, keepdims=True) - units * spread)


def column_sum(values):
    return jnp.sum(values.astype(f32), axis=0, keepdims=True)


def split_cores(values, rows):
    inner = values.shape[0] // rows
    return values.reshape((inner // 4, 2, 2, rows, values.shape[1]))


def middle_kernel(packed, place_ref, begin_ref, context_ref, w_out_ref, one_hbm, two_hbm, *refs):
    small_ref, hidden_bias_ref, slot_ref, slot_grad_ref, layer_ref, g_out_ref, *refs = refs
    d_pre_ref, d_context_ref, sums_ref, hidden_sum_ref, g_one_ref, *refs = refs
    if not packed:
        g_two_ref, *refs = refs
    w_in_ref, w_back_ref, act_ref, slope_ref, d_inner_ref, total_ref, load_sems, *refs = refs
    count, width = begin_ref.shape
    parts = w_in_ref.shape[0]
    context = context_ref[...]
    w_in = lambda part: w_in_ref[part].reshape(width, width)
    if packed:
        buffer_ref, store_sems = refs
        core = place_ref[2]
        devices = buffer_ref.shape[1] * 4
        d_rows, h_rows = width // devices, width * parts // devices
        blocks_each = width // h_rows // 4
        w_back = lambda part: w_back_ref[pl.ds(part * blocks_each, blocks_each)].reshape(width, width)
        loads = []
        for side, source in enumerate((one_hbm, two_hbm)):
            in_rows, back_rows = pl.ds(0, parts * d_rows), pl.ds(parts * d_rows, h_rows)
            target = buffer_ref.at[side, :, :, in_rows]
            loads.append(pltpu.make_async_copy(source.at[:, :, in_rows], target, load_sems.at[side]))
            target = w_back_ref.at[:, side ^ core]
            loads.append(pltpu.make_async_copy(source.at[:, :, back_rows], target, load_sems.at[2 + side]))
    else:
        w_back = lambda part: w_back_ref[part]
        loads = [
            pltpu.make_async_copy(one_hbm, w_in_ref, load_sems.at[0]),
            pltpu.make_async_copy(two_hbm, w_back_ref, load_sems.at[1]),
        ]
    for load in loads:
        load.start()

    row = lambda i: small_ref[i : i + 1, :]
    attended = dot(context, w_out_ref[...]) + row(2)
    units, scale = unit_rows(begin_ref[...] + attended)
    mid = units * row(6) + row(3)
    mid_rows = mid.astype(bf16)
    total_ref[...] = mid + row(4)
    for load in loads:
        load.wait()

    def unpack(block, carry):
        for side in range(2):
            for pair in range(parts // 2):
                at = pair * 2 * d_rows
                both = buffer_ref[side, block, :, at : at + 2 * d_rows].astype(f32)
                for which in range(2):
                    rows = both[:, which * d_rows : (which + 1) * d_rows].reshape(2 * d_rows, width)
                    w_in_ref[2 * pair + which, block, side ^ core] = rows.astype(bf16)
        return carry

    if packed:
        lax.fori_loop(0, devices // 4, unpack, 0)

    def forward_part(part, carry):
        inner = dot(mid_rows, w_in(part)) + hidden_bias_ref[pl.ds(part, 1), :]
        share = 0.5 * lax.erf(inner * (2.0**-0.5)) + 0.5
        bell = jnp.exp(inner * inner * -0.5) * (0.5 * 2.0**0.5 / jnp.pi**0.5)
        act = (inner * share).astype(bf16)
        act_ref[part] = act
        slope_ref[part] = (share + inner * bell).astype(bf16)
        total_ref[...] += dot(act, w_back(part))
        return carry

    lax.fori_loop(0, parts, forward_part, 0)
    out_units, out_scale = unit_rows(total_ref[...])
    layer_ref[...] = (out_units * row(7) + row(5)).astype(bf16)[: layer_ref.shape[0]]

    token_ids = lax.broadcasted_iota(jnp.int32, (count, slot_ref.shape[1]), 0)
    slot_hot = jnp.where(slot_ref[...] == token_ids, 1.0, 0.0).astype(bf16)
    out_cot = dot(slot_hot, slot_grad_ref[...])
    sums_ref[3:4, :] = column_sum(out_cot)
    sums_ref[5:6, :] = column_sum(out_cot * out_units)
    d_sum = unit_rows_back(out_units, out_scale, out_cot * row(7))
    sums_ref[2:3, :] = column_sum(d_sum.astype(bf16))
    d_outer = d_sum.astype(bf16)
    total_ref[...] = d_sum
    rows_t = mid.T.astype(bf16)

    def stores(at, rows, first, blocks, sem):
        copies = []
        for side in range(2):
            for step in range(blocks // 2):
                z = first // 2 + step
                source = buffer_ref.at[side, pl.ds(2 * z, 2), :, pl.ds(at, rows)]
                target = g_one_ref.at[side, :, :, z, pl.ds(at, rows)]
                copies.append(pltpu.make_async_copy(source, target, store_sems.at[side, step, sem]))
        return copies

    def store_back(part):
        return stores(parts * d_rows, h_rows, part * blocks_each, blocks_each, part)

    def store_in(pair):
        return stores(pl.multiple_of(pair * 2 * d_rows, 16), 2 * d_rows, 0, devices // 4, parts + pair)

    def backward_part(part, carry):
        d_act = dot_nt(d_outer, w_back(part))
        d_inner = (d_act * slope_ref[part].astype(f32)).astype(bf16)
        hidden_sum_ref[pl.ds(part, 1), :] = column_sum(d_inner)
        total_ref[...] += dot_nt(d_inner, w_in(part))
        d_inner_ref[part] = d_inner
        g_back = dot_tn(act_ref[part], d_outer).astype(bf16)
        if packed:
            blocks = split_cores(g_back, h_rows)
            at = pl.ds(part * blocks_each, blocks_each)
            for side in range(2):
                buffer_ref[side, at, :, parts * d_rows :] = blocks[:, side]
            for copy in store_back(part):
                copy.start()
        else:
            g_two_ref[part] = g_back
            g_one_ref[part] = dot(rows_t, d_inner).astype(bf16)
        return carry

    lax.fori_loop(0, parts, backward_part, 0)

    def pack_pair(pair, carry):
        at = pl.ds(pl.multiple_of(pair * 2 * d_rows, 16), 2 * d_rows)
        for left in range(0, width, 256):
            columns = slice(left, left + 256)
            pieces = [
                dot(rows_t, d_inner_ref[2 * pair + which, :, columns]).reshape(devices, d_rows, 256)
                for which in range(2)
            ]
            joined = jnp.concatenate(pieces, axis=1).astype(bf16).reshape(devices // 4, 2, 2, 2 * d_rows, 256)
            for side in range(2):
                buffer_ref[side, :, :, at, columns] = joined[:, side]
        for copy in store_in(pair):
            copy.start()
        return carry

    if packed:
        lax.fori_loop(0, parts // 2, pack_pair, 0)

    d_mid = total_ref[...]
    d_pre = unit_rows_back(units, scale, d_mid * row(6))
    d_pre_ref[...] = d_pre
    d_att = d_pre.astype(bf16)
    g_out_ref[...] = dot_tn(context, d_att).astype(bf16)
    d_context_ref[...] = dot_nt(d_att, w_out_ref[...]).astype(bf16)
    sums_ref[0:1, :] = column_sum(d_att)
    sums_ref[1:2, :] = column_sum(d_mid)
    sums_ref[4:5, :] = column_sum(d_mid * units)
    sums_ref[6:8, :] = jnp.zeros((2, width), f32)
    if packed:
        for part in range(parts):
            for copy in store_back(part):
                copy.wait()
        for pair in range(parts // 2):
            for copy in store_in(pair):
                copy.wait()


def middle(place, packed, devices, live, begin, context, w_attn_out, w_one, w_two, small, hidden_bias, slots, slot_grads):
    count, width = begin.shape
    parts = hidden_bias.shape[0]
    hidden = parts * width
    vmem = pl.BlockSpec(memory_space=pltpu.VMEM)
    away = pl.BlockSpec(memory_space=pl.ANY)
    if packed:
        weights = [(parts, devices // 4, 2, 2 * width // devices, width), (devices // 4, 2, 2, hidden // devices, width)]
    else:
        weights = [(parts, width, width)] * 2
    scratch = [pltpu.VMEM(shape, bf16) for shape in weights + [(parts, count, width)] * 3]
    scratch += [pltpu.VMEM((count, width), f32), pltpu.SemaphoreType.DMA((4,))]
    if packed:
        rows = 2 * hidden // devices
        grads = (jax.ShapeDtypeStruct((2, 2, 2, devices // 8, rows, width), bf16),)
        scratch += [
            pltpu.VMEM((2, devices // 4, 2, rows, width), bf16),
            pltpu.SemaphoreType.DMA((2, devices // 8, parts + parts // 2)),
        ]
    else:
        grads = (jax.ShapeDtypeStruct((parts, width, width), bf16),) * 2
    grad_space = away if packed else vmem
    return pl.pallas_call(
        partial(middle_kernel, packed),
        in_specs=[pl.BlockSpec(memory_space=pltpu.SMEM)] + [vmem] * 3 + [away] * 2 + [vmem] * 4,
        out_specs=(vmem,) * 6 + (grad_space,) * len(grads),
        out_shape=(
            jax.ShapeDtypeStruct((live, width), bf16),
            jax.ShapeDtypeStruct((width, width), bf16),
            jax.ShapeDtypeStruct((count, width), f32),
            jax.ShapeDtypeStruct((count, width), bf16),
            jax.ShapeDtypeStruct((8, width), f32),
            jax.ShapeDtypeStruct((parts, width), f32),
        )
        + grads,
        scratch_shapes=scratch,
        compiler_params=params(),
        cost_estimate=cost(12 * count * width * hidden, 30e6),
    )(place, begin, context, w_attn_out, w_one, w_two, small, hidden_bias, slots, slot_grads)


def store_blocks(buffer_ref, targets, sems, blocks, first, at, first_sem, core):
    spaces, rows = blocks.shape[0], blocks.shape[3]
    for which in range(2):
        buffer_ref[which ^ core, first : first + spaces, :, at : at + rows] = blocks[:, which]
    copies = []
    for side, target in enumerate(targets):
        source = buffer_ref.at[side, pl.ds(first, spaces), :, pl.ds(at, rows)]
        target = target.at[pl.ds(first, spaces), :, pl.ds(at, rows)]
        copies.append(pltpu.make_async_copy(source, target, sems.at[first_sem + side]))
        copies[-1].start()
    return copies


def qkv_back_kernel(halves, packed, place_ref, *refs):
    d_refs, refs = refs[: 3 * halves], refs[3 * halves :]
    g_out_ref, rows_ref = refs[:2]
    g_one_ref, g_two_ref, sums_ref = refs[-5:-2] if packed else refs[-3:]
    count, width = rows_ref.shape
    rows_t = rows_ref[...].astype(f32).T.astype(bf16)
    grads = [
        jnp.concatenate([d_refs[3 * half + part][...] for half in range(halves)], axis=1) for part in range(3)
    ]
    sums_ref[...] = jnp.zeros((8, width), f32)
    sums_ref[0:1, :] = column_sum(grads[0])
    sums_ref[1:2, :] = column_sum(grads[2])
    if not packed:
        for part in range(3):
            g_one_ref[:, part * width : (part + 1) * width] = dot(rows_t, grads[part]).astype(bf16)
        g_two_ref[...] = g_out_ref[...]
        return
    buffer_ref, sems = refs[-2:]
    core = place_ref[2]
    devices = buffer_ref.shape[1] * 4
    d_rows = width // devices
    for left in range(0, width, 256):
        columns = slice(left, left + 256)
        pieces = [dot(rows_t, grad[:, columns]).reshape(devices, d_rows, 256) for grad in grads]
        pieces.append(g_out_ref[:, columns].astype(f32).reshape(devices, d_rows, 256))
        joined = jnp.concatenate(pieces, axis=1).astype(bf16).reshape(devices // 4, 2, 2, 4 * d_rows, 256)
        for which in range(2):
            buffer_ref[which ^ core, :, :, :, columns] = joined[:, which]
    copies = [
        pltpu.make_async_copy(buffer_ref.at[side], target, sems.at[side])
        for side, target in enumerate((g_one_ref, g_two_ref))
    ]
    for copy in copies:
        copy.start()
    for copy in copies:
        copy.wait()


def qkv_back(place, packed, devices, d_halves, g_out, begin_rows, after=()):
    count, width = begin_rows.shape
    vmem = pl.BlockSpec(memory_space=pltpu.VMEM)
    away = pl.BlockSpec(memory_space=pl.ANY)
    d_all = [d for half in d_halves for d in half]
    scratch = []
    if packed:
        half = (devices // 4, 2, 4 * (width // devices), width)
        grads = (jax.ShapeDtypeStruct(half, bf16),) * 2
        scratch = [pltpu.VMEM((2,) + half, bf16), pltpu.SemaphoreType.DMA((2,))]
    else:
        grads = (jax.ShapeDtypeStruct((width, 3 * width), bf16), jax.ShapeDtypeStruct((width, width), bf16))
    grad_space = away if packed else vmem
    return pl.pallas_call(
        partial(qkv_back_kernel, len(d_halves), packed),
        in_specs=[pl.BlockSpec(memory_space=pltpu.SMEM)] + [vmem] * (len(d_all) + 2) + waits(after),
        out_specs=(grad_space, grad_space, vmem),
        out_shape=grads + (jax.ShapeDtypeStruct((8, width), f32),),
        scratch_shapes=scratch,
        compiler_params=params(),
        cost_estimate=cost(6 * count * width * width, 10e6),
    )(place, *d_all, g_out, begin_rows, *after)


def embed_back_kernel(halves, packed, place_ref, *refs):
    d_refs, refs = refs[: 3 * halves], refs[3 * halves :]
    w_hbm, refs = refs[:3], refs[3:]
    d_pre_ref, coords_ref = refs[:2]
    scratch = 4 if packed else 2
    outs = refs[-scratch - (3 if packed else 2) : -scratch]
    input_grad_ref = outs[0]
    w_ref, load_sems = refs[-scratch:][:2]
    count, width = d_pre_ref.shape
    loads = [pltpu.make_async_copy(w_hbm[part], w_ref.at[part], load_sems.at[part]) for part in range(3)]
    for copy in loads:
        copy.start()
    total = d_pre_ref[...]
    for part in range(3):
        loads[part].wait()
        grad = jnp.concatenate([d_refs[3 * half + part][...] for half in range(halves)], axis=1)
        total += dot_nt(grad, w_ref[part])
    input_grad_ref[...] = total
    low = total.astype(bf16)
    if packed:
        buffer_ref, store_sems = refs[-2:]
        devices, t_rows = buffer_ref.shape[1] * 4, buffer_ref.shape[3]
        half = t_rows * devices // 2
    else:
        half = outs[1].shape[0] // 2
    values = lax.broadcasted_iota(jnp.int32, (half, count), 0)
    copies = []
    for side in range(2):
        hot = jnp.where(coords_ref[side : side + 1, :] == values, 1.0, 0.0).astype(bf16)
        g_table = dot(hot, low).astype(bf16)
        if packed:
            blocks = split_cores(g_table, t_rows)
            first = side * blocks.shape[0]
            copies += store_blocks(buffer_ref, outs[1:], store_sems, blocks, first, 0, 2 * side, place_ref[2])
        else:
            outs[1][side * half : (side + 1) * half, :] = g_table
    for copy in copies:
        copy.wait()


def embed_back(place, packed, devices, d_halves, w_qkv, d_pre, coords, table_rows, after=()):
    count, width = d_pre.shape
    vmem = pl.BlockSpec(memory_space=pltpu.VMEM)
    away = pl.BlockSpec(memory_space=pl.ANY)
    d_all = [d for half in d_halves for d in half]
    scratch = [pltpu.VMEM((3, width, width), bf16), pltpu.SemaphoreType.DMA((3,))]
    if packed:
        half = (devices // 4, 2, table_rows // devices, width)
        grads = (jax.ShapeDtypeStruct(half, bf16),) * 2
        scratch += [pltpu.VMEM((2,) + half, bf16), pltpu.SemaphoreType.DMA((4,))]
    else:
        grads = (jax.ShapeDtypeStruct((table_rows, width), bf16),)
    return pl.pallas_call(
        partial(embed_back_kernel, len(d_halves), packed),
        in_specs=[pl.BlockSpec(memory_space=pltpu.SMEM)]
        + [vmem] * len(d_all)
        + [away] * 3
        + [vmem] * 2
        + waits(after),
        out_specs=(vmem,) + ((away,) if packed else (vmem,)) * len(grads),
        out_shape=(jax.ShapeDtypeStruct((count, width), f32),) + grads,
        scratch_shapes=scratch,
        compiler_params=params(),
        cost_estimate=cost(2 * count * width * (table_rows + 3 * width), 15e6),
    )(place, *d_all, *w_qkv, d_pre, coords, *after)


GROUP = 8
TABLE_BLOCKS = 6
TABLES = ((0, B1), (5, B2), (11, B2))


def table_kernel(halves, index_ref, *refs):
    d_refs = refs[:halves]
    out_ref, total_ref = refs[-2:]
    keys, count = d_refs[0].shape[1:]
    columns = 2 * HEADS * GROUP

    @pl.when(pl.program_id(0) == 0)
    def _():
        total_ref[...] = jnp.zeros_like(total_ref)

    d_scores = jnp.concatenate([d_ref[...].astype(f32) for d_ref in d_refs], axis=0)
    packed = index_ref[:, :count]
    base = 0
    for shift, buckets in TABLES:
        bucket = lax.shift_right_logical(packed, shift) & (buckets - 1)
        upper, lowest = lax.shift_right_logical(bucket, 1).astype(f32), bucket & 1
        uppers = buckets // 2
        values = lax.broadcasted_iota(jnp.int32, (uppers, count), 0).astype(f32).astype(bf16)
        left, right = [], []
        for first in range(0, keys, GROUP):
            group = slice(first, first + GROUP)
            hot = [
                jnp.where(jnp.broadcast_to(upper[k : k + 1], values.shape).astype(bf16) == values, bf16(1), bf16(0))
                for k in range(first, first + GROUP)
            ]
            left.append(jnp.concatenate(hot, axis=0))
            split = [
                jnp.where((lowest[group] == bit)[None], d_scores[:, group, :], 0.0).reshape(HEADS * GROUP, count)
                for bit in range(2)
            ]
            right.append(jnp.concatenate(split, axis=0).astype(bf16))
        total_ref[base : base + uppers * GROUP, :] += dot_nt(
            jnp.concatenate(left, axis=1), jnp.concatenate(right, axis=1)
        )
        base += uppers * GROUP

    @pl.when(pl.program_id(0) == pl.num_programs(0) - 1)
    def _():
        base, pieces = 0, []
        for _, buckets in TABLES:
            shape = (GROUP, buckets // 2, columns)
            block = total_ref[base : base + shape[0] * shape[1], :].reshape(shape)
            own = lax.broadcasted_iota(jnp.int32, shape, 2) % GROUP == lax.broadcasted_iota(jnp.int32, shape, 0)
            pieces.append(jnp.sum(jnp.where(own, block, 0.0), axis=0))
            base += shape[0] * shape[1]
        out_ref[...] = jnp.concatenate(pieces, axis=0)


def table_grad(packed, d_halves, first, last, after=()):
    count = packed.shape[0]
    keys = count // TABLE_BLOCKS
    uppers = (B1 + 2 * B2) // 2
    columns = 2 * HEADS * GROUP
    return pl.pallas_call(
        partial(table_kernel, len(d_halves)),
        grid=(last - first,),
        in_specs=[pl.BlockSpec((keys, packed.shape[1]), lambda i: (i + first, 0))]
        + [pl.BlockSpec((d.shape[0], keys, count), lambda i: (0, i + first, 0)) for d in d_halves]
        + waits(after),
        out_specs=full((uppers, columns)),
        out_shape=jax.ShapeDtypeStruct((uppers, columns), f32),
        scratch_shapes=[pltpu.VMEM((uppers * GROUP, columns), f32)],
        compiler_params=params(),
        cost_estimate=cost(1e10, 2 * HEADS * count * count),
    )(packed, *d_halves, *after)


def unfold_table(folded):
    uppers = folded.shape[0]
    return folded.reshape(uppers, 2, HEADS, GROUP).sum(axis=3).reshape(2 * uppers, HEADS)


PLACE = ("z", "x", "c", "y")


def swap(values, axis, size, bit):
    return lax.ppermute(values, axis, [(i, i ^ bit) for i in range(size)])


def pack_kernel(w_qkv_ref, w_out_ref, table_ref, biases_ref, gains_ref, ff_bias_ref, w_in_ref, w_back_ref, *refs):
    attn_ref, ff_ref, small_ref = refs
    rows, width = w_out_ref.shape
    parts = lambda ref: [ref[:, at : at + width].astype(f32) for at in range(0, ref.shape[1], width)]
    beside = parts(w_qkv_ref) + [w_out_ref[...].astype(f32)]
    attn_ref[: 4 * rows, :] = jnp.concatenate(beside, axis=0).astype(bf16)
    table_end = 4 * rows + table_ref.shape[0]
    attn_ref[4 * rows : table_end, :] = table_ref[...]
    count, shard = biases_ref.shape
    small_ref[...] = jnp.zeros_like(small_ref)
    small_ref[:count, :shard] = biases_ref[...].astype(f32)
    small_ref[count:8, :shard] = gains_ref[...].astype(f32)
    small_ref[8:9, : ff_bias_ref.shape[1]] = ff_bias_ref[...].astype(f32)
    attn_ref[table_end:, :] = small_ref[...].astype(bf16)
    in_parts = parts(w_in_ref)
    ff_ref[: len(in_parts) * rows, :] = jnp.concatenate(in_parts, axis=0).astype(bf16)
    ff_ref[len(in_parts) * rows :, :] = w_back_ref[...]


def pack(w_qkv, w_attn_out, dcpe_table, biases, norm_gains, ff_bias, w_ff_in, w_ff_out):
    rows, width = w_attn_out.shape
    attn_rows = 4 * rows + dcpe_table.shape[0] + 16
    ff_rows = w_ff_in.shape[1] // width * rows + w_ff_out.shape[0]
    return pl.pallas_call(
        pack_kernel,
        out_shape=(
            jax.ShapeDtypeStruct((attn_rows, width), bf16),
            jax.ShapeDtypeStruct((ff_rows, width), bf16),
        ),
        scratch_shapes=[pltpu.VMEM((16, width), f32)],
        compiler_params=params(),
        cost_estimate=cost(1e6, 1e6),
    )(w_qkv, w_attn_out, dcpe_table, biases, norm_gains, ff_bias.reshape(1, -1), w_ff_in, w_ff_out)


def spread_kernel(pieces, cuts, place_ref, *refs):
    outs = refs[-len(cuts) :]
    for piece in range(pieces):

        @pl.when(pl.program_id(0) == piece)
        def _(piece=piece):
            for index, (out_ref, (at, rows)) in enumerate(zip(outs, cuts)):
                source = refs[index * pieces + piece]
                extent = source.shape[:-2]
                out_ref[...] = source[..., at : at + rows, :].reshape(out_ref.shape)


def spread(place, axes, groups, cuts, after=()):
    pieces = len(groups[0])
    operands, in_specs, out_specs, out_shapes = [], [], [], []
    for axis, group, (at, rows) in zip(axes, groups, cuts):
        shape = group[0].shape
        operands += group
        in_specs += [pl.BlockSpec(shape, lambda step, place, zeros=(0,) * len(shape): zeros)] * pieces
        lead = len(shape) - 2
        out_specs.append(
            pl.BlockSpec(
                shape[:-2] + (1, rows, shape[-1]),
                lambda step, place, lead=lead, axis=axis: (0,) * lead + (place[axis] ^ step, 0, 0),
            )
        )
        out_shapes.append(jax.ShapeDtypeStruct(shape[:-2] + (pieces, rows, shape[-1]), bf16))
    return pl.pallas_call(
        partial(spread_kernel, pieces, cuts),
        grid_spec=pltpu.PrefetchScalarGridSpec(
            num_scalar_prefetch=1, grid=(pieces,), in_specs=in_specs + waits(after), out_specs=out_specs
        ),
        out_shape=out_shapes,
        compiler_params=params(),
        cost_estimate=cost(1e6, 1e6),
    )(place, *operands, *after)


def join_kernel(cut, place_ref, head_ref, head_came_ref, tail_ref, tail_came_ref, *refs):
    out_ref = refs[-1]
    mine_x, mine_y = place_ref[1], place_ref[3]
    out_ref[0, :, mine_y, :cut] = head_ref[0]
    out_ref[0, :, 1 - mine_y, :cut] = head_came_ref[0]
    out_ref[0, mine_x, :, cut:] = tail_ref[0]
    out_ref[0, 1 - mine_x, :, cut:] = tail_came_ref[0]


def join(place, head, head_came, tail, tail_came, after=()):
    spaces, _, cut, width = head.shape
    rows = cut + tail.shape[2]
    return pl.pallas_call(
        partial(join_kernel, cut),
        grid_spec=pltpu.PrefetchScalarGridSpec(
            num_scalar_prefetch=1,
            grid=(spaces,),
            in_specs=[pl.BlockSpec((1, 2, cut, width), lambda s, p: (s, 0, 0, 0))] * 2
            + [pl.BlockSpec((1, 2, rows - cut, width), lambda s, p: (s, 0, 0, 0))] * 2
            + waits(after),
            out_specs=pl.BlockSpec((1, 2, 2, rows, width), lambda s, p: (s, 0, 0, 0, 0)),
        ),
        out_shape=jax.ShapeDtypeStruct((spaces, 2, 2, rows, width), bf16),
        compiler_params=params(),
        cost_estimate=cost(1e6, 1e6),
    )(place, head, head_came, tail, tail_came, *after)


def combine_kernel(sources, place_ref, *refs):
    count = sum(len(source) for source in sources)
    kept, came, outs = refs[:count], refs[count : 2 * count], refs[-len(sources) :]
    at = 0
    for source, out_ref in zip(sources, outs):
        first = 0
        for _ in source:
            total = kept[at][...].astype(f32) + came[at][...].astype(f32)
            rows, width = total.shape[-2:]
            out_ref[0, :, first : first + rows, :] = total.astype(bf16).reshape(out_ref.shape[1], rows, width)
            first += rows
            at += 1


def combine(place, steps, outs, after=(), worth=1e6):
    kept, came, in_specs = [], [], []
    out_specs, out_shapes = [], []
    for out in outs:
        for first, second, block, index in out:
            kept.append(first)
            came.append(second)
            in_specs.append(pl.BlockSpec(block, index))
        inner = 1
        for extent in out[0][2][1:-2]:
            inner *= extent
        shape = (inner, sum(entry[2][-2] for entry in out), out[0][2][-1])
        out_specs.append(pl.BlockSpec((1,) + shape, lambda step, place: (step, 0, 0, 0)))
        out_shapes.append(jax.ShapeDtypeStruct((steps,) + shape, bf16))
    return pl.pallas_call(
        partial(combine_kernel, [[None] * len(out) for out in outs]),
        grid_spec=pltpu.PrefetchScalarGridSpec(
            num_scalar_prefetch=1, grid=(steps,), in_specs=in_specs * 2 + waits(after), out_specs=out_specs
        ),
        out_shape=out_shapes,
        compiler_params=params(),
        cost_estimate=cost(worth, worth),
    )(place, *kept, *came, *after)


class PackedSum:
    def __init__(self, place, keep, away, sizes):
        self.place, self.sizes = place, sizes
        shape = (sizes["z"], sizes["x"], sizes["y"]) + keep.shape[2:]
        self.cut, self.width = keep.shape[2] // 2, keep.shape[3]
        self.keep, self.came = keep.reshape(shape), swap(away, "c", 2, 1).reshape(shape)

    def send_first(self, after):
        block_x, block_y = (1, 1, 2, self.cut, self.width), (1, 2, 1, self.cut, self.width)
        pair = (self.keep, self.came)
        keep_a, away_a, keep_b, away_b = combine(
            self.place,
            self.sizes["z"],
            [
                [pair + (block_x, lambda s, p: (s, p[1], 0, 0, 0))],
                [pair + (block_x, lambda s, p: (s, 1 - p[1], 0, 0, 0))],
                [pair + (block_y, lambda s, p: (s, 0, p[3], 1, 0))],
                [pair + (block_y, lambda s, p: (s, 0, 1 - p[3], 1, 0))],
            ],
            after,
        )
        self.pairs = ((keep_a, swap(away_a, "x", 2, 1)), (keep_b, swap(away_b, "y", 2, 1)))
        return [away_a, away_b]

    def send_second(self, after):
        block = (1, 1, self.cut, self.width)
        pair_a, pair_b = self.pairs
        keep_a, away_a, keep_b, away_b = combine(
            self.place,
            self.sizes["z"],
            [
                [pair_a + (block, lambda s, p: (s, p[3], 0, 0))],
                [pair_a + (block, lambda s, p: (s, 1 - p[3], 0, 0))],
                [pair_b + (block, lambda s, p: (s, p[1], 0, 0))],
                [pair_b + (block, lambda s, p: (s, 1 - p[1], 0, 0))],
            ],
            after,
        )
        self.pairs = ((keep_a, swap(away_a, "y", 2, 1)), (keep_b, swap(away_b, "x", 2, 1)))
        return [away_a, away_b]


def send_along_z(place, pairs, after):
    step = lambda pair, other: pair + ((1,) + pair[0].shape[1:], lambda s, p: (p[0] ^ other, 0, 0, 0))
    keep, *away = combine(place, 1, [[step(pair, other) for pair in pairs] for other in range(4)], after)
    return keep, [swap(rows, "z", 4, 1 + other) for other, rows in enumerate(away)], away


def finish_kernel(keep_ref, one_ref, two_ref, three_ref, *refs):
    qkv_ref, out_ref, table_ref = refs[-3:]
    total = keep_ref[0, 0].astype(f32) + one_ref[0, 0].astype(f32)
    total += two_ref[0, 0].astype(f32) + three_ref[0, 0].astype(f32)
    rows, width = out_ref.shape
    for part in range(3):
        qkv_ref[:, part * width : (part + 1) * width] = total[part * rows : (part + 1) * rows]
    out_ref[...] = total[3 * rows : 4 * rows]
    table_ref[...] = total[4 * rows :]


def finish_attn(keep, came, rows, after):
    packed, width = keep.shape[2:]
    return pl.pallas_call(
        finish_kernel,
        in_specs=[pl.BlockSpec(memory_space=pltpu.VMEM)] * 4 + waits(after),
        out_shape=(
            jax.ShapeDtypeStruct((rows, 3 * width), f32),
            jax.ShapeDtypeStruct((rows, width), f32),
            jax.ShapeDtypeStruct((packed - 4 * rows, width), f32),
        ),
        compiler_params=params(),
        cost_estimate=cost(1e6, 1e6),
    )(keep, *came, *after)


def finish_ff_kernel(own_ref, *refs):
    in_ref, back_ref = refs[-2:]
    total = own_ref[...].astype(f32)
    rows, width = in_ref.shape[0], back_ref.shape[1]
    parts = in_ref.shape[1] // width
    for part in range(parts):
        in_ref[:, part * width : (part + 1) * width] = total[part * rows : (part + 1) * rows]
    back_ref[...] = total[parts * rows :]


def finish_ff(own, rows, parts, after):
    packed, width = own.shape
    return pl.pallas_call(
        finish_ff_kernel,
        in_specs=[pl.BlockSpec(memory_space=pltpu.VMEM)] + waits(after),
        out_shape=(
            jax.ShapeDtypeStruct((rows, parts * width), f32),
            jax.ShapeDtypeStruct((packed - parts * rows, width), f32),
        ),
        compiler_params=params(),
        cost_estimate=cost(1e6, 1e6),
    )(own, *after)


class Sum:
    def __init__(self, blocks, sizes):
        self.sizes = sizes
        devices = sizes["z"] * sizes["x"] * sizes["c"] * sizes["y"]
        self.terms = [blocks.reshape(tuple(sizes[a] for a in PLACE) + (-1, blocks.shape[-1]))]
        self.came = None
        self.next_bit = {a: 1 for a in PLACE}

    def part(self, dim, which):
        total = None
        for term in self.terms:
            shape = term.shape
            view = term.reshape(shape[:dim] + (shape[dim] // 2, 2) + shape[dim + 1 :])
            piece = lax.dynamic_index_in_dim(view, which, axis=dim + 1, keepdims=False)
            total = piece if total is None else (total.astype(f32) + piece.astype(f32))
        return total.astype(bf16)

    def send(self, axis):
        self.land()
        dim, bit, size = PLACE.index(axis), self.next_bit[axis], self.sizes[axis]
        self.next_bit[axis] = 2 * bit
        mine = lax.axis_index(axis) // bit % 2
        away = self.part(dim, 1 - mine)
        self.came = swap(away, axis, size, bit)
        self.kept = self.part(dim, mine)
        return away

    def land(self):
        if self.came is not None:
            self.terms = [self.kept, self.came]
            self.came = None

    def open_steps(self, axis):
        return self.next_bit[axis] < self.sizes[axis]

    def result(self):
        self.land()
        total = self.terms[0].astype(f32) + self.terms[1].astype(f32)
        return total.reshape(total.shape[4:])


def sum_step(values, axis, sizes):
    bit = 1
    while bit < sizes[axis]:
        values = values + swap(values, axis, sizes[axis], bit)
        bit *= 2
    return values


def small_sums(sums, more_sums, hidden_sum, folded, rel_table, width):
    table_sum = jnp.pad(unfold_table(folded).reshape(-1), (0, -rel_table.size % width)).reshape(-1, width)
    return jnp.concatenate([more_sums[:2], sums[:6], hidden_sum, table_sum], axis=0)


def column_parts(matrix, width):
    return [matrix[:, at : at + width] for at in range(0, matrix.shape[1], width)]


def blocks_of(parts, devices):
    return jnp.concatenate([part.reshape(devices, -1, part.shape[1]) for part in parts], axis=1)


def take(blocks, at, rows):
    return blocks[:, at : at + rows].reshape(-1, blocks.shape[2])


def on_device(
    sizes,
    tokens,
    coords,
    rel_pos,
    rel_box,
    entity_pairs,
    entity_grad,
    w_qkv,
    w_attn_out,
    dcpe_table,
    biases,
    norm_gains,
    w_ff_in,
    w_ff_out,
    ff_bias,
    rel_table,
):
    devices = sizes["z"] * sizes["x"] * sizes["c"] * sizes["y"]
    live, width = tokens.shape[1], tokens.shape[2]
    hidden = ff_bias.shape[0] * devices
    count = -(-live // 64) * 64
    extra = count - live
    shard, ff_shard = biases.shape[1], ff_bias.shape[0]
    d_rows, t_rows, h_rows = w_qkv.shape[0], dcpe_table.shape[0], w_ff_out.shape[0]
    ff_parts = hidden // width

    fast = sizes == {"z": 4, "x": 2, "c": 2, "y": 2} and d_rows % 8 == 0
    place = jnp.stack([lax.axis_index(axis) for axis in PLACE]).astype(jnp.int32)
    pairs = HEADS // 2
    at = 4 * d_rows + t_rows

    packed = packed_buckets(rel_pos.reshape(live, 1, live), rel_box[0].transpose(1, 0, 2), count)
    lookup = lookup_rows(rel_table)
    near, far = lookup[:HEADS], lookup[HEADS:]
    places = jnp.pad(coords[0], ((0, 0), (0, extra)), constant_values=OUTSIDE)
    slots = entity_pairs.reshape(1, -1)
    slot_grads = entity_grad.reshape(slots.shape[1], width)
    padded = jnp.pad(tokens[0], ((0, extra), (0, 0)))

    if fast:
        attn_own, ff_own = pack(w_qkv, w_attn_out, dcpe_table, biases, norm_gains, ff_bias, w_ff_in, w_ff_out)
    else:
        vectors = jnp.pad(jnp.concatenate([biases, norm_gains], axis=0), ((0, 0), (0, width - shard)))
        small_own = jnp.concatenate([vectors, jnp.pad(ff_bias[None], ((0, 7), (0, width - ff_shard)))], axis=0)
        attn_own = jnp.concatenate(column_parts(w_qkv, width) + [w_attn_out, dcpe_table, small_own], axis=0)
        ff_own = jnp.concatenate(column_parts(w_ff_in, width) + [w_ff_out], axis=0)
    whole = lax.all_gather(attn_own, PLACE, axis=0)

    if fast:
        cut = ff_own.shape[0] // 2
        by_z = [ff_own] + [swap(ff_own, "z", 4, bit) for bit in (1, 2, 3)]
        bias_one = score_bias(packed, near, live)
        head, tail = spread(place, (0, 0), [by_z, by_z], [(0, cut), (cut, cut)], [bias_one])
        head_came, tail_came = swap(head, "x", 2, 1), swap(tail, "y", 2, 1)
        bias_two = score_bias(packed, far, live, [head, tail])
        groups = [(head, head_came), (tail, tail_came)]
        head, tail = spread(place, (1, 3), groups, [(0, cut), (0, cut)], [bias_two])
        head_came, tail_came = swap(head, "y", 2, 1), swap(tail, "x", 2, 1)
        begin, begin_rows, united, w_parts, small, hidden_bias = embed_packed(
            padded, places.T, whole, t_rows, ff_parts, [head, tail, slots, slot_grads]
        )
        w_one = join(place, head, head_came, tail, tail_came, [begin])
        w_two = swap(w_one, "c", 2, 1)
        attention, context = attend(united, bias_one, bias_two, [w_one])
        w_one, w_two = (w.reshape((devices // 4, 2) + w.shape[3:]) for w in (w_one, w_two))
    else:
        small = whole[:, at : at + 8, :shard].transpose(1, 0, 2).reshape(8, width).astype(f32)
        hidden_bias = whole[:, at + 8, :ff_shard].reshape(ff_parts, width).astype(f32)
        second = lax.all_gather(ff_own, PLACE, axis=0)
        w_parts = [take(whole, i * d_rows, d_rows) for i in range(4)]
        full_table = take(whole, 4 * d_rows, t_rows)
        w_one = jnp.stack([take(second, i * d_rows, d_rows) for i in range(ff_parts)])
        w_two = take(second, ff_parts * d_rows, h_rows).reshape(ff_parts, width, width)
        begin, begin_rows, united = embed(padded, places.T, small, [full_table] + w_parts[:3])
        attention, context = attend(united, score_bias(packed, near, live), score_bias(packed, far, live))
    layer_out, g_out, d_pre, d_context, sums, hidden_sum, *g_ff = middle(
        place, fast, devices, live, begin, context, w_parts[3], w_one, w_two, small, hidden_bias, slots, slot_grads
    )

    d_query, d_key, d_value, d_scores = attend_back(united, attention, d_context)
    halves = ((d_query, d_key, d_value),)
    table = partial(table_grad, packed, (d_scores,))
    if fast:
        ff = g_ff[0].reshape((-1,) + g_ff[0].shape[3:])
        ff = lax.psum_scatter(ff, ("c", "x", "y"), scatter_dimension=0, tiled=False)
        g_one, g_two, more_sums = qkv_back(place, fast, devices, halves, g_out, begin_rows)
        attn = PackedSum(place, g_one, g_two, sizes)
        input_grad, g_one, g_two = embed_back(
            place, fast, devices, halves, w_parts[:3], d_pre, places, t_rows * devices, [more_sums]
        )
        position = PackedSum(place, g_one, g_two, sizes)
        sent = attn.send_first([input_grad])
        sent = position.send_first(sent)
        early = table(0, 3, sent)
        sent = attn.send_second([early])
        later = table(3, TABLE_BLOCKS, sent)
        sent = position.send_second([later])
        ff, small_sum, _ = lax.optimization_barrier(
            (ff, small_sums(sums, more_sums, hidden_sum, early + later, rel_table, width), sent[0])
        )
        ff = lax.psum_scatter(ff, "z", scatter_dimension=0, tiled=False)
        for axis in ("c", "x", "y"):
            small_sum = small_sum + swap(small_sum, axis, sizes[axis], 1)
        keep, came, away = send_along_z(place, attn.pairs + position.pairs, [small_sum])
        small_sum, input_grad, _ = lax.optimization_barrier((small_sum, input_grad, away[0]))
        small_sum = small_sum + swap(small_sum, "z", sizes["z"], 1)
        g_in, g_back = finish_ff(ff, d_rows, ff_parts, [small_sum])
        small_sum, g_in = lax.optimization_barrier((small_sum, g_in))
        small_sum = small_sum + swap(small_sum, "z", sizes["z"], 2)
        g_qkv, g_out, g_table = finish_attn(keep, came, d_rows, [g_in])
    else:
        g_qkv, g_out, more_sums = qkv_back(place, fast, devices, halves, g_out, begin_rows)
        input_grad, g_table = embed_back(
            place, fast, devices, halves, w_parts[:3], d_pre, places, t_rows * devices
        )
        folded = table(0, TABLE_BLOCKS)
        g_in, g_back = jnp.concatenate(list(g_ff[0]), axis=1), g_ff[1].reshape(hidden, width)
        totals = [Sum(grad, sizes) for grad in (g_in, g_back, g_qkv, g_out, g_table)]
        for axis in PLACE:
            while totals[0].open_steps(axis):
                for total in totals:
                    total.send(axis)
        g_in, g_back, g_qkv, g_out, g_table = (total.result() for total in totals)
        small_sum = small_sums(sums, more_sums, hidden_sum, folded, rel_table, width)
        for axis in PLACE:
            small_sum = sum_step(small_sum, axis, sizes)

    index = lax.axis_index(PLACE)
    vectors = lax.dynamic_slice_in_dim(small_sum[:8], index * shard, shard, axis=1)
    ff_sum = small_sum[8 : 8 + ff_parts].reshape(-1)
    table_sum = small_sum[8 + ff_parts :].reshape(-1)[: rel_table.size].reshape(rel_table.shape)
    return (
        layer_out[None],
        input_grad[None, :live],
        g_qkv,
        g_out,
        g_table,
        vectors[:6],
        vectors[6:],
        g_in,
        g_back,
        lax.dynamic_slice_in_dim(ff_sum, index * ff_shard, ff_shard, axis=0),
        table_sum,
    )


def solution(mesh):
    outer, inner = mesh.shape["dp"], mesh.shape["fsdp"]
    sizes = {"z": outer // 4, "x": 2, "c": 2, "y": inner}
    split = Mesh(mesh.devices.reshape(tuple(sizes[a] for a in PLACE)), PLACE)
    rows = P(PLACE, None)
    three = P(PLACE, None, None)
    four = P(PLACE, None, None, None)
    columns = P(None, PLACE)
    return jax.shard_map(
        partial(on_device, sizes),
        mesh=split,
        in_specs=(three, three, three, four, three, four, rows, rows, rows, columns, columns, rows, rows, P(PLACE), P()),
        out_specs=(three, three, rows, rows, rows, columns, columns, rows, rows, P(PLACE), P()),
        check_vma=False,
    )
```

```python
from functools import partial

import jax
import jax.numpy as jnp
from jax import lax
from jax.experimental import pallas as pl
from jax.experimental.pallas import tpu as pltpu
from jax.sharding import Mesh
from jax.sharding import PartitionSpec as P

HEADS = 12
HEAD_DIM = 64
B1 = 32
B2 = 64
PAIR = 2 * HEAD_DIM
EPSILON = 1e-05
VMEM_LIMIT = 58 * 2**20
NEVER = -1e30
OUTSIDE = -4096

bf16 = jnp.bfloat16
f32 = jnp.float32


def dot(a, b):
    return jnp.dot(a, b, preferred_element_type=f32)


def dot_nt(a, b):
    return lax.dot_general(a, b, (((1,), (1,)), ((), ())), preferred_element_type=f32)


def dot_tn(a, b):
    return lax.dot_general(a, b, (((0,), (0,)), ((), ())), preferred_element_type=f32)


def params(limit=VMEM_LIMIT):
    return pltpu.CompilerParams(vmem_limit_bytes=limit)


def cost(flops, moved):
    return pl.CostEstimate(flops=int(flops / 1000), bytes_accessed=int(moved / 1000), transcendentals=0)


def waits(arrays):
    return [pl.BlockSpec(memory_space=pl.ANY)] * len(arrays)


def full(shape):
    return pl.BlockSpec(shape, lambda *_: (0,) * len(shape))


def buckets_kernel(pos_ref, box_ref, out_ref, rows_ref):
    live = pos_ref.shape[0]
    whole = live // 8 * 8
    rows_ref[...] = jnp.zeros_like(rows_ref)

    def packed(at):
        return pos_ref[at, 0, :] + box_ref[at, 0, :] * 32 + box_ref[at, 1, :] * 2048

    def eight_rows(step, carry):
        at = pl.ds(pl.multiple_of(step * 8, 8), 8)
        rows_ref[at, :live] = packed(at)
        return carry

    lax.fori_loop(0, whole // 8, eight_rows, 0)
    if whole < live:
        rows_ref[whole:live, :live] = packed(pl.ds(whole, live - whole))
    out_ref[...] = rows_ref[...].T[: out_ref.shape[0]]


def packed_buckets(rel_pos, rel_box, count):
    wide = -(-count // 128) * 128
    return pl.pallas_call(
        buckets_kernel,
        out_shape=jax.ShapeDtypeStruct((count, wide), jnp.int32),
        scratch_shapes=[pltpu.VMEM((wide, wide), jnp.int32)],
        compiler_params=params(),
        cost_estimate=cost(1e6, 1e6),
    )(rel_pos, rel_box)


def bias_kernel(live, index_ref, table_ref, *refs):
    out_ref = refs[-1]
    heads, rows, width = out_ref.shape
    first_row = pl.program_id(0) * rows
    tables = [jnp.broadcast_to(table_ref[r : r + 1, :], (8, 128)) for r in range(2 * heads)]

    def eight_rows(step, carry):
        at = pl.multiple_of(step * 8, 8)
        key_ids = first_row + at + lax.broadcasted_iota(jnp.int32, (8, 128), 0)
        dead = jnp.where(key_ids < live, 0.0, NEVER)
        for left in range(0, width, 128):
            packed = index_ref[pl.ds(at, 8), left : left + 128]
            flat = packed & (B1 - 1)
            across = (lax.shift_right_logical(packed, 5) & (B2 - 1)) + B1
            downward = lax.shift_right_logical(packed, 11)
            for head in range(heads):
                low, high = tables[2 * head], tables[2 * head + 1]
                looked = (
                    jnp.take_along_axis(low, flat, axis=1, mode="promise_in_bounds")
                    + jnp.take_along_axis(low, across, axis=1, mode="promise_in_bounds")
                    + jnp.take_along_axis(high, downward, axis=1, mode="promise_in_bounds")
                    + dead
                )
                right = min(left + 128, width)
                out_ref[head, pl.ds(at, 8), left:right] = looked[:, : right - left]
        return carry

    lax.fori_loop(0, rows // 8, eight_rows, 0)


def score_bias(packed, lookup, live, after=()):
    keys = width = packed.shape[0]
    heads = lookup.shape[0] // 2
    rows = 64
    return pl.pallas_call(
        partial(bias_kernel, live),
        grid=(keys // rows,),
        in_specs=[pl.BlockSpec((rows, packed.shape[1]), lambda i: (i, 0)), full(lookup.shape)] + waits(after),
        out_specs=pl.BlockSpec((heads, rows, width), lambda i: (0, i, 0)),
        out_shape=jax.ShapeDtypeStruct((heads, keys, width), f32),
        compiler_params=params(),
        cost_estimate=cost(3e10, 4 * heads * keys * width),
    )(packed, lookup, *after)


def lookup_rows(rel_table):
    near = jnp.pad(rel_table[: B1 + B2].T, ((0, 0), (0, 128 - B1 - B2)))
    far = jnp.pad(rel_table[B1 + B2 :].T, ((0, 0), (0, 128 - B2)))
    return jnp.stack([near, far], axis=1).reshape(2 * HEADS, 128).astype(f32)


def project(tokens, places_ref, table_half, weights, small_ref, begin_ref, rows_ref, united_ref):
    count, width = tokens.shape
    total = tokens.astype(f32)
    for side in range(2):
        table = table_half(side)
        columns = lax.broadcasted_iota(jnp.int32, (count, table.shape[0]), 1)
        hot = jnp.where(places_ref[:, side : side + 1] == columns, 1.0, 0.0).astype(bf16)
        total += dot(hot, table)
    begin_ref[...] = total
    rows = total.astype(bf16)
    rows_ref[...] = rows
    query, key, value = weights()
    united_ref[:, :width] = ((dot(rows, query) + small_ref[0:1, :]) * 0.125).astype(bf16)
    united_ref[:, width : 2 * width] = dot(rows, key).astype(bf16)
    united_ref[:, 2 * width :] = (dot(rows, value) + small_ref[1:2, :]).astype(bf16)


def embed_kernel(token_ref, places_ref, table_ref, query_ref, key_ref, value_ref, small_ref, *outs):
    half = table_ref.shape[0] // 2
    project(
        token_ref[...],
        places_ref,
        lambda side: table_ref[side * half : (side + 1) * half, :],
        lambda: (query_ref[...], key_ref[...], value_ref[...]),
        small_ref,
        *outs,
    )


def spread_vectors(raw, ff_parts):
    devices = raw.shape[0]
    width = ff_parts[0].shape[1]
    shard, ff_shard = width // devices, width * len(ff_parts) // devices
    column = lax.broadcasted_iota(jnp.int32, (1, width), 1).astype(f32)
    lane = lax.broadcasted_iota(jnp.int32, (128, width), 0).astype(f32)
    low = raw.astype(f32)

    def copied(rows, extent):
        block = jnp.floor((column + 0.5) * (1.0 / extent))
        copies = jnp.where(column - block * extent == lane, 1.0, 0.0).astype(bf16)
        return dot(rows.astype(bf16), copies), block

    repeated, block = copied(low[:, :8].reshape(devices * 8, 128), shard)
    device = lax.broadcasted_iota(jnp.int32, (devices, 8, width), 0).astype(f32)
    vectors = jnp.sum(jnp.where(block == device, repeated.reshape(devices, 8, width), 0.0), axis=0)
    repeated, block = copied(low[:, 8:9].reshape(devices, 128), ff_shard)
    device = lax.broadcasted_iota(jnp.int32, (devices, width), 0).astype(f32)
    for part, ref in enumerate(ff_parts):
        first = part * (width // ff_shard)
        ref[...] = jnp.sum(jnp.where(block + first == device, repeated, 0.0), axis=0, keepdims=True)
    return vectors


def embed_packed_kernel(token_ref, places_ref, whole_hbm, *refs):
    united_ref, small_ref, hidden_bias_ref, *hbm_refs = refs[-18:-9]
    near_ref, far_ref, table_ref, raw_ref, begin_ref, rows_ref, weight_ref, load_sems, store_sems = refs[-9:]
    devices, pair, width = near_ref.shape
    at = 2 * pair
    raw_at = at + table_ref.shape[1]
    loads = [
        pltpu.make_async_copy(whole_hbm.at[:, pl.ds(at, table_ref.shape[1])], table_ref, load_sems.at[0]),
        pltpu.make_async_copy(whole_hbm.at[:, pl.ds(0, pair)], near_ref, load_sems.at[1]),
        pltpu.make_async_copy(whole_hbm.at[:, pl.ds(pair, pair)], far_ref, load_sems.at[2]),
        pltpu.make_async_copy(whole_hbm.at[:, pl.ds(raw_at, 16), pl.ds(0, 128)], raw_ref, load_sems.at[3]),
    ]
    for load in loads:
        load.start()
    stores = []

    def store(source, target):
        stores.append(pltpu.make_async_copy(source, target, store_sems.at[len(stores)]))
        stores[-1].start()

    loads[3].wait()
    parts = hidden_bias_ref.shape[0]
    small_ref[...] = spread_vectors(raw_ref[...], [hidden_bias_ref.at[pl.ds(part, 1)] for part in range(parts)])
    loads[0].wait()

    def table_half(side):
        rows = table_ref[side * devices // 2 : (side + 1) * devices // 2]
        return rows.reshape(devices // 2 * rows.shape[1], width)

    def weights():
        store(begin_ref, hbm_refs[0])
        store(rows_ref, hbm_refs[1])
        for index, ref in enumerate((near_ref, far_ref)):
            loads[1 + index].wait()
            both = ref[...].astype(f32)
            for which in range(2):
                part = 2 * index + which
                rows = both[:, which * pair // 2 : (which + 1) * pair // 2]
                weight_ref[part] = rows.reshape(width, width).astype(bf16)
                store(weight_ref.at[part], hbm_refs[2 + part])
        return [weight_ref[part] for part in range(3)]

    project(token_ref[...], places_ref, table_half, weights, small_ref, begin_ref, rows_ref, united_ref)
    for copy in stores:
        copy.wait()


def embed_packed(tokens, places, whole, table_rows, ff_parts, after):
    count, width = tokens.shape
    devices = whole.shape[0]
    d_rows = width // devices
    vmem = pl.BlockSpec(memory_space=pltpu.VMEM)
    away = pl.BlockSpec(memory_space=pl.ANY)
    square = jax.ShapeDtypeStruct((width, width), bf16)
    united, small, hidden_bias, begin, rows, *weights = pl.pallas_call(
        embed_packed_kernel,
        in_specs=[vmem] * 2 + [away] + waits(after),
        out_specs=(vmem,) * 3 + (away,) * 6,
        out_shape=(
            jax.ShapeDtypeStruct((count, 3 * width), bf16),
            jax.ShapeDtypeStruct((8, width), f32),
            jax.ShapeDtypeStruct((ff_parts, width), f32),
            jax.ShapeDtypeStruct((count, width), f32),
            jax.ShapeDtypeStruct((count, width), bf16),
        )
        + (square,) * 4,
        scratch_shapes=[
            pltpu.VMEM((devices, 2 * d_rows, width), bf16),
            pltpu.VMEM((devices, 2 * d_rows, width), bf16),
            pltpu.VMEM((devices, table_rows, width), bf16),
            pltpu.VMEM((devices, 16, 128), bf16),
            pltpu.VMEM((count, width), f32),
            pltpu.VMEM((count, width), bf16),
            pltpu.VMEM((4, width, width), bf16),
            pltpu.SemaphoreType.DMA((4,)),
            pltpu.SemaphoreType.DMA((6,)),
        ],
        compiler_params=params(),
        cost_estimate=cost(2 * count * width * 5 * width, 12e6),
    )(tokens, places, whole, *after)
    return begin, rows, united, weights, small, hidden_bias


def embed(tokens, places, small, weights):
    count, width = tokens.shape
    return pl.pallas_call(
        embed_kernel,
        out_shape=(
            jax.ShapeDtypeStruct((count, width), f32),
            jax.ShapeDtypeStruct((count, width), bf16),
            jax.ShapeDtypeStruct((count, 3 * width), bf16),
        ),
        compiler_params=params(),
        cost_estimate=cost(2 * count * width * 5 * width, 12e6),
    )(tokens, places, *weights, small)


def head_mask(head):
    return lax.broadcasted_iota(jnp.int32, (1, PAIR), 1) // HEAD_DIM == head


def attend_kernel(half, query_ref, key_ref, value_ref, *refs):
    bias_refs = refs[:2]
    attention_ref, context_ref = refs[-2:]
    query, key = query_ref[...], key_ref[...]
    value_t = value_ref[...].astype(f32).T.astype(bf16)

    def pair(bias_ref):
        parts = []
        for head in range(2):
            scores = dot_nt(jnp.where(head_mask(head), key, 0), query) + bias_ref[head]
            raised = jnp.exp(scores - jnp.max(scores, axis=0, keepdims=True))
            attention = (raised * (1.0 / jnp.sum(raised, axis=0, keepdims=True))).astype(bf16)
            attention_ref[head] = attention
            parts.append(dot(value_t[head * HEAD_DIM : (head + 1) * HEAD_DIM], attention))
        context_ref[...] = jnp.concatenate(parts, axis=0).T.astype(bf16)

    first = pl.program_id(0) < half

    @pl.when(first)
    def _():
        pair(bias_refs[0])

    @pl.when(jnp.logical_not(first))
    def _():
        pair(bias_refs[1])


def attend(united, bias_one, bias_two, after=()):
    count = united.shape[0]
    pairs = HEADS // 2
    half = bias_one.shape[0] // 2
    column = lambda shift: pl.BlockSpec((count, PAIR), lambda p: (0, p + shift))
    square = lambda index: pl.BlockSpec((2, count, count), lambda p: (index(p), 0, 0))
    return pl.pallas_call(
        partial(attend_kernel, half),
        grid=(pairs,),
        in_specs=[
            column(0),
            column(pairs),
            column(2 * pairs),
            square(lambda p: jnp.minimum(p, half - 1)),
            square(lambda p: jnp.maximum(p - half, 0)),
        ]
        + waits(after),
        out_specs=(square(lambda p: p), column(0)),
        out_shape=(
            jax.ShapeDtypeStruct((HEADS, count, count), bf16),
            jax.ShapeDtypeStruct((count, HEADS * HEAD_DIM), bf16),
        ),
        compiler_params=params(),
        cost_estimate=cost(4 * HEADS * count * count * HEAD_DIM, 6 * HEADS * count * count),
    )(united, united, united, bias_one, bias_two, *after)


def attend_back_kernel(query_ref, key_ref, value_ref, attention_ref, d_context_ref, *refs):
    d_query_ref, d_key_ref, d_value_ref, d_scores_ref = refs[-4:]
    query, value, d_context = query_ref[...], value_ref[...], d_context_ref[...]
    key_t = key_ref[...].astype(f32).T.astype(bf16)
    parts = []
    d_key = jnp.zeros(query.shape, f32)
    d_value = jnp.zeros(query.shape, f32)
    for head in range(2):
        mask = head_mask(head)
        d_attention = dot_nt(jnp.where(mask, value, 0), d_context)
        attention_low = attention_ref[head]
        attention = attention_low.astype(f32)
        centre = jnp.sum(attention * d_attention, axis=0, keepdims=True)
        d_scores = (attention * (d_attention - centre)).astype(bf16)
        d_scores_ref[head] = d_scores
        d_key += dot(d_scores, jnp.where(mask, query, 0))
        d_value += dot(attention_low, jnp.where(mask, d_context, 0))
        parts.append(dot(key_t[head * HEAD_DIM : (head + 1) * HEAD_DIM], d_scores))
    d_query_ref[...] = jnp.concatenate(parts, axis=0).T.astype(bf16) * bf16(0.125)
    d_key_ref[...] = d_key.astype(bf16)
    d_value_ref[...] = d_value.astype(bf16)


def attend_back(united, attention, d_context):
    count = united.shape[0]
    pairs = HEADS // 2
    column = lambda shift: pl.BlockSpec((count, PAIR), lambda p: (0, p + shift))
    square = pl.BlockSpec((2, count, count), lambda p: (p, 0, 0))
    joined = jax.ShapeDtypeStruct((count, HEADS * HEAD_DIM), bf16)
    return pl.pallas_call(
        attend_back_kernel,
        grid=(pairs,),
        in_specs=[column(0), column(pairs), column(2 * pairs), square, column(0)],
        out_specs=(column(0), column(0), column(0), square),
        out_shape=(joined, joined, joined, jax.ShapeDtypeStruct((HEADS, count, count), bf16)),
        compiler_params=params(),
        cost_estimate=cost(8 * HEADS * count * count * HEAD_DIM, 4 * HEADS * count * count),
    )(united, united, united, attention, d_context)


def unit_rows(values):
    centred = values - jnp.mean(values, axis=1, keepdims=True)
    scale = lax.rsqrt(jnp.mean(centred * centred, axis=1, keepdims=True) + EPSILON)
    return centred * scale, scale


def unit_rows_back(units, scale, d_units):
    spread = jnp.mean(d_units * units, axis=1, keepdims=True)
    return scale * (d_units - jnp.mean(d_units, axis=1, keepdims=True) - units * spread)


def column_sum(values):
    return jnp.sum(values.astype(f32), axis=0, keepdims=True)


def split_cores(values, rows):
    inner = values.shape[0] // rows
    return values.reshape((inner // 4, 2, 2, rows, values.shape[1]))


def middle_kernel(packed, place_ref, begin_ref, context_ref, w_out_ref, one_hbm, two_hbm, *refs):
    small_ref, hidden_bias_ref, slot_ref, slot_grad_ref, layer_ref, g_out_ref, *refs = refs
    d_pre_ref, d_context_ref, sums_ref, hidden_sum_ref, g_one_ref, *refs = refs
    if not packed:
        g_two_ref, *refs = refs
    w_in_ref, w_back_ref, act_ref, slope_ref, d_inner_ref, total_ref, load_sems, *refs = refs
    count, width = begin_ref.shape
    parts = w_in_ref.shape[0]
    context = context_ref[...]
    w_in = lambda part: w_in_ref[part].reshape(width, width)
    if packed:
        buffer_ref, store_sems = refs
        core = place_ref[2]
        devices = buffer_ref.shape[1] * 4
        d_rows, h_rows = width // devices, width * parts // devices
        blocks_each = width // h_rows // 4
        w_back = lambda part: w_back_ref[pl.ds(part * blocks_each, blocks_each)].reshape(width, width)
        loads = []
        for side, source in enumerate((one_hbm, two_hbm)):
            in_rows, back_rows = pl.ds(0, parts * d_rows), pl.ds(parts * d_rows, h_rows)
            target = buffer_ref.at[side, :, :, in_rows]
            loads.append(pltpu.make_async_copy(source.at[:, :, in_rows], target, load_sems.at[side]))
            target = w_back_ref.at[:, side ^ core]
            loads.append(pltpu.make_async_copy(source.at[:, :, back_rows], target, load_sems.at[2 + side]))
    else:
        w_back = lambda part: w_back_ref[part]
        loads = [
            pltpu.make_async_copy(one_hbm, w_in_ref, load_sems.at[0]),
            pltpu.make_async_copy(two_hbm, w_back_ref, load_sems.at[1]),
        ]
    for load in loads:
        load.start()

    row = lambda i: small_ref[i : i + 1, :]
    attended = dot(context, w_out_ref[...]) + row(2)
    units, scale = unit_rows(begin_ref[...] + attended)
    mid = units * row(6) + row(3)
    mid_rows = mid.astype(bf16)
    total_ref[...] = mid + row(4)
    for load in loads:
        load.wait()

    def unpack(block, carry):
        for side in range(2):
            for pair in range(parts // 2):
                at = pair * 2 * d_rows
                both = buffer_ref[side, block, :, at : at + 2 * d_rows].astype(f32)
                for which in range(2):
                    rows = both[:, which * d_rows : (which + 1) * d_rows].reshape(2 * d_rows, width)
                    w_in_ref[2 * pair + which, block, side ^ core] = rows.astype(bf16)
        return carry

    if packed:
        lax.fori_loop(0, devices // 4, unpack, 0)

    def forward_part(part, carry):
        inner = dot(mid_rows, w_in(part)) + hidden_bias_ref[pl.ds(part, 1), :]
        share = 0.5 * lax.erf(inner * (2.0**-0.5)) + 0.5
        bell = jnp.exp(inner * inner * -0.5) * (0.5 * 2.0**0.5 / jnp.pi**0.5)
        act = (inner * share).astype(bf16)
        act_ref[part] = act
        slope_ref[part] = (share + inner * bell).astype(bf16)
        total_ref[...] += dot(act, w_back(part))
        return carry

    lax.fori_loop(0, parts, forward_part, 0)
    out_units, out_scale = unit_rows(total_ref[...])
    layer_ref[...] = (out_units * row(7) + row(5)).astype(bf16)[: layer_ref.shape[0]]

    token_ids = lax.broadcasted_iota(jnp.int32, (count, slot_ref.shape[1]), 0)
    slot_hot = jnp.where(slot_ref[...] == token_ids, 1.0, 0.0).astype(bf16)
    out_cot = dot(slot_hot, slot_grad_ref[...])
    sums_ref[3:4, :] = column_sum(out_cot)
    sums_ref[5:6, :] = column_sum(out_cot * out_units)
    d_sum = unit_rows_back(out_units, out_scale, out_cot * row(7))
    sums_ref[2:3, :] = column_sum(d_sum.astype(bf16))
    d_outer = d_sum.astype(bf16)
    total_ref[...] = d_sum
    rows_t = mid.T.astype(bf16)

    def stores(at, rows, first, blocks, sem):
        copies = []
        for side in range(2):
            for step in range(blocks // 2):
                z = first // 2 + step
                source = buffer_ref.at[side, pl.ds(2 * z, 2), :, pl.ds(at, rows)]
                target = g_one_ref.at[side, :, :, z, pl.ds(at, rows)]
                copies.append(pltpu.make_async_copy(source, target, store_sems.at[side, step, sem]))
        return copies

    def store_back(part):
        return stores(parts * d_rows, h_rows, part * blocks_each, blocks_each, part)

    def store_in(pair):
        return stores(pl.multiple_of(pair * 2 * d_rows, 16), 2 * d_rows, 0, devices // 4, parts + pair)

    def backward_part(part, carry):
        d_act = dot_nt(d_outer, w_back(part))
        d_inner = (d_act * slope_ref[part].astype(f32)).astype(bf16)
        hidden_sum_ref[pl.ds(part, 1), :] = column_sum(d_inner)
        total_ref[...] += dot_nt(d_inner, w_in(part))
        d_inner_ref[part] = d_inner
        g_back = dot_tn(act_ref[part], d_outer).astype(bf16)
        if packed:
            blocks = split_cores(g_back, h_rows)
            at = pl.ds(part * blocks_each, blocks_each)
            for side in range(2):
                buffer_ref[side, at, :, parts * d_rows :] = blocks[:, side]
            for copy in store_back(part):
                copy.start()
        else:
            g_two_ref[part] = g_back
            g_one_ref[part] = dot(rows_t, d_inner).astype(bf16)
        return carry

    lax.fori_loop(0, parts, backward_part, 0)

    def pack_pair(pair, carry):
        at = pl.ds(pl.multiple_of(pair * 2 * d_rows, 16), 2 * d_rows)
        for left in range(0, width, 256):
            columns = slice(left, left + 256)
            pieces = [
                dot(rows_t, d_inner_ref[2 * pair + which, :, columns]).reshape(devices, d_rows, 256)
                for which in range(2)
            ]
            joined = jnp.concatenate(pieces, axis=1).astype(bf16).reshape(devices // 4, 2, 2, 2 * d_rows, 256)
            for side in range(2):
                buffer_ref[side, :, :, at, columns] = joined[:, side]
        for copy in store_in(pair):
            copy.start()
        return carry

    if packed:
        lax.fori_loop(0, parts // 2, pack_pair, 0)

    d_mid = total_ref[...]
    d_pre = unit_rows_back(units, scale, d_mid * row(6))
    d_pre_ref[...] = d_pre
    d_att = d_pre.astype(bf16)
    g_out_ref[...] = dot_tn(context, d_att).astype(bf16)
    d_context_ref[...] = dot_nt(d_att, w_out_ref[...]).astype(bf16)
    sums_ref[0:1, :] = column_sum(d_att)
    sums_ref[1:2, :] = column_sum(d_mid)
    sums_ref[4:5, :] = column_sum(d_mid * units)
    sums_ref[6:8, :] = jnp.zeros((2, width), f32)
    if packed:
        for part in range(parts):
            for copy in store_back(part):
                copy.wait()
        for pair in range(parts // 2):
            for copy in store_in(pair):
                copy.wait()


def middle(place, packed, devices, live, begin, context, w_attn_out, w_one, w_two, small, hidden_bias, slots, slot_grads):
    count, width = begin.shape
    parts = hidden_bias.shape[0]
    hidden = parts * width
    vmem = pl.BlockSpec(memory_space=pltpu.VMEM)
    away = pl.BlockSpec(memory_space=pl.ANY)
    if packed:
        weights = [(parts, devices // 4, 2, 2 * width // devices, width), (devices // 4, 2, 2, hidden // devices, width)]
    else:
        weights = [(parts, width, width)] * 2
    scratch = [pltpu.VMEM(shape, bf16) for shape in weights + [(parts, count, width)] * 3]
    scratch += [pltpu.VMEM((count, width), f32), pltpu.SemaphoreType.DMA((4,))]
    if packed:
        rows = 2 * hidden // devices
        grads = (jax.ShapeDtypeStruct((2, 2, 2, devices // 8, rows, width), bf16),)
        scratch += [
            pltpu.VMEM((2, devices // 4, 2, rows, width), bf16),
            pltpu.SemaphoreType.DMA((2, devices // 8, parts + parts // 2)),
        ]
    else:
        grads = (jax.ShapeDtypeStruct((parts, width, width), bf16),) * 2
    grad_space = away if packed else vmem
    return pl.pallas_call(
        partial(middle_kernel, packed),
        in_specs=[pl.BlockSpec(memory_space=pltpu.SMEM)] + [vmem] * 3 + [away] * 2 + [vmem] * 4,
        out_specs=(vmem,) * 6 + (grad_space,) * len(grads),
        out_shape=(
            jax.ShapeDtypeStruct((live, width), bf16),
            jax.ShapeDtypeStruct((width, width), bf16),
            jax.ShapeDtypeStruct((count, width), f32),
            jax.ShapeDtypeStruct((count, width), bf16),
            jax.ShapeDtypeStruct((8, width), f32),
            jax.ShapeDtypeStruct((parts, width), f32),
        )
        + grads,
        scratch_shapes=scratch,
        compiler_params=params(62464000),
        cost_estimate=cost(12 * count * width * hidden, 30e6),
    )(place, begin, context, w_attn_out, w_one, w_two, small, hidden_bias, slots, slot_grads)


def store_blocks(buffer_ref, targets, sems, blocks, first, at, first_sem, core):
    spaces, rows = blocks.shape[0], blocks.shape[3]
    for which in range(2):
        buffer_ref[which ^ core, first : first + spaces, :, at : at + rows] = blocks[:, which]
    copies = []
    for side, target in enumerate(targets):
        source = buffer_ref.at[side, pl.ds(first, spaces), :, pl.ds(at, rows)]
        target = target.at[pl.ds(first, spaces), :, pl.ds(at, rows)]
        copies.append(pltpu.make_async_copy(source, target, sems.at[first_sem + side]))
        copies[-1].start()
    return copies


def qkv_back_kernel(halves, packed, place_ref, *refs):
    d_refs, refs = refs[: 3 * halves], refs[3 * halves :]
    g_out_ref, rows_ref = refs[:2]
    g_one_ref, g_two_ref, sums_ref = refs[-5:-2] if packed else refs[-3:]
    count, width = rows_ref.shape
    rows_t = rows_ref[...].astype(f32).T.astype(bf16)
    grads = [
        jnp.concatenate([d_refs[3 * half + part][...] for half in range(halves)], axis=1) for part in range(3)
    ]
    sums_ref[...] = jnp.zeros((8, width), f32)
    sums_ref[0:1, :] = column_sum(grads[0])
    sums_ref[1:2, :] = column_sum(grads[2])
    if not packed:
        for part in range(3):
            g_one_ref[:, part * width : (part + 1) * width] = dot(rows_t, grads[part]).astype(bf16)
        g_two_ref[...] = g_out_ref[...]
        return
    buffer_ref, sems = refs[-2:]
    core = place_ref[2]
    devices = buffer_ref.shape[1] * 4
    d_rows = width // devices
    for left in range(0, width, 256):
        columns = slice(left, left + 256)
        pieces = [dot(rows_t, grad[:, columns]).reshape(devices, d_rows, 256) for grad in grads]
        pieces.append(g_out_ref[:, columns].astype(f32).reshape(devices, d_rows, 256))
        joined = jnp.concatenate(pieces, axis=1).astype(bf16).reshape(devices // 4, 2, 2, 4 * d_rows, 256)
        for which in range(2):
            buffer_ref[which ^ core, :, :, :, columns] = joined[:, which]
    copies = [
        pltpu.make_async_copy(buffer_ref.at[side], target, sems.at[side])
        for side, target in enumerate((g_one_ref, g_two_ref))
    ]
    for copy in copies:
        copy.start()
    for copy in copies:
        copy.wait()


def qkv_back(place, packed, devices, d_halves, g_out, begin_rows, after=()):
    count, width = begin_rows.shape
    vmem = pl.BlockSpec(memory_space=pltpu.VMEM)
    away = pl.BlockSpec(memory_space=pl.ANY)
    d_all = [d for half in d_halves for d in half]
    scratch = []
    if packed:
        half = (devices // 4, 2, 4 * (width // devices), width)
        grads = (jax.ShapeDtypeStruct(half, bf16),) * 2
        scratch = [pltpu.VMEM((2,) + half, bf16), pltpu.SemaphoreType.DMA((2,))]
    else:
        grads = (jax.ShapeDtypeStruct((width, 3 * width), bf16), jax.ShapeDtypeStruct((width, width), bf16))
    grad_space = away if packed else vmem
    return pl.pallas_call(
        partial(qkv_back_kernel, len(d_halves), packed),
        in_specs=[pl.BlockSpec(memory_space=pltpu.SMEM)] + [vmem] * (len(d_all) + 2) + waits(after),
        out_specs=(grad_space, grad_space, vmem),
        out_shape=grads + (jax.ShapeDtypeStruct((8, width), f32),),
        scratch_shapes=scratch,
        compiler_params=params(),
        cost_estimate=cost(6 * count * width * width, 10e6),
    )(place, *d_all, g_out, begin_rows, *after)


def embed_back_kernel(halves, packed, place_ref, *refs):
    d_refs, refs = refs[: 3 * halves], refs[3 * halves :]
    w_hbm, refs = refs[:3], refs[3:]
    d_pre_ref, coords_ref = refs[:2]
    scratch = 4 if packed else 2
    outs = refs[-scratch - (3 if packed else 2) : -scratch]
    input_grad_ref = outs[0]
    w_ref, load_sems = refs[-scratch:][:2]
    count, width = d_pre_ref.shape
    loads = [pltpu.make_async_copy(w_hbm[part], w_ref.at[part], load_sems.at[part]) for part in range(3)]
    for copy in loads:
        copy.start()
    total = d_pre_ref[...]
    for part in range(3):
        loads[part].wait()
        grad = jnp.concatenate([d_refs[3 * half + part][...] for half in range(halves)], axis=1)
        total += dot_nt(grad, w_ref[part])
    input_grad_ref[...] = total
    low = total.astype(bf16)
    if packed:
        buffer_ref, store_sems = refs[-2:]
        devices, t_rows = buffer_ref.shape[1] * 4, buffer_ref.shape[3]
        half = t_rows * devices // 2
    else:
        half = outs[1].shape[0] // 2
    values = lax.broadcasted_iota(jnp.int32, (half, count), 0)
    copies = []
    for side in range(2):
        hot = jnp.where(coords_ref[side : side + 1, :] == values, 1.0, 0.0).astype(bf16)
        g_table = dot(hot, low).astype(bf16)
        if packed:
            blocks = split_cores(g_table, t_rows)
            first = side * blocks.shape[0]
            copies += store_blocks(buffer_ref, outs[1:], store_sems, blocks, first, 0, 2 * side, place_ref[2])
        else:
            outs[1][side * half : (side + 1) * half, :] = g_table
    for copy in copies:
        copy.wait()


def embed_back(place, packed, devices, d_halves, w_qkv, d_pre, coords, table_rows, after=()):
    count, width = d_pre.shape
    vmem = pl.BlockSpec(memory_space=pltpu.VMEM)
    away = pl.BlockSpec(memory_space=pl.ANY)
    d_all = [d for half in d_halves for d in half]
    scratch = [pltpu.VMEM((3, width, width), bf16), pltpu.SemaphoreType.DMA((3,))]
    if packed:
        half = (devices // 4, 2, table_rows // devices, width)
        grads = (jax.ShapeDtypeStruct(half, bf16),) * 2
        scratch += [pltpu.VMEM((2,) + half, bf16), pltpu.SemaphoreType.DMA((4,))]
    else:
        grads = (jax.ShapeDtypeStruct((table_rows, width), bf16),)
    return pl.pallas_call(
        partial(embed_back_kernel, len(d_halves), packed),
        in_specs=[pl.BlockSpec(memory_space=pltpu.SMEM)]
        + [vmem] * len(d_all)
        + [away] * 3
        + [vmem] * 2
        + waits(after),
        out_specs=(vmem,) + ((away,) if packed else (vmem,)) * len(grads),
        out_shape=(jax.ShapeDtypeStruct((count, width), f32),) + grads,
        scratch_shapes=scratch,
        compiler_params=params(),
        cost_estimate=cost(2 * count * width * (table_rows + 3 * width), 15e6),
    )(place, *d_all, *w_qkv, d_pre, coords, *after)


GROUP = 8
TABLE_BLOCKS = 6
TABLES = ((0, B1), (5, B2), (11, B2))


def table_kernel(halves, index_ref, *refs):
    d_refs = refs[:halves]
    out_ref, total_ref = refs[-2:]
    keys, count = d_refs[0].shape[1:]
    columns = 2 * HEADS * GROUP

    @pl.when(pl.program_id(0) == 0)
    def _():
        total_ref[...] = jnp.zeros_like(total_ref)

    d_scores = jnp.concatenate([d_ref[...].astype(f32) for d_ref in d_refs], axis=0)
    packed = index_ref[:, :count]
    base = 0
    for shift, buckets in TABLES:
        bucket = lax.shift_right_logical(packed, shift) & (buckets - 1)
        upper, lowest = lax.shift_right_logical(bucket, 1).astype(f32), bucket & 1
        uppers = buckets // 2
        values = lax.broadcasted_iota(jnp.int32, (uppers, count), 0).astype(f32).astype(bf16)
        left, right = [], []
        for first in range(0, keys, GROUP):
            group = slice(first, first + GROUP)
            hot = [
                jnp.where(jnp.broadcast_to(upper[k : k + 1], values.shape).astype(bf16) == values, bf16(1), bf16(0))
                for k in range(first, first + GROUP)
            ]
            left.append(jnp.concatenate(hot, axis=0))
            split = [
                jnp.where((lowest[group] == bit)[None], d_scores[:, group, :], 0.0).reshape(HEADS * GROUP, count)
                for bit in range(2)
            ]
            right.append(jnp.concatenate(split, axis=0).astype(bf16))
        total_ref[base : base + uppers * GROUP, :] += dot_nt(
            jnp.concatenate(left, axis=1), jnp.concatenate(right, axis=1)
        )
        base += uppers * GROUP

    @pl.when(pl.program_id(0) == pl.num_programs(0) - 1)
    def _():
        base, pieces = 0, []
        for _, buckets in TABLES:
            shape = (GROUP, buckets // 2, columns)
            block = total_ref[base : base + shape[0] * shape[1], :].reshape(shape)
            own = lax.broadcasted_iota(jnp.int32, shape, 2) % GROUP == lax.broadcasted_iota(jnp.int32, shape, 0)
            pieces.append(jnp.sum(jnp.where(own, block, 0.0), axis=0))
            base += shape[0] * shape[1]
        out_ref[...] = jnp.concatenate(pieces, axis=0)


def table_grad(packed, d_halves, first, last, after=()):
    count = packed.shape[0]
    keys = count // TABLE_BLOCKS
    uppers = (B1 + 2 * B2) // 2
    columns = 2 * HEADS * GROUP
    return pl.pallas_call(
        partial(table_kernel, len(d_halves)),
        grid=(last - first,),
        in_specs=[pl.BlockSpec((keys, packed.shape[1]), lambda i: (i + first, 0))]
        + [pl.BlockSpec((d.shape[0], keys, count), lambda i: (0, i + first, 0)) for d in d_halves]
        + waits(after),
        out_specs=full((uppers, columns)),
        out_shape=jax.ShapeDtypeStruct((uppers, columns), f32),
        scratch_shapes=[pltpu.VMEM((uppers * GROUP, columns), f32)],
        compiler_params=params(),
        cost_estimate=cost(1e10, 2 * HEADS * count * count),
    )(packed, *d_halves, *after)


def unfold_table(folded):
    uppers = folded.shape[0]
    return folded.reshape(uppers, 2, HEADS, GROUP).sum(axis=3).reshape(2 * uppers, HEADS)


PLACE = ("z", "x", "c", "y")


def swap(values, axis, size, bit):
    return lax.ppermute(values, axis, [(i, i ^ bit) for i in range(size)])


def pack_kernel(w_qkv_ref, w_out_ref, table_ref, biases_ref, gains_ref, ff_bias_ref, w_in_ref, w_back_ref, *refs):
    attn_ref, ff_ref, small_ref = refs
    rows, width = w_out_ref.shape
    parts = lambda ref: [ref[:, at : at + width].astype(f32) for at in range(0, ref.shape[1], width)]
    beside = parts(w_qkv_ref) + [w_out_ref[...].astype(f32)]
    attn_ref[: 4 * rows, :] = jnp.concatenate(beside, axis=0).astype(bf16)
    table_end = 4 * rows + table_ref.shape[0]
    attn_ref[4 * rows : table_end, :] = table_ref[...]
    count, shard = biases_ref.shape
    small_ref[...] = jnp.zeros_like(small_ref)
    small_ref[:count, :shard] = biases_ref[...].astype(f32)
    small_ref[count:8, :shard] = gains_ref[...].astype(f32)
    small_ref[8:9, : ff_bias_ref.shape[1]] = ff_bias_ref[...].astype(f32)
    attn_ref[table_end:, :] = small_ref[...].astype(bf16)
    in_parts = parts(w_in_ref)
    ff_ref[: len(in_parts) * rows, :] = jnp.concatenate(in_parts, axis=0).astype(bf16)
    ff_ref[len(in_parts) * rows :, :] = w_back_ref[...]


def pack(w_qkv, w_attn_out, dcpe_table, biases, norm_gains, ff_bias, w_ff_in, w_ff_out):
    rows, width = w_attn_out.shape
    attn_rows = 4 * rows + dcpe_table.shape[0] + 16
    ff_rows = w_ff_in.shape[1] // width * rows + w_ff_out.shape[0]
    return pl.pallas_call(
        pack_kernel,
        out_shape=(
            jax.ShapeDtypeStruct((attn_rows, width), bf16),
            jax.ShapeDtypeStruct((ff_rows, width), bf16),
        ),
        scratch_shapes=[pltpu.VMEM((16, width), f32)],
        compiler_params=params(),
        cost_estimate=cost(1e6, 1e6),
    )(w_qkv, w_attn_out, dcpe_table, biases, norm_gains, ff_bias.reshape(1, -1), w_ff_in, w_ff_out)


def spread_kernel(pieces, cuts, place_ref, *refs):
    outs = refs[-len(cuts) :]
    for piece in range(pieces):

        @pl.when(pl.program_id(0) == piece)
        def _(piece=piece):
            for index, (out_ref, (at, rows)) in enumerate(zip(outs, cuts)):
                source = refs[index * pieces + piece]
                extent = source.shape[:-2]
                out_ref[...] = source[..., at : at + rows, :].reshape(out_ref.shape)


def spread(place, axes, groups, cuts, after=()):
    pieces = len(groups[0])
    operands, in_specs, out_specs, out_shapes = [], [], [], []
    for axis, group, (at, rows) in zip(axes, groups, cuts):
        shape = group[0].shape
        operands += group
        in_specs += [pl.BlockSpec(shape, lambda step, place, zeros=(0,) * len(shape): zeros)] * pieces
        lead = len(shape) - 2
        out_specs.append(
            pl.BlockSpec(
                shape[:-2] + (1, rows, shape[-1]),
                lambda step, place, lead=lead, axis=axis: (0,) * lead + (place[axis] ^ step, 0, 0),
            )
        )
        out_shapes.append(jax.ShapeDtypeStruct(shape[:-2] + (pieces, rows, shape[-1]), bf16))
    return pl.pallas_call(
        partial(spread_kernel, pieces, cuts),
        grid_spec=pltpu.PrefetchScalarGridSpec(
            num_scalar_prefetch=1, grid=(pieces,), in_specs=in_specs + waits(after), out_specs=out_specs
        ),
        out_shape=out_shapes,
        compiler_params=params(),
        cost_estimate=cost(1e6, 1e6),
    )(place, *operands, *after)


def join_kernel(cut, place_ref, head_ref, head_came_ref, tail_ref, tail_came_ref, *refs):
    out_ref = refs[-1]
    mine_x, mine_y = place_ref[1], place_ref[3]
    out_ref[0, :, mine_y, :cut] = head_ref[0]
    out_ref[0, :, 1 - mine_y, :cut] = head_came_ref[0]
    out_ref[0, mine_x, :, cut:] = tail_ref[0]
    out_ref[0, 1 - mine_x, :, cut:] = tail_came_ref[0]


def join(place, head, head_came, tail, tail_came, after=()):
    spaces, _, cut, width = head.shape
    rows = cut + tail.shape[2]
    return pl.pallas_call(
        partial(join_kernel, cut),
        grid_spec=pltpu.PrefetchScalarGridSpec(
            num_scalar_prefetch=1,
            grid=(spaces,),
            in_specs=[pl.BlockSpec((1, 2, cut, width), lambda s, p: (s, 0, 0, 0))] * 2
            + [pl.BlockSpec((1, 2, rows - cut, width), lambda s, p: (s, 0, 0, 0))] * 2
            + waits(after),
            out_specs=pl.BlockSpec((1, 2, 2, rows, width), lambda s, p: (s, 0, 0, 0, 0)),
        ),
        out_shape=jax.ShapeDtypeStruct((spaces, 2, 2, rows, width), bf16),
        compiler_params=params(),
        cost_estimate=cost(1e6, 1e6),
    )(place, head, head_came, tail, tail_came, *after)


def combine_kernel(sources, place_ref, *refs):
    count = sum(len(source) for source in sources)
    kept, came, outs = refs[:count], refs[count : 2 * count], refs[-len(sources) :]
    at = 0
    for source, out_ref in zip(sources, outs):
        first = 0
        for _ in source:
            total = kept[at][...].astype(f32) + came[at][...].astype(f32)
            rows, width = total.shape[-2:]
            out_ref[0, :, first : first + rows, :] = total.astype(bf16).reshape(out_ref.shape[1], rows, width)
            first += rows
            at += 1


def combine(place, steps, outs, after=(), worth=1e6):
    kept, came, in_specs = [], [], []
    out_specs, out_shapes = [], []
    for out in outs:
        for first, second, block, index in out:
            kept.append(first)
            came.append(second)
            in_specs.append(pl.BlockSpec(block, index))
        inner = 1
        for extent in out[0][2][1:-2]:
            inner *= extent
        shape = (inner, sum(entry[2][-2] for entry in out), out[0][2][-1])
        out_specs.append(pl.BlockSpec((1,) + shape, lambda step, place: (step, 0, 0, 0)))
        out_shapes.append(jax.ShapeDtypeStruct((steps,) + shape, bf16))
    return pl.pallas_call(
        partial(combine_kernel, [[None] * len(out) for out in outs]),
        grid_spec=pltpu.PrefetchScalarGridSpec(
            num_scalar_prefetch=1, grid=(steps,), in_specs=in_specs * 2 + waits(after), out_specs=out_specs
        ),
        out_shape=out_shapes,
        compiler_params=params(),
        cost_estimate=cost(worth, worth),
    )(place, *kept, *came, *after)


class PackedSum:
    def __init__(self, place, keep, away, sizes):
        self.place, self.sizes = place, sizes
        shape = (sizes["z"], sizes["x"], sizes["y"]) + keep.shape[2:]
        self.cut, self.width = keep.shape[2] // 2, keep.shape[3]
        self.keep, self.came = keep.reshape(shape), swap(away, "c", 2, 1).reshape(shape)

    def send_first(self, after):
        block_x, block_y = (1, 1, 2, self.cut, self.width), (1, 2, 1, self.cut, self.width)
        pair = (self.keep, self.came)
        keep_a, away_a, keep_b, away_b = combine(
            self.place,
            self.sizes["z"],
            [
                [pair + (block_x, lambda s, p: (s, p[1], 0, 0, 0))],
                [pair + (block_x, lambda s, p: (s, 1 - p[1], 0, 0, 0))],
                [pair + (block_y, lambda s, p: (s, 0, p[3], 1, 0))],
                [pair + (block_y, lambda s, p: (s, 0, 1 - p[3], 1, 0))],
            ],
            after,
        )
        self.pairs = ((keep_a, swap(away_a, "x", 2, 1)), (keep_b, swap(away_b, "y", 2, 1)))
        return [away_a, away_b]

    def send_second(self, after):
        block = (1, 1, self.cut, self.width)
        pair_a, pair_b = self.pairs
        keep_a, away_a, keep_b, away_b = combine(
            self.place,
            self.sizes["z"],
            [
                [pair_a + (block, lambda s, p: (s, p[3], 0, 0))],
                [pair_a + (block, lambda s, p: (s, 1 - p[3], 0, 0))],
                [pair_b + (block, lambda s, p: (s, p[1], 0, 0))],
                [pair_b + (block, lambda s, p: (s, 1 - p[1], 0, 0))],
            ],
            after,
        )
        self.pairs = ((keep_a, swap(away_a, "y", 2, 1)), (keep_b, swap(away_b, "x", 2, 1)))
        return [away_a, away_b]


def send_along_z(place, pairs, after):
    step = lambda pair, other: pair + ((1,) + pair[0].shape[1:], lambda s, p: (p[0] ^ other, 0, 0, 0))
    keep, *away = combine(place, 1, [[step(pair, other) for pair in pairs] for other in range(4)], after)
    return keep, [swap(rows, "z", 4, 1 + other) for other, rows in enumerate(away)], away


def finish_kernel(keep_ref, one_ref, two_ref, three_ref, *refs):
    qkv_ref, out_ref, table_ref = refs[-3:]
    total = keep_ref[0, 0].astype(f32) + one_ref[0, 0].astype(f32)
    total += two_ref[0, 0].astype(f32) + three_ref[0, 0].astype(f32)
    rows, width = out_ref.shape
    for part in range(3):
        qkv_ref[:, part * width : (part + 1) * width] = total[part * rows : (part + 1) * rows]
    out_ref[...] = total[3 * rows : 4 * rows]
    table_ref[...] = total[4 * rows :]


def finish_attn(keep, came, rows, after):
    packed, width = keep.shape[2:]
    return pl.pallas_call(
        finish_kernel,
        in_specs=[pl.BlockSpec(memory_space=pltpu.VMEM)] * 4 + waits(after),
        out_shape=(
            jax.ShapeDtypeStruct((rows, 3 * width), f32),
            jax.ShapeDtypeStruct((rows, width), f32),
            jax.ShapeDtypeStruct((packed - 4 * rows, width), f32),
        ),
        compiler_params=params(),
        cost_estimate=cost(1e6, 1e6),
    )(keep, *came, *after)


def finish_ff_kernel(own_ref, *refs):
    in_ref, back_ref = refs[-2:]
    total = own_ref[...].astype(f32)
    rows, width = in_ref.shape[0], back_ref.shape[1]
    parts = in_ref.shape[1] // width
    for part in range(parts):
        in_ref[:, part * width : (part + 1) * width] = total[part * rows : (part + 1) * rows]
    back_ref[...] = total[parts * rows :]


def finish_ff(own, rows, parts, after):
    packed, width = own.shape
    return pl.pallas_call(
        finish_ff_kernel,
        in_specs=[pl.BlockSpec(memory_space=pltpu.VMEM)] + waits(after),
        out_shape=(
            jax.ShapeDtypeStruct((rows, parts * width), f32),
            jax.ShapeDtypeStruct((packed - parts * rows, width), f32),
        ),
        compiler_params=params(),
        cost_estimate=cost(1e6, 1e6),
    )(own, *after)


class Sum:
    def __init__(self, blocks, sizes):
        self.sizes = sizes
        devices = sizes["z"] * sizes["x"] * sizes["c"] * sizes["y"]
        self.terms = [blocks.reshape(tuple(sizes[a] for a in PLACE) + (-1, blocks.shape[-1]))]
        self.came = None
        self.next_bit = {a: 1 for a in PLACE}

    def part(self, dim, which):
        total = None
        for term in self.terms:
            shape = term.shape
            view = term.reshape(shape[:dim] + (shape[dim] // 2, 2) + shape[dim + 1 :])
            piece = lax.dynamic_index_in_dim(view, which, axis=dim + 1, keepdims=False)
            total = piece if total is None else (total.astype(f32) + piece.astype(f32))
        return total.astype(bf16)

    def send(self, axis):
        self.land()
        dim, bit, size = PLACE.index(axis), self.next_bit[axis], self.sizes[axis]
        self.next_bit[axis] = 2 * bit
        mine = lax.axis_index(axis) // bit % 2
        away = self.part(dim, 1 - mine)
        self.came = swap(away, axis, size, bit)
        self.kept = self.part(dim, mine)
        return away

    def land(self):
        if self.came is not None:
            self.terms = [self.kept, self.came]
            self.came = None

    def open_steps(self, axis):
        return self.next_bit[axis] < self.sizes[axis]

    def result(self):
        self.land()
        total = self.terms[0].astype(f32) + self.terms[1].astype(f32)
        return total.reshape(total.shape[4:])


def sum_step(values, axis, sizes):
    bit = 1
    while bit < sizes[axis]:
        values = values + swap(values, axis, sizes[axis], bit)
        bit *= 2
    return values


def small_sums(sums, more_sums, hidden_sum, folded, rel_table, width):
    table_sum = jnp.pad(unfold_table(folded).reshape(-1), (0, -rel_table.size % width)).reshape(-1, width)
    return jnp.concatenate([more_sums[:2], sums[:6], hidden_sum, table_sum], axis=0)


def column_parts(matrix, width):
    return [matrix[:, at : at + width] for at in range(0, matrix.shape[1], width)]


def blocks_of(parts, devices):
    return jnp.concatenate([part.reshape(devices, -1, part.shape[1]) for part in parts], axis=1)


def take(blocks, at, rows):
    return blocks[:, at : at + rows].reshape(-1, blocks.shape[2])


def on_device(
    sizes,
    tokens,
    coords,
    rel_pos,
    rel_box,
    entity_pairs,
    entity_grad,
    w_qkv,
    w_attn_out,
    dcpe_table,
    biases,
    norm_gains,
    w_ff_in,
    w_ff_out,
    ff_bias,
    rel_table,
):
    devices = sizes["z"] * sizes["x"] * sizes["c"] * sizes["y"]
    live, width = tokens.shape[1], tokens.shape[2]
    hidden = ff_bias.shape[0] * devices
    count = -(-live // 64) * 64
    extra = count - live
    shard, ff_shard = biases.shape[1], ff_bias.shape[0]
    d_rows, t_rows, h_rows = w_qkv.shape[0], dcpe_table.shape[0], w_ff_out.shape[0]
    ff_parts = hidden // width

    fast = sizes == {"z": 4, "x": 2, "c": 2, "y": 2} and d_rows % 8 == 0
    place = jnp.stack([lax.axis_index(axis) for axis in PLACE]).astype(jnp.int32)
    pairs = HEADS // 2
    at = 4 * d_rows + t_rows

    packed = packed_buckets(rel_pos.reshape(live, 1, live), rel_box[0].transpose(1, 0, 2), count)
    lookup = lookup_rows(rel_table)
    near, far = lookup[:HEADS], lookup[HEADS:]
    places = jnp.pad(coords[0], ((0, 0), (0, extra)), constant_values=OUTSIDE)
    slots = entity_pairs.reshape(1, -1)
    slot_grads = entity_grad.reshape(slots.shape[1], width)
    padded = jnp.pad(tokens[0], ((0, extra), (0, 0)))

    if fast:
        attn_own, ff_own = pack(w_qkv, w_attn_out, dcpe_table, biases, norm_gains, ff_bias, w_ff_in, w_ff_out)
    else:
        vectors = jnp.pad(jnp.concatenate([biases, norm_gains], axis=0), ((0, 0), (0, width - shard)))
        small_own = jnp.concatenate([vectors, jnp.pad(ff_bias[None], ((0, 7), (0, width - ff_shard)))], axis=0)
        attn_own = jnp.concatenate(column_parts(w_qkv, width) + [w_attn_out, dcpe_table, small_own], axis=0)
        ff_own = jnp.concatenate(column_parts(w_ff_in, width) + [w_ff_out], axis=0)
    whole = lax.all_gather(attn_own, PLACE, axis=0)

    if fast:
        cut = ff_own.shape[0] // 2
        by_z = [ff_own] + [swap(ff_own, "z", 4, bit) for bit in (1, 2, 3)]
        bias_one = score_bias(packed, near, live)
        head, tail = spread(place, (0, 0), [by_z, by_z], [(0, cut), (cut, cut)], [bias_one])
        head_came, tail_came = swap(head, "x", 2, 1), swap(tail, "y", 2, 1)
        bias_two = score_bias(packed, far, live, [head, tail])
        groups = [(head, head_came), (tail, tail_came)]
        head, tail = spread(place, (1, 3), groups, [(0, cut), (0, cut)], [bias_two])
        head_came, tail_came = swap(head, "y", 2, 1), swap(tail, "x", 2, 1)
        begin, begin_rows, united, w_parts, small, hidden_bias = embed_packed(
            padded, places.T, whole, t_rows, ff_parts, [head, tail, slots, slot_grads]
        )
        w_one = join(place, head, head_came, tail, tail_came, [begin])
        w_two = swap(w_one, "c", 2, 1)
        attention, context = attend(united, bias_one, bias_two, [w_one])
        w_one, w_two = (w.reshape((devices // 4, 2) + w.shape[3:]) for w in (w_one, w_two))
    else:
        small = whole[:, at : at + 8, :shard].transpose(1, 0, 2).reshape(8, width).astype(f32)
        hidden_bias = whole[:, at + 8, :ff_shard].reshape(ff_parts, width).astype(f32)
        second = lax.all_gather(ff_own, PLACE, axis=0)
        w_parts = [take(whole, i * d_rows, d_rows) for i in range(4)]
        full_table = take(whole, 4 * d_rows, t_rows)
        w_one = jnp.stack([take(second, i * d_rows, d_rows) for i in range(ff_parts)])
        w_two = take(second, ff_parts * d_rows, h_rows).reshape(ff_parts, width, width)
        begin, begin_rows, united = embed(padded, places.T, small, [full_table] + w_parts[:3])
        attention, context = attend(united, score_bias(packed, near, live), score_bias(packed, far, live))
    layer_out, g_out, d_pre, d_context, sums, hidden_sum, *g_ff = middle(
        place, fast, devices, live, begin, context, w_parts[3], w_one, w_two, small, hidden_bias, slots, slot_grads
    )

    d_query, d_key, d_value, d_scores = attend_back(united, attention, d_context)
    halves = ((d_query, d_key, d_value),)
    table = partial(table_grad, packed, (d_scores,))
    if fast:
        ff = g_ff[0].reshape((-1,) + g_ff[0].shape[3:])
        ff = lax.psum_scatter(ff, ("c", "x", "y"), scatter_dimension=0, tiled=False)
        g_one, g_two, more_sums = qkv_back(place, fast, devices, halves, g_out, begin_rows)
        attn = PackedSum(place, g_one, g_two, sizes)
        input_grad, g_one, g_two = embed_back(
            place, fast, devices, halves, w_parts[:3], d_pre, places, t_rows * devices, [more_sums]
        )
        position = PackedSum(place, g_one, g_two, sizes)
        sent = attn.send_first([input_grad])
        sent = position.send_first(sent)
        early = table(0, 3, sent)
        sent = attn.send_second([early])
        later = table(3, TABLE_BLOCKS, sent)
        sent = position.send_second([later])
        ff, small_sum, _ = lax.optimization_barrier(
            (ff, small_sums(sums, more_sums, hidden_sum, early + later, rel_table, width), sent[0])
        )
        ff = lax.psum_scatter(ff, "z", scatter_dimension=0, tiled=False)
        for axis in ("c", "x", "y"):
            small_sum = small_sum + swap(small_sum, axis, sizes[axis], 1)
        keep, came, away = send_along_z(place, attn.pairs + position.pairs, [small_sum])
        small_sum, input_grad, _ = lax.optimization_barrier((small_sum, input_grad, away[0]))
        small_sum = small_sum + swap(small_sum, "z", sizes["z"], 1)
        g_in, g_back = finish_ff(ff, d_rows, ff_parts, [small_sum])
        small_sum, g_in = lax.optimization_barrier((small_sum, g_in))
        small_sum = small_sum + swap(small_sum, "z", sizes["z"], 2)
        g_qkv, g_out, g_table = finish_attn(keep, came, d_rows, [g_in])
    else:
        g_qkv, g_out, more_sums = qkv_back(place, fast, devices, halves, g_out, begin_rows)
        input_grad, g_table = embed_back(
            place, fast, devices, halves, w_parts[:3], d_pre, places, t_rows * devices
        )
        folded = table(0, TABLE_BLOCKS)
        g_in, g_back = jnp.concatenate(list(g_ff[0]), axis=1), g_ff[1].reshape(hidden, width)
        totals = [Sum(grad, sizes) for grad in (g_in, g_back, g_qkv, g_out, g_table)]
        for axis in PLACE:
            while totals[0].open_steps(axis):
                for total in totals:
                    total.send(axis)
        g_in, g_back, g_qkv, g_out, g_table = (total.result() for total in totals)
        small_sum = small_sums(sums, more_sums, hidden_sum, folded, rel_table, width)
        for axis in PLACE:
            small_sum = sum_step(small_sum, axis, sizes)

    index = lax.axis_index(PLACE)
    vectors = lax.dynamic_slice_in_dim(small_sum[:8], index * shard, shard, axis=1)
    ff_sum = small_sum[8 : 8 + ff_parts].reshape(-1)
    table_sum = small_sum[8 + ff_parts :].reshape(-1)[: rel_table.size].reshape(rel_table.shape)
    return (
        layer_out[None],
        input_grad[None, :live],
        g_qkv,
        g_out,
        g_table,
        vectors[:6],
        vectors[6:],
        g_in,
        g_back,
        lax.dynamic_slice_in_dim(ff_sum, index * ff_shard, ff_shard, axis=0),
        table_sum,
    )


def solution(mesh):
    outer, inner = mesh.shape["dp"], mesh.shape["fsdp"]
    sizes = {"z": outer // 4, "x": 2, "c": 2, "y": inner}
    split = Mesh(mesh.devices.reshape(tuple(sizes[a] for a in PLACE)), PLACE)
    rows = P(PLACE, None)
    three = P(PLACE, None, None)
    four = P(PLACE, None, None, None)
    columns = P(None, PLACE)
    return jax.shard_map(
        partial(on_device, sizes),
        mesh=split,
        in_specs=(three, three, three, four, three, four, rows, rows, rows, columns, columns, rows, rows, P(PLACE), P()),
        out_specs=(three, three, rows, rows, rows, columns, columns, rows, rows, P(PLACE), P()),
        check_vma=False,
    )
```
